256 devices in a mesh: dp: 32 (over z, y_lo, core), replica: 8 (over y_hi, x).
Axes of the slice: x: 4, y: 4 (y_hi: 2, y_lo: 2; y = y_hi * 2 + y_lo), z: 8, core: 2. Of those that a mesh axis runs over, the one named last changes fastest.
Arguments:
- first_view: float32 [8192, 4096], P('dp'), may hold values from -266 to 266
- second_view: float32 [8192, 4096], P('dp'), may hold values from -266 to 266
Outputs:
- grad_first: float32 [8192, 4096], P('dp', 'replica')
- grad_second: float32 [8192, 4096], P('dp', 'replica')
The draws below stay inside these ranges and needn't reach their ends.
All inputs are finite; a program needn't handle non-finite values.
Results may differ from the reference program's by a relative error of at most 0.015.
Values may be sent and summed in bfloat16 or wider, within the bound.
A program may use at most 128 MiB of HBM per device.

```python
import math
import jax
import jax.numpy as jnp
from jax import lax

D = 4096
BATCH = 8192


def view_pair(key):
    keys = jax.random.split(key, 13)
    shape = (BATCH, D)
    positions = jnp.arange(BATCH).astype(jnp.float32)
    rising = jnp.exp(jnp.log(3.0) * positions / max(BATCH - 1, 1))[:, None]
    row_scale = rising * jnp.exp(jnp.log(4.0) * jax.random.uniform(keys[0], (BATCH, 1)))

    def rough(subkey, size):
        pair = jax.random.split(subkey)
        bell = jax.random.truncated_normal(pair[1], -4.0, 4.0, size)
        return bell
    factor_count = max(D // 16, 8)
    factors = rough(keys[11], (BATCH, factor_count))
    decay = jnp.exp(-0.5 * jnp.arange(factor_count).astype(jnp.float32) / factor_count)
    mixing = jnp.sqrt(3.0) * jax.random.uniform(keys[12], (factor_count, D), minval=-1.0, maxval=1.0) * decay[:, None]
    energy = (1.0 - math.exp(-1.0)) / (1.0 - math.exp(-1.0 / factor_count))
    blended = jnp.dot(factors, mixing, precision=lax.Precision.HIGHEST) / math.sqrt(energy)
    blended = jnp.clip(blended, -4.0, 4.0)
    shared = 0.5 * rough(keys[1], shape) + blended
    noise_level = jnp.exp(jax.random.uniform(keys[4], (1, D), minval=jnp.log(0.12), maxval=jnp.log(1.2)))
    first = shared + noise_level * rough(keys[5], shape)
    second = shared + noise_level * rough(keys[6], shape)
    scale_first = jnp.exp(jax.random.uniform(keys[7], (1, D), minval=jnp.log(0.5), maxval=jnp.log(2.0)))
    scale_second = jnp.exp(jax.random.uniform(keys[8], (1, D), minval=jnp.log(0.5), maxval=jnp.log(2.0)))
    offset_first = jax.random.uniform(keys[9], (1, D), minval=-2.0, maxval=2.0)
    offset_second = jax.random.uniform(keys[10], (1, D), minval=-2.0, maxval=2.0)
    return (offset_first + scale_first * row_scale * first, offset_second + scale_second * row_scale * second)


def draw_first_view(key, part):
    pair = view_pair(key)
    return pair[0]


def draw_second_view(key, part):
    pair = view_pair(key)
    return pair[1]


def setup_inputs(seed: int = 0) -> dict:
    key_of = jax.random.split(jax.random.key(seed), 3)
    first_view = draw_first_view(jax.random.fold_in(key_of[2], 71), 0)
    second_view = draw_second_view(jax.random.fold_in(key_of[2], 71), 0)
    return {"first_view": first_view, "second_view": second_view}


LAMBDA = 0.0051
EPS = 1e-05

def normalize(view, batch):
    mean = lax.optimization_barrier(jnp.sum(view, 0)) / batch
    deviation = view - mean
    variance = lax.optimization_barrier(jnp.sum(deviation * deviation, 0)) / batch
    inverse = lax.rsqrt(variance + EPS)
    return (deviation * inverse, inverse)

def backward(grad_norm, norm, inverse, batch):
    first_mean = lax.optimization_barrier(jnp.sum(grad_norm, 0)) / batch
    second_mean = lax.optimization_barrier(jnp.sum(grad_norm * norm, 0)) / batch
    return inverse * (grad_norm - first_mean - norm * second_mean)

def reference(first_view, second_view):
    batch = first_view.shape[0]
    width = first_view.shape[1]
    norm_first, rstd_first = normalize(first_view, batch)
    norm_second, rstd_second = normalize(second_view, batch)
    sent_first = norm_first.astype(jnp.bfloat16)
    sent_second = norm_second.astype(jnp.bfloat16)
    corr = jnp.dot(sent_first.T, sent_second, preferred_element_type=jnp.float32) / batch
    index = jnp.arange(width, dtype=jnp.int32)
    on_diag = index[:, None] == index[None, :]
    grad_corr = jnp.where(on_diag, -2.0 * (1.0 - corr), 2.0 * LAMBDA * corr).astype(jnp.bfloat16)
    grad_norm_first = jnp.dot(sent_second, grad_corr.T, preferred_element_type=jnp.float32)
    grad_norm_second = jnp.dot(sent_first, grad_corr, preferred_element_type=jnp.float32)
    grad_first = backward(grad_norm_first, norm_first, rstd_first, batch)
    grad_second = backward(grad_norm_second, norm_second, rstd_second, batch)
    return (grad_first, grad_second)
```

```python
import jax
import jax.numpy as jnp
from jax import lax
from jax.experimental import pallas as pl
from jax.experimental.pallas import tpu as pltpu
from jax.sharding import PartitionSpec as P

LAMBDA = 0.0051
EPS = 1e-05
MESH = pl.DeviceIdType.MESH
F32 = jnp.float32
BF16 = jnp.bfloat16
BATCH = 8192

OWN = (2, 1, 8, 9, 3, 7, 10, 11)
STAT_SIB = (1, 2, 0, 4)
STAT_NON = (1, 2, 5, 6)
KB = (2, 3, 6, 7)
AB = (0, 1, 4, 5)

M_Y = 0
M_ST1 = 11
M_ST2 = 16
M_C = 23
M_ZR = 31
M_ZG = 47
M_GD = 63
M_P1O = 79
M_P1S = 81
M_P1N = 83
M_P2O = 85
M_P2R = 87
M_P2L = 89
M_X = 91
M_ALL = 92

HIGH = lax.Precision.HIGHEST


def nt(a, b, precision=None):
    return lax.dot_general(
        a, b, (((1,), (1,)), ((), ())), preferred_element_type=F32, precision=precision
    )


def tn(a, b, precision=None):
    return lax.dot_general(
        a, b, (((0,), (0,)), ((), ())), preferred_element_type=F32, precision=precision
    )


def nn(a, b):
    return lax.dot_general(a, b, (((1,), (0,)), ((), ())), preferred_element_type=F32)


def ab(a):
    return a + 2 * lax.div(a, 2)


def kb(k):
    return k + 2 + 2 * lax.div(k, 2)


def kernel(
    first, second, out1, out2,
    raw, cen, oth, xt, stat, smsg, st1, st2m, st2, fin, scl, fix, nrm, cown, csend, crecv, zs, zr, g,
    acc1, acc2, rsq, csq, rowsq, colsq,
    p1, p1in, p1relay, p2, p2in, p2relay, xs, xr, ob1, ob2, ss, rs, ls, os_,
):
    dp = lax.axis_index("dp")
    rep = lax.axis_index("replica")
    c = lax.rem(dp, 2)
    ylo = lax.rem(lax.div(dp, 2), 2)
    z = lax.div(dp, 4)
    yhi = lax.div(rep, 4)
    x = lax.rem(rep, 4)

    def dev(x_, yhi_, ylo_, z_, c_):
        return (z_ * 4 + ylo_ * 2 + c_, yhi_ * 4 + x_)

    core = dev(x, yhi, ylo, z, 1 - c)
    sib = dev(x, yhi, 1 - ylo, z, c)
    sibc = dev(x, yhi, 1 - ylo, z, 1 - c)
    non = dev(x, 1 - yhi, 1 - ylo, z, c)
    nonc = dev(x, 1 - yhi, 1 - ylo, z, 1 - c)
    right = dev(lax.rem(x + 1, 4), yhi, ylo, z, c)
    left = dev(lax.rem(x + 3, 4), yhi, ylo, z, c)
    zdev = [dev(x, yhi, ylo, lax.rem(z + q, 8), c) for q in range(8)]
    zto = (zdev[1], zdev[7])

    def load(i, ref, col):
        return pltpu.make_async_copy(
            ref.at[:, pl.ds(pl.multiple_of(col, 256), 256)], raw.at[i], ls.at[i]
        )

    pieces = [lax.rem(x + k, 4) * 512 for k in range(4)]
    base = yhi * 2048
    mine = x * 512
    lo = ylo * 256
    hi = 256 - lo
    loads = [
        load(0, second, base + pieces[0] + hi),
        load(1, first, base + mine + hi),
        load(2, first, base + mine + lo),
        load(3, first, 2048 - base + mine + lo),
        load(4, second, base + pieces[1] + hi),
        load(5, second, 2048 - base + pieces[2] + hi),
        load(6, second, 2048 - base + pieces[3] + hi),
        load(7, first, 2048 - base + mine + hi),
    ] + [load(8 + k, second, base + pieces[k] + lo) for k in range(4)]
    for cp in loads:
        cp.start()

    barrier = pltpu.get_barrier_semaphore()
    partners = [core, sib, sibc, non, nonc, right, left] + zdev[1:]
    for d in partners:
        pl.semaphore_signal(barrier, inc=1, device_id=d, device_id_type=MESH)

    def make(i, src, dst, to):
        return pltpu.make_async_remote_copy(
            src_ref=src, dst_ref=dst, send_sem=ss.at[i], recv_sem=rs.at[i], device_id=to, device_id_type=MESH
        )

    sends = []

    def send(i, src, dst, to):
        cp = make(i, src, dst, to)
        cp.start()
        sends.append(cp)
        return cp

    def local_stats(i, carry):
        pltpu.make_async_copy(first.at[:, pl.ds(0, 256)], raw.at[i], ls.at[i]).wait()
        v = raw[i]
        m = jnp.sum(v, 0, keepdims=True) * (1.0 / 256)
        dv = v - m
        r = dv.astype(BF16)
        cen[i] = r
        stat[i, 0:1, :] = m
        stat[i, 1:2, :] = jnp.sum(dv * dv, 0, keepdims=True)
        stat[i, 2:3, :] = jnp.sum(r.astype(F32), 0, keepdims=True)
        stat[i, 3:4, :] = jnp.zeros_like(m)
        return carry

    top, low = pl.ds(0, 128), pl.ds(128, 128)
    lax.fori_loop(0, 1, local_stats, 0)
    pl.semaphore_wait(barrier, len(partners))
    yk0 = send(M_Y + 0, cen.at[0], oth.at[2], sib)
    lax.fori_loop(1, 4, local_stats, 0)
    xin0 = [
        send(M_Y + 1, cen.at[1], oth.at[0], sib),
        send(M_Y + 2, cen.at[1], oth.at[4], non),
    ]
    xin1 = [
        send(M_Y + 3, cen.at[2, top], oth.at[1, top], sib),
        send(M_Y + 4, cen.at[3, low], oth.at[1, low], non),
    ]
    xin2 = [send(M_Y + 5, cen.at[2], oth.at[5], non)]
    lax.fori_loop(4, 12, local_stats, 0)

    def comoment(i, j):
        return jnp.sum((raw[i] - stat[i, 0:1, :]) * (raw[j] - stat[j, 0:1, :]), 0, keepdims=True)

    for n in range(4):
        smsg[0, n] = stat[STAT_SIB[n]]
        smsg[1, n] = stat[STAT_NON[n]]
    for b in range(8):
        st1[0, b] = stat[OWN[b]]
    smsg[0, 0, 3:4, :] = comoment(1, 0)
    st1[0, 0, 3:4, :] = comoment(2, 8)
    st_in = [
        send(M_ST1 + 0, smsg.at[0], st1.at[2, pl.ds(0, 4)], sib),
        send(M_ST1 + 1, smsg.at[1], st1.at[2, pl.ds(4, 4)], non),
        send(M_ST1 + 2, smsg.at[0], st1.at[3, pl.ds(0, 4)], sibc),
        send(M_ST1 + 3, smsg.at[1], st1.at[3, pl.ds(4, 4)], nonc),
        send(M_ST1 + 4, st1.at[0], st1.at[1], core),
    ]
    yk0.wait_recv()
    yk1 = send(M_Y + 6, oth.at[2], oth.at[3], left)
    yk3 = send(M_Y + 7, oth.at[2], oth.at[7], right)
    for a in range(4):
        xt[0, a] = cen[OWN[AB[a]]].T
    for cp in st_in:
        cp.wait_recv()
    yk1.wait_recv()
    yk2 = [send(M_Y + 8, oth.at[3, top], oth.at[6, top], left)]
    yk3.wait_recv()
    yk2.append(send(M_Y + 9, oth.at[7, low], oth.at[6, low], right))

    def merge(rows_of, slots, count):
        devs = []
        res = []
        for b in range(8):
            rows = [rows_of(s, b) for s in range(slots)]
            total = sum(rows[1:], rows[0])
            m = total[0:1] * (1.0 / slots)
            dv = [r[0:1] - m for r in rows]
            m2 = total[1:2] + count * sum([d * d for d in dv[1:]], dv[0] * dv[0])
            devs.append(dv)
            res.append([m, m2, total[2:3], total[3:4]])
        cross = sum([p * q for p, q in zip(devs[0][1:], devs[2][1:])], devs[0][0] * devs[2][0])
        res[0][3] = res[0][3] + count * cross
        return res

    for b, r in enumerate(merge(lambda s, b: st1[s, b], 4, 256.0)):
        for n in range(4):
            st2m[0, b, n : n + 1, :] = r[n]
    for q in range(8):
        zq = lax.rem(z + q, 8)
        fa = ab(2 * c + lax.div(zq, 4))
        fk = kb(lax.rem(zq, 4))
        if q:
            for b in range(8):
                st2m[q, b] = st2m[0, b]
        for s in range(4):
            st2m[q, 8, s : s + 1, :] = st1[s, fa, 0:1, :]
            st2m[q, 9, s : s + 1, :] = st1[s, fk, 0:1, :]
    st2_in = [send(M_ST2 + q - 1, st2m.at[q], st2.at[q - 1], zdev[q]) for q in range(1, 8)]

    for cps, a in ((xin0, (0, 2)), (xin1, (1,)), (xin2, (3,))):
        for cp in cps:
            cp.wait_recv()
        for n in a:
            xt[1, n] = oth[AB[n]].T
    for cp in yk2:
        cp.wait_recv()

    def corr(s, carry):
        r = jnp.where(lax.rem(s, 2) == 1, 4 - lax.div(s + 1, 2), 4 + lax.div(s, 2))
        d = lax.rem(z + r, 8)
        i = lax.div(d, 4)
        k = lax.rem(d, 4)
        y0 = cen[8 + k]
        y1 = oth[kb(k)]
        a = 2 * (1 - c) + i
        csend[s] = (nn(xt[0, a], y0) + nn(xt[1, a], y1)).astype(BF16)
        make(M_C + s, csend.at[s], crecv.at[s], core).start()
        a = 2 * c + i
        cown[s] = nn(xt[0, a], y0) + nn(xt[1, a], y1)
        return carry

    def c_recv(s):
        make(M_C + s, csend.at[s], crecv.at[s], core).wait_recv()

    def zslot(d, t, u):
        return d * 8 + (t - 1) * 2 + u

    z_in = {}

    def chain(t):
        dist = 5 - t
        slot = (8 - 2 * dist - 1, 8 - 2 * dist) if dist < 4 else (0, 0)
        for d in range(2):
            if t > 1 or d == 0:
                c_recv(slot[d])
        for u in range(2):
            for d in range(2):
                if t == 1 and u != d:
                    continue
                n = slot[d]
                v = cown[n, 128 * u : 128 * u + 128] + crecv[n, 128 * u : 128 * u + 128].astype(F32)
                if (d, t - 1, u) in z_in:
                    z_in[(d, t - 1, u)].wait_recv()
                    v = v + zr[zslot(d, t - 1, u)].astype(F32)
                i = zslot(d, t, u)
                zs[i] = v.astype(BF16)
                z_in[(d, t, u)] = send(M_ZR + i, zs.at[i], zr.at[i], zto[d])

    lax.fori_loop(0, 3, corr, 0)
    chain(1)
    lax.fori_loop(3, 8, corr, 0)
    chain(2)

    for cp in st2_in:
        cp.wait_recv()
    whole = merge(lambda s, b: st2m[0, b] if s == 0 else st2[s - 1, b], 8, 1024.0)
    rstds = []
    for b, r in enumerate(whole):
        rstd = lax.rsqrt(r[1] * (1.0 / BATCH) + EPS)
        fin[b, 0:1, :] = r[0] + r[2] * (1.0 / BATCH)
        fin[b, 1:2, :] = rstd
        fin[b, 2:3, :] = r[0]
        fin[b, 3:4, :] = jnp.zeros_like(rstd)
        rstds.append(rstd)
    cii = whole[0][3] * rstds[0] * rstds[2] * (1.0 / BATCH)
    fin[8, 0:1, :] = cii
    fin[8, 1:2, :] = (-2.0 * (1.0 - cii)).astype(BF16).astype(F32)

    def norm(b, carry):
        for src, slot, o in ((None, 0, 0), (oth, 2, 1)):
            shift = st1[slot, b, 0:1, :] - fin[b, 0:1, :]
            scale = fin[b, 1:2, :]
            for h in range(2):
                rows = slice(128 * h, 128 * h + 128)
                v = own_block(b, h) if o == 0 else oth[b, rows]
                nrm[b, o * 256 + 128 * h : o * 256 + 128 * h + 128, :] = (
                    (v.astype(F32) + shift) * scale
                ).astype(BF16)
        return carry

    def own_block(b, h):
        p = lax.div(b, 4)
        q = lax.rem(b, 4)
        view1 = jnp.where(p == 0, 2 - q, 3 + 4 * q)
        idx = jnp.where(q < 2, view1, 6 + q + 2 * p)
        return cen[idx, 128 * h : 128 * h + 128]

    lax.fori_loop(0, 4, norm, 0)
    chain(3)
    lax.fori_loop(4, 8, norm, 0)

    fa = ab(2 * c + lax.div(z, 4))
    fk = kb(lax.rem(z, 4))
    pad = jnp.zeros((7, 256), F32)
    ra = jnp.concatenate([fin[fa, 1:2, :] * (2.0 * LAMBDA / BATCH), pad], 0)
    rk = jnp.concatenate([fin[fk, 1:2, :], pad], 0)
    rows_id = lax.broadcasted_iota(jnp.int32, (256, 256), 0)
    cols_id = lax.broadcasted_iota(jnp.int32, (256, 256), 1)
    off = rows_id + (c + z) * 256 != cols_id
    scl[...] = jnp.where(off, tn(ra, rk, HIGH), 0.0)
    mu_a = [(st2m[0, 8] if s == 0 else st2[s - 1, 8]) - fin[fa, 2:3, :] for s in range(8)]
    mu_k = [(st2m[0, 9] if s == 0 else st2[s - 1, 9]) - fin[fk, 2:3, :] for s in range(8)]
    fix[...] = scl[...] * tn(jnp.concatenate(mu_a, 0) * 256.0, jnp.concatenate(mu_k, 0), HIGH)
    chain(4)

    for n in range(4):
        acc1[n] = jnp.zeros((512, 256), F32)
        acc2[n] = jnp.zeros((512, 256), F32)
    rsq[...] = jnp.zeros_like(rsq)
    csq[...] = jnp.zeros_like(csq)

    c_recv(7)
    g_in = {}
    for u in range(2):
        rows = slice(128 * u, 128 * u + 128)
        v = cown[7, rows] + crecv[7, rows].astype(F32)
        for d in range(2):
            z_in[(d, 4, u)].wait_recv()
            v = v + zr[zslot(d, 4, u)].astype(F32)
        g[c, z, u] = (v * scl[rows] + fix[rows]).astype(BF16)
        for d in range(2):
            i = zslot(d, 1, u)
            send(M_ZG + i, g.at[c, z, u], g.at[c, z, u], zto[d])
        send(M_GD + 14 + u, g.at[c, z, u], g.at[c, z, u], core)

    def gather_step(t, last):
        for u in range(2):
            for d in range(2):
                if last and u != d:
                    continue
                i = d * 8 + (t - 1) * 2 + u
                source = lax.rem(z + (8 - t if d == 0 else t), 8)
                part = g.at[c, source, u]
                make(M_ZG + i, part, part, zto[d]).wait_recv()
                if not last:
                    onward = make(M_ZG + i + 2, part, part, zto[d])
                    if u == d:
                        onward.start()
                    else:
                        pl.when(t < 3)(onward.start)
                make(M_GD + (d * 7 + 6 if last else d * 7 + (t - 1) * 2 + u), part, part, core).start()

    def use(j, zs_):
        a = 2 * j + lax.div(zs_, 4)
        k = lax.rem(zs_, 4)
        ga = g[j, zs_].reshape(256, 256)
        acc1[a] += nt(nrm[kb(k)], ga)
        acc2[k] += nn(nrm[ab(a)], ga)
        v = ga.astype(F32)
        s = v * v
        rsq[a] += s[:, 0:128] + s[:, 128:256]
        csq[k] += jnp.sum(s.reshape(32, 8, 256), 0)

    def from_core(i):
        part = g.at[0, 0, 0]
        make(M_GD + i, part, part, core).wait_recv()

    use(c, z)
    from_core(14)
    from_core(15)
    use(1 - c, z)

    def step(t, carry):
        gather_step(t, False)

        def two(n, inner):
            use(c, lax.rem(z + (8 - t) + n * 2 * t, 8))
            return inner

        lax.fori_loop(0, 2, two, 0)

        def two_other(n, inner):
            for u in range(2):
                from_core(n * 7 + (t - 1) * 2 + u)
            use(1 - c, lax.rem(z + (8 - t) + n * 2 * t, 8))
            return inner

        lax.fori_loop(0, 2, two_other, 0)
        return carry

    lax.fori_loop(1, 4, step, 0)
    gather_step(4, True)

    def final_two(n, carry):
        use(lax.rem(c + n, 2), lax.rem(z + 4, 8))
        return carry

    from_core(6)
    from_core(13)
    lax.fori_loop(0, 2, final_two, 0)

    for a in range(4):
        rowsq[a] = nt(jnp.ones((8, 128), F32), rsq[a], HIGH) * (0.5 / LAMBDA)
        colsq[a] = jnp.sum(csq[a], 0, keepdims=True) * (0.5 / LAMBDA)

    def partial1(a, o):
        b = AB[a]
        rows = slice(o * 256, o * 256 + 256)
        f = nrm[b, rows].astype(F32)
        v = acc1[a, rows] - f * rowsq[a, 0:1, :]
        if a == 0:
            v = v + (nrm[2, rows].astype(F32) - f * fin[8, 0:1, :]) * fin[8, 1:2, :]
        return v * fin[b, 1:2, :]

    def partial2(k, o):
        b = KB[k]
        rows = slice(o * 256, o * 256 + 256)
        s = nrm[b, rows].astype(F32)
        v = acc2[k, rows] - s * colsq[k]
        if k == 0:
            v = v + (nrm[0, rows].astype(F32) - s * fin[8, 0:1, :]) * fin[8, 1:2, :]
        return v * fin[b, 1:2, :]

    p2[2, 0] = partial2(2, 0).astype(BF16)
    relay2 = [send(M_P2O + 0, p2.at[2, 0], p2relay.at[0], right)]
    p2[2, 1] = partial2(2, 1).astype(BF16)
    relay2.append(send(M_P2O + 1, p2.at[2, 1], p2relay.at[1], left))
    p1[0, 2] = partial1(2, 0).astype(BF16)
    relay1 = [send(M_P1O + 0, p1.at[0, 2], p1relay.at[0], sib)]
    p1[0, 3] = partial1(3, 0).astype(BF16)
    relay1.append(send(M_P1O + 1, p1.at[0, 3], p1relay.at[1], non))
    p2[1, 1] = partial2(1, 1).astype(BF16)
    in2 = [send(M_P2R + 1, p2.at[1, 1], p2in.at[0, 1], right)]
    p2[3, 0] = partial2(3, 0).astype(BF16)
    in2.append(send(M_P2L + 0, p2.at[3, 0], p2in.at[1, 0], left))
    p1[1, 2] = partial1(2, 1).astype(BF16)
    in1 = [send(M_P1N + 1, p1.at[1, 2], p1in.at[1, 1], non)]
    p1[1, 1] = partial1(1, 1).astype(BF16)
    in1.append(send(M_P1S + 0, p1.at[1, 1], p1in.at[0, 0], sib))
    v1 = partial2(1, 0)
    relay2[0].wait_recv()
    p2[1, 0] = (v1 + p2relay[0].astype(F32)).astype(BF16)
    in2.append(send(M_P2R + 0, p2.at[1, 0], p2in.at[0, 0], right))
    v3 = partial2(3, 1)
    relay2[1].wait_recv()
    p2[3, 1] = (v3 + p2relay[1].astype(F32)).astype(BF16)
    in2.append(send(M_P2L + 1, p2.at[3, 1], p2in.at[1, 1], left))
    v = partial1(3, 1)
    relay1[0].wait_recv()
    p1[1, 3] = (v + p1relay[0].astype(F32)).astype(BF16)
    in1.append(send(M_P1N + 0, p1.at[1, 3], p1in.at[1, 0], non))
    v = partial1(0, 1)
    relay1[1].wait_recv()
    p1[1, 0] = (v + p1relay[1].astype(F32)).astype(BF16)
    in1.append(send(M_P1S + 1, p1.at[1, 0], p1in.at[0, 1], sib))

    ob1[0] = partial1(0, 0)
    ob1[1] = partial1(1, 0)
    ob2[0] = partial2(0, 1)
    ob2[1] = partial2(0, 0)
    for cp in in2:
        cp.wait_recv()
    xs[...] = (ob2[0] + p2in[0, 1].astype(F32) + p2in[1, 1].astype(F32)).astype(BF16)
    x_in = send(M_X, xs, xr, sib)
    outs = []

    def put(src, ref, col, i):
        cp = pltpu.make_async_copy(src, ref.at[:, pl.ds(pl.multiple_of(col, 256), 256)], os_.at[i])
        cp.start()
        outs.append(cp)

    ob2[1] = ob2[1] + p2in[0, 0].astype(F32) + p2in[1, 0].astype(F32)
    put(ob2.at[1], out2, lo, 0)
    for cp in in1:
        cp.wait_recv()
    for e in range(2):
        ob1[e] = ob1[e] + p1in[0, e].astype(F32) + p1in[1, e].astype(F32)
        put(ob1.at[e], out1, lo if e == 0 else hi, 1 + e)
    x_in.wait_recv()
    ob2[0] = xr[...].astype(F32)
    put(ob2.at[0], out2, hi, 3)
    for cp in outs:
        cp.wait()
    for cp in sends:
        cp.wait_send()

    def sent(i, part):
        make(i, part, part, core).wait_send()

    for s in range(8):
        sent(M_C + s, csend.at[s])
    for d in range(2):
        for t in range(2, 5):
            for u in range(2):
                if t < 4 or u == d:
                    sent(M_ZG + zslot(d, t, u), g.at[0, 0, 0])
    for i in range(14):
        sent(M_GD + i, g.at[0, 0, 0])


def body(first, second):
    v = pltpu.VMEM
    out = jax.ShapeDtypeStruct((256, 512), F32)
    anywhere = pl.BlockSpec(memory_space=pl.ANY)
    return pl.pallas_call(
        kernel,
        out_shape=(out, out),
        in_specs=[anywhere, anywhere],
        out_specs=(anywhere, anywhere),
        scratch_shapes=[
            v((12, 256, 256), F32),
            v((12, 256, 256), BF16),
            v((8, 256, 256), BF16),
            v((2, 4, 256, 256), BF16),
            v((12, 4, 256), F32),
            v((2, 4, 4, 256), F32),
            v((4, 8, 4, 256), F32),
            v((8, 10, 4, 256), F32),
            v((7, 10, 4, 256), F32),
            v((9, 4, 256), F32),
            v((256, 256), F32),
            v((256, 256), F32),
            v((8, 512, 256), BF16),
            v((8, 256, 256), F32),
            v((8, 256, 256), BF16),
            v((8, 256, 256), BF16),
            v((16, 128, 256), BF16),
            v((16, 128, 256), BF16),
            v((2, 8, 2, 128, 256), BF16),
            v((4, 512, 256), F32),
            v((4, 512, 256), F32),
            v((4, 256, 128), F32),
            v((4, 8, 256), F32),
            v((4, 8, 256), F32),
            v((4, 1, 256), F32),
            v((2, 4, 256, 256), BF16),
            v((2, 2, 256, 256), BF16),
            v((2, 256, 256), BF16),
            v((4, 2, 256, 256), BF16),
            v((2, 2, 256, 256), BF16),
            v((2, 256, 256), BF16),
            v((256, 256), BF16),
            v((256, 256), BF16),
            v((2, 256, 256), F32),
            v((2, 256, 256), F32),
            pltpu.SemaphoreType.DMA((M_ALL,)),
            pltpu.SemaphoreType.DMA((M_ALL,)),
            pltpu.SemaphoreType.DMA((12,)),
            pltpu.SemaphoreType.DMA((4,)),
        ],
        compiler_params=pltpu.CompilerParams(
            collective_id=0, has_side_effects=True, vmem_limit_bytes=56 * 1024 * 1024
        ),
    )(first, second)


def solution(mesh):
    return jax.shard_map(
        body,
        mesh=mesh,
        in_specs=(P("dp", None), P("dp", None)),
        out_specs=(P("dp", "replica"), P("dp", "replica")),
        check_vma=False,
    )
```

```python
import jax
import jax.numpy as jnp
from jax import lax
from jax.experimental import pallas as pl
from jax.experimental.pallas import tpu as pltpu
from jax.sharding import PartitionSpec as P

LAMBDA = 0.0051
EPS = 1e-05
MESH = pl.DeviceIdType.MESH
F32 = jnp.float32
BF16 = jnp.bfloat16
BATCH = 8192

OWN = (3, 2, 9, 10, 7, 8, 11, 12)
STAT_SIB = (2, 3, 0, 4)
STAT_NON = (2, 3, 5, 6)
KB = (2, 3, 6, 7)
AB = (0, 1, 4, 5)

M_Y = 0
M_ST1 = 12
M_ST2 = 17
M_C = 24
M_ZR = 32
M_ZG = 48
M_GD = 64
M_P1O = 84
M_P1S = 86
M_P1N = 88
M_P2O = 90
M_P2R = 94
M_P2L = 98
M_X = 102
M_ALL = 103

HIGH = lax.Precision.HIGHEST


def nt(a, b, precision=None):
    return lax.dot_general(
        a, b, (((1,), (1,)), ((), ())), preferred_element_type=F32, precision=precision
    )


def tn(a, b, precision=None):
    return lax.dot_general(
        a, b, (((0,), (0,)), ((), ())), preferred_element_type=F32, precision=precision
    )


def nn(a, b):
    return lax.dot_general(a, b, (((1,), (0,)), ((), ())), preferred_element_type=F32)


def ab(a):
    return a + 2 * lax.div(a, 2)


def kb(k):
    return k + 2 + 2 * lax.div(k, 2)


def kernel(
    first, second, out1, out2,
    raw, cen, oth, xt, stat, smsg, st1, st2m, st2, fin, scl, fix, nrm, cown, csend, crecv, zs, zr, g,
    acc1, acc2, rsq, csq, rowsq, colsq,
    p1, p1in, p1relay, p2, p2in, p2relay, xs, xr, ob1, ob2, ss, rs, ls, os_,
):
    dp = lax.axis_index("dp")
    rep = lax.axis_index("replica")
    c = lax.rem(dp, 2)
    ylo = lax.rem(lax.div(dp, 2), 2)
    z = lax.div(dp, 4)
    yhi = lax.div(rep, 4)
    x = lax.rem(rep, 4)

    def dev(x_, yhi_, ylo_, z_, c_):
        return (z_ * 4 + ylo_ * 2 + c_, yhi_ * 4 + x_)

    core = dev(x, yhi, ylo, z, 1 - c)
    sib = dev(x, yhi, 1 - ylo, z, c)
    sibc = dev(x, yhi, 1 - ylo, z, 1 - c)
    non = dev(x, 1 - yhi, 1 - ylo, z, c)
    nonc = dev(x, 1 - yhi, 1 - ylo, z, 1 - c)
    right = dev(lax.rem(x + 1, 4), yhi, ylo, z, c)
    left = dev(lax.rem(x + 3, 4), yhi, ylo, z, c)
    zdev = [dev(x, yhi, ylo, lax.rem(z + q, 8), c) for q in range(8)]
    zto = (zdev[1], zdev[7])

    def load(i, ref, col):
        return pltpu.make_async_copy(
            ref.at[:, pl.ds(pl.multiple_of(col, 256), 256)], raw.at[i], ls.at[i]
        )

    pieces = [lax.rem(x + k, 4) * 512 for k in range(4)]
    base = yhi * 2048
    mine = x * 512
    lo = ylo * 256
    hi = 256 - lo
    loads = [
        load(0, second, base + pieces[0] + hi),
        load(1, second, 2048 - base + pieces[0] + hi),
        load(2, first, base + mine + hi),
        load(3, first, base + mine + lo),
        load(4, second, base + pieces[1] + hi),
        load(5, second, 2048 - base + pieces[2] + hi),
        load(6, second, 2048 - base + pieces[3] + hi),
        load(7, first, 2048 - base + mine + lo),
        load(8, first, 2048 - base + mine + hi),
    ] + [load(9 + k, second, base + pieces[k] + lo) for k in range(4)]
    for cp in loads:
        cp.start()

    barrier = pltpu.get_barrier_semaphore()
    partners = [core, sib, sibc, non, nonc, right, left] + zdev[1:]
    for d in partners:
        pl.semaphore_signal(barrier, inc=1, device_id=d, device_id_type=MESH)

    def make(i, src, dst, to):
        return pltpu.make_async_remote_copy(
            src_ref=src, dst_ref=dst, send_sem=ss.at[i], recv_sem=rs.at[i], device_id=to, device_id_type=MESH
        )

    sends = []

    def send(i, src, dst, to):
        cp = make(i, src, dst, to)
        cp.start()
        sends.append(cp)
        return cp

    def local_stats(i, carry):
        pltpu.make_async_copy(first.at[:, pl.ds(0, 256)], raw.at[i], ls.at[i]).wait()
        v = raw[i]
        m = jnp.sum(v, 0, keepdims=True) * (1.0 / 256)
        dv = v - m
        r = dv.astype(BF16)
        cen[i] = r
        stat[i, 0:1, :] = m
        stat[i, 1:2, :] = jnp.sum(dv * dv, 0, keepdims=True)
        stat[i, 2:3, :] = jnp.sum(r.astype(F32), 0, keepdims=True)
        stat[i, 3:4, :] = jnp.zeros_like(m)
        return carry

    top, low = pl.ds(0, 128), pl.ds(128, 128)
    lax.fori_loop(0, 2, local_stats, 0)
    pl.semaphore_wait(barrier, len(partners))
    y_top = send(M_Y + 0, cen.at[0, top], oth.at[2, top], sib)
    y_low = send(M_Y + 1, cen.at[1, low], oth.at[2, low], non)
    lax.fori_loop(2, 4, local_stats, 0)
    x_in = [
        send(M_Y + 2, cen.at[2], oth.at[0], sib),
        send(M_Y + 3, cen.at[2], oth.at[4], non),
        send(M_Y + 4, cen.at[3], oth.at[1], sib),
        send(M_Y + 5, cen.at[3], oth.at[5], non),
    ]
    lax.fori_loop(4, 13, local_stats, 0)

    def comoment(i, j):
        return jnp.sum((raw[i] - stat[i, 0:1, :]) * (raw[j] - stat[j, 0:1, :]), 0, keepdims=True)

    for n in range(4):
        smsg[0, n] = stat[STAT_SIB[n]]
        smsg[1, n] = stat[STAT_NON[n]]
    for b in range(8):
        st1[0, b] = stat[OWN[b]]
    smsg[0, 0, 3:4, :] = comoment(2, 0)
    st1[0, 0, 3:4, :] = comoment(3, 9)
    st_in = [
        send(M_ST1 + 0, smsg.at[0], st1.at[2, pl.ds(0, 4)], sib),
        send(M_ST1 + 1, smsg.at[1], st1.at[2, pl.ds(4, 4)], non),
        send(M_ST1 + 2, smsg.at[0], st1.at[3, pl.ds(0, 4)], sibc),
        send(M_ST1 + 3, smsg.at[1], st1.at[3, pl.ds(4, 4)], nonc),
        send(M_ST1 + 4, st1.at[0], st1.at[1], core),
    ]
    y_top.wait_recv()
    t1 = send(M_Y + 6, oth.at[2, top], oth.at[3, top], left)
    t3 = send(M_Y + 7, oth.at[2, top], oth.at[7, top], right)
    y_low.wait_recv()
    l1 = send(M_Y + 8, oth.at[2, low], oth.at[3, low], left)
    l3 = send(M_Y + 9, oth.at[2, low], oth.at[7, low], right)
    for a in range(4):
        xt[0, a] = cen[OWN[AB[a]]].T
    t1.wait_recv()
    yk2 = [send(M_Y + 10, oth.at[3, top], oth.at[6, top], left)]
    t3.wait_recv()
    l3.wait_recv()
    yk2.append(send(M_Y + 11, oth.at[7, low], oth.at[6, low], right))
    for cp in st_in:
        cp.wait_recv()

    def merge(rows_of, slots, count):
        devs = []
        res = []
        for b in range(8):
            rows = [rows_of(s, b) for s in range(slots)]
            total = sum(rows[1:], rows[0])
            m = total[0:1] * (1.0 / slots)
            dv = [r[0:1] - m for r in rows]
            m2 = total[1:2] + count * sum([d * d for d in dv[1:]], dv[0] * dv[0])
            devs.append(dv)
            res.append([m, m2, total[2:3], total[3:4]])
        cross = sum([p * q for p, q in zip(devs[0][1:], devs[2][1:])], devs[0][0] * devs[2][0])
        res[0][3] = res[0][3] + count * cross
        return res

    for b, r in enumerate(merge(lambda s, b: st1[s, b], 4, 256.0)):
        for n in range(4):
            st2m[0, b, n : n + 1, :] = r[n]
    for q in range(8):
        zq = lax.rem(z + q, 8)
        fa = ab(2 * c + lax.div(zq, 4))
        fk = kb(lax.rem(zq, 4))
        if q:
            for b in range(8):
                st2m[q, b] = st2m[0, b]
        for s in range(4):
            st2m[q, 8, s : s + 1, :] = st1[s, fa, 0:1, :]
            st2m[q, 9, s : s + 1, :] = st1[s, fk, 0:1, :]
    st2_in = [send(M_ST2 + q - 1, st2m.at[q], st2.at[q - 1], zdev[q]) for q in range(1, 8)]

    for n in range(4):
        acc1[n] = jnp.zeros((512, 256), F32)
        acc2[n] = jnp.zeros((512, 256), F32)
    rsq[...] = jnp.zeros_like(rsq)
    csq[...] = jnp.zeros_like(csq)
    for cp, n in zip(x_in, (0, 2, 1, 3)):
        cp.wait_recv()
        xt[1, n] = oth[AB[n]].T
    l1.wait_recv()
    for cp in yk2:
        cp.wait_recv()

    def corr(s, carry):
        r = jnp.where(lax.rem(s, 2) == 1, 4 - lax.div(s + 1, 2), 4 + lax.div(s, 2))
        d = lax.rem(z + r, 8)
        i = lax.div(d, 4)
        k = lax.rem(d, 4)
        y0 = cen[9 + k]
        y1 = oth[kb(k)]
        a = 2 * (1 - c) + i
        csend[s] = (nn(xt[0, a], y0) + nn(xt[1, a], y1)).astype(BF16)
        make(M_C + s, csend.at[s], crecv.at[s], core).start()
        a = 2 * c + i
        cown[s] = nn(xt[0, a], y0) + nn(xt[1, a], y1)
        return carry

    def c_recv(s):
        make(M_C + s, csend.at[s], crecv.at[s], core).wait_recv()

    def zslot(d, t, u):
        return d * 8 + (t - 1) * 2 + u

    z_in = {}

    def chain(t, far):
        dist = 5 - t
        slot = (7 - 2 * dist, 8 - 2 * dist) if dist < 4 else (0, 0)
        if (t, far) in ((1, True), (2, False), (3, False), (4, False)):
            c_recv(slot[0])
            if t > 1:
                c_recv(slot[1])
        for d in range(2):
            u = d if far else 1 - d
            n = slot[d]
            rows = slice(128 * u, 128 * u + 128)
            v = cown[n, rows] + crecv[n, rows].astype(F32)
            if (d, t - 1, u) in z_in:
                z_in[(d, t - 1, u)].wait_recv()
                v = v + zr[zslot(d, t - 1, u)].astype(F32)
            i = zslot(d, t, u)
            zs[i] = v.astype(BF16)
            z_in[(d, t, u)] = send(M_ZR + i, zs.at[i], zr.at[i], zto[d])

    lax.fori_loop(0, 3, corr, 0)
    chain(1, True)
    chain(2, False)
    lax.fori_loop(3, 5, corr, 0)
    chain(2, True)
    lax.fori_loop(5, 8, corr, 0)
    chain(3, False)

    for cp in st2_in:
        cp.wait_recv()
    whole = merge(lambda s, b: st2m[0, b] if s == 0 else st2[s - 1, b], 8, 1024.0)
    rstds = []
    for b, r in enumerate(whole):
        rstd = lax.rsqrt(r[1] * (1.0 / BATCH) + EPS)
        fin[b, 0:1, :] = r[0] + r[2] * (1.0 / BATCH)
        fin[b, 1:2, :] = rstd
        fin[b, 2:3, :] = r[0]
        fin[b, 3:4, :] = jnp.zeros_like(rstd)
        rstds.append(rstd)
    cii = whole[0][3] * rstds[0] * rstds[2] * (1.0 / BATCH)
    fin[8, 0:1, :] = cii
    fin[8, 1:2, :] = (-2.0 * (1.0 - cii)).astype(BF16).astype(F32)

    def norm(b, carry):
        for src, slot, o in ((None, 0, 0), (oth, 2, 1)):
            shift = st1[slot, b, 0:1, :] - fin[b, 0:1, :]
            scale = fin[b, 1:2, :]
            for h in range(2):
                rows = slice(128 * h, 128 * h + 128)
                v = own_block(b, h) if o == 0 else oth[b, rows]
                nrm[b, o * 256 + 128 * h : o * 256 + 128 * h + 128, :] = (
                    (v.astype(F32) + shift) * scale
                ).astype(BF16)
        return carry

    def own_block(b, h):
        p = lax.div(b, 4)
        q = lax.rem(b, 4)
        idx = jnp.where(q < 2, jnp.where(p == 0, 3 - q, 7 + q), 7 + q + 2 * p)
        return cen[idx, 128 * h : 128 * h + 128]

    chain(3, True)
    lax.fori_loop(0, 4, norm, 0)
    chain(4, False)
    lax.fori_loop(4, 8, norm, 0)

    fa = ab(2 * c + lax.div(z, 4))
    fk = kb(lax.rem(z, 4))
    pad = jnp.zeros((7, 256), F32)
    ra = jnp.concatenate([fin[fa, 1:2, :] * (2.0 * LAMBDA / BATCH), pad], 0)
    rk = jnp.concatenate([fin[fk, 1:2, :], pad], 0)
    rows_id = lax.broadcasted_iota(jnp.int32, (256, 256), 0)
    cols_id = lax.broadcasted_iota(jnp.int32, (256, 256), 1)
    off = rows_id + (c + z) * 256 != cols_id
    scl[...] = jnp.where(off, tn(ra, rk, HIGH), 0.0)
    mu_a = [(st2m[0, 8] if s == 0 else st2[s - 1, 8]) - fin[fa, 2:3, :] for s in range(8)]
    mu_k = [(st2m[0, 9] if s == 0 else st2[s - 1, 9]) - fin[fk, 2:3, :] for s in range(8)]
    fix[...] = scl[...] * tn(jnp.concatenate(mu_a, 0) * 256.0, jnp.concatenate(mu_k, 0), HIGH)
    chain(4, True)

    c_recv(7)
    for u in range(2):
        rows = slice(128 * u, 128 * u + 128)
        v = cown[7, rows] + crecv[7, rows].astype(F32)
        for d in (1 - u, u):
            z_in[(d, 4, u)].wait_recv()
            v = v + zr[zslot(d, 4, u)].astype(F32)
        g[c, z, u] = (v * scl[rows] + fix[rows]).astype(BF16)
        for d in (u, 1 - u):
            i = zslot(d, 1, u)
            send(M_ZG + i, g.at[c, z, u], g.at[c, z, u], zto[d])
        send(M_GD + u, g.at[c, z, u], g.at[c, z, u], core)

    def arrive(t, far, onward):
        for d in range(2):
            u = d if far else 1 - d
            i = d * 8 + (t - 1) * 2 + u
            source = lax.rem(z + (8 - t if d == 0 else t), 8)
            part = g.at[c, source, u]
            make(M_ZG + i, part, part, zto[d]).wait_recv()
            if onward is not None:
                start = make(M_ZG + i + 2, part, part, zto[d]).start
                if onward is True:
                    start()
                else:
                    pl.when(onward)(start)
            make(M_GD + 4 * t + 2 * d + u, part, part, core).start()

    def use(j, zs_):
        a = 2 * j + lax.div(zs_, 4)
        k = lax.rem(zs_, 4)
        ga = g[j, zs_].reshape(256, 256)
        acc1[a] += nt(nrm[kb(k)], ga)
        acc2[k] += nn(nrm[ab(a)], ga)
        v = ga.astype(F32)
        s = v * v
        rsq[a] += s[:, 0:128] + s[:, 128:256]
        csq[k] += jnp.sum(s.reshape(32, 8, 256), 0)

    def from_core(t, d, u):
        part = g.at[0, 0, 0]
        make(M_GD + 4 * t + 2 * d + u, part, part, core).wait_recv()

    def uses(t, mine_too):
        def one(n, inner):
            if not mine_too:
                for u in range(2):
                    from_core(t, n, u)
            use(c if mine_too else 1 - c, lax.rem(z + (8 - t) + n * 2 * t, 8))
            return inner

        lax.fori_loop(0, jnp.where(t == 0, 1, 2), one, 0)

    uses(0, True)

    def step(t, carry):
        arrive(t, True, True)
        uses(t - 1, False)
        arrive(t, False, t < 3)
        uses(t, True)
        return carry

    lax.fori_loop(1, 4, step, 0)
    uses(3, False)
    arrive(4, True, None)

    def final_two(n, carry):
        use(lax.rem(c + n, 2), lax.rem(z + 4, 8))
        return carry

    lax.fori_loop(0, 1, final_two, 0)
    from_core(4, 0, 0)
    from_core(4, 1, 1)
    lax.fori_loop(1, 2, final_two, 0)

    for a in range(4):
        rowsq[a] = nt(jnp.ones((8, 128), F32), rsq[a], HIGH) * (0.5 / LAMBDA)
        colsq[a] = jnp.sum(csq[a], 0, keepdims=True) * (0.5 / LAMBDA)

    def partial1(a, o):
        b = AB[a]
        rows = slice(o * 256, o * 256 + 256)
        f = nrm[b, rows].astype(F32)
        v = acc1[a, rows] - f * rowsq[a, 0:1, :]
        if a == 0:
            v = v + (nrm[2, rows].astype(F32) - f * fin[8, 0:1, :]) * fin[8, 1:2, :]
        return v * fin[b, 1:2, :]

    def partial2(k, o):
        b = KB[k]
        rows = slice(o * 256, o * 256 + 256)
        s = nrm[b, rows].astype(F32)
        v = acc2[k, rows] - s * colsq[k]
        if k == 0:
            v = v + (nrm[0, rows].astype(F32) - s * fin[8, 0:1, :]) * fin[8, 1:2, :]
        return v * fin[b, 1:2, :]

    def p2_relay(o):
        p2[2, o] = partial2(2, o).astype(BF16)
        return [
            send(M_P2O + 2 * o, p2.at[2, o, top], p2relay.at[o, top], right),
            send(M_P2O + 2 * o + 1, p2.at[2, o, low], p2relay.at[o, low], left),
        ]

    def p2_send(o):
        p2[1, o] = partial2(1, o).astype(BF16)
        a = send(M_P2R + 2 * o, p2.at[1, o, low], p2in.at[0, o, low], right)
        p2[3, o] = partial2(3, o).astype(BF16)
        return [a, send(M_P2L + 2 * o, p2.at[3, o, top], p2in.at[1, o, top], left)]

    def p2_add(o, relay):
        relay[0].wait_recv()
        p2[1, o, top] = (p2[1, o, top].astype(F32) + p2relay[o, top].astype(F32)).astype(BF16)
        a = send(M_P2R + 2 * o + 1, p2.at[1, o, top], p2in.at[0, o, top], right)
        relay[1].wait_recv()
        p2[3, o, low] = (p2[3, o, low].astype(F32) + p2relay[o, low].astype(F32)).astype(BF16)
        return [a, send(M_P2L + 2 * o + 1, p2.at[3, o, low], p2in.at[1, o, low], left)]

    relay2 = p2_relay(1)
    p1[0, 2] = partial1(2, 0).astype(BF16)
    relay1 = [send(M_P1O + 0, p1.at[0, 2], p1relay.at[0], sib)]
    p1[0, 3] = partial1(3, 0).astype(BF16)
    relay1.append(send(M_P1O + 1, p1.at[0, 3], p1relay.at[1], non))
    in2 = p2_send(1)
    relay20 = p2_relay(0)
    p1[1, 2] = partial1(2, 1).astype(BF16)
    in1 = [send(M_P1N + 1, p1.at[1, 2], p1in.at[1, 1], non)]
    p1[1, 1] = partial1(1, 1).astype(BF16)
    in1.append(send(M_P1S + 0, p1.at[1, 1], p1in.at[0, 0], sib))
    in2 += p2_add(1, relay2)
    in20 = p2_send(0)
    ob1[0] = partial1(3, 1)
    ob1[1] = partial1(0, 1)
    ob2[0] = partial2(0, 1)
    ob2[1] = partial2(0, 0)
    relay1[0].wait_recv()
    p1[1, 3] = (ob1[0] + p1relay[0].astype(F32)).astype(BF16)
    in1.append(send(M_P1N + 0, p1.at[1, 3], p1in.at[1, 0], non))
    relay1[1].wait_recv()
    p1[1, 0] = (ob1[1] + p1relay[1].astype(F32)).astype(BF16)
    in20 += p2_add(0, relay20)
    for cp in in2:
        cp.wait_recv()
    xs[...] = (ob2[0] + p2in[0, 1].astype(F32) + p2in[1, 1].astype(F32)).astype(BF16)
    x_in = send(M_X, xs, xr, sib)
    in1.append(send(M_P1S + 1, p1.at[1, 0], p1in.at[0, 1], sib))
    ob1[0] = partial1(0, 0)
    ob1[1] = partial1(1, 0)
    outs = []

    def put(src, ref, col, i):
        cp = pltpu.make_async_copy(src, ref.at[:, pl.ds(pl.multiple_of(col, 256), 256)], os_.at[i])
        cp.start()
        outs.append(cp)

    for cp in in20:
        cp.wait_recv()
    ob2[1] = ob2[1] + p2in[0, 0].astype(F32) + p2in[1, 0].astype(F32)
    put(ob2.at[1], out2, lo, 0)
    for cp in in1:
        cp.wait_recv()
    for e in range(2):
        ob1[e] = ob1[e] + p1in[0, e].astype(F32) + p1in[1, e].astype(F32)
        put(ob1.at[e], out1, lo if e == 0 else hi, 1 + e)
    x_in.wait_recv()
    ob2[0] = xr[...].astype(F32)
    put(ob2.at[0], out2, hi, 3)
    for cp in outs:
        cp.wait()
    for cp in sends:
        cp.wait_send()

    def sent(i, part):
        make(i, part, part, core).wait_send()

    for s in range(8):
        sent(M_C + s, csend.at[s])
    for d in range(2):
        for t in range(1, 5):
            for u in range(2):
                if t > 1 and (t < 4 or u == d):
                    sent(M_ZG + zslot(d, t, u), g.at[0, 0, 0])
                if t < 4 or u == d:
                    sent(M_GD + 4 * t + 2 * d + u, g.at[0, 0, 0])


def write_kernel(a, b, out1, out2, sem):
    cps = []
    for n, (src, dst) in enumerate(((a, out1), (b, out2))):
        for q in range(4):
            rows = pl.ds(64 * q, 64)
            cps.append(pltpu.make_async_copy(src.at[rows], dst.at[rows], sem.at[4 * n + q]))
    for cp in cps:
        cp.start()
    for cp in cps:
        cp.wait()


def body(first, second):
    v = pltpu.VMEM
    out = jax.ShapeDtypeStruct((256, 512), F32)
    anywhere = pl.BlockSpec(memory_space=pl.ANY)
    parts = pl.pallas_call(
        kernel,
        out_shape=(out, out),
        in_specs=[anywhere, anywhere],
        out_specs=(anywhere, anywhere),
        scratch_shapes=[
            v((13, 256, 256), F32),
            v((13, 256, 256), BF16),
            v((8, 256, 256), BF16),
            v((2, 4, 256, 256), BF16),
            v((13, 4, 256), F32),
            v((2, 4, 4, 256), F32),
            v((4, 8, 4, 256), F32),
            v((8, 10, 4, 256), F32),
            v((7, 10, 4, 256), F32),
            v((9, 4, 256), F32),
            v((256, 256), F32),
            v((256, 256), F32),
            v((8, 512, 256), BF16),
            v((8, 256, 256), F32),
            v((8, 256, 256), BF16),
            v((8, 256, 256), BF16),
            v((16, 128, 256), BF16),
            v((16, 128, 256), BF16),
            v((2, 8, 2, 128, 256), BF16),
            v((4, 512, 256), F32),
            v((4, 512, 256), F32),
            v((4, 256, 128), F32),
            v((4, 8, 256), F32),
            v((4, 8, 256), F32),
            v((4, 1, 256), F32),
            v((2, 4, 256, 256), BF16),
            v((2, 2, 256, 256), BF16),
            v((2, 256, 256), BF16),
            v((4, 2, 256, 256), BF16),
            v((2, 2, 256, 256), BF16),
            v((2, 256, 256), BF16),
            v((256, 256), BF16),
            v((256, 256), BF16),
            v((2, 256, 256), F32),
            v((2, 256, 256), F32),
            pltpu.SemaphoreType.DMA((M_ALL,)),
            pltpu.SemaphoreType.DMA((M_ALL,)),
            pltpu.SemaphoreType.DMA((13,)),
            pltpu.SemaphoreType.DMA((4,)),
        ],
        compiler_params=pltpu.CompilerParams(
            collective_id=0, has_side_effects=True, vmem_limit_bytes=56 * 1024 * 1024
        ),
    )(first, second)
    return pl.pallas_call(
        write_kernel,
        out_shape=(out, out),
        in_specs=[anywhere, anywhere],
        out_specs=(anywhere, anywhere),
        scratch_shapes=[pltpu.SemaphoreType.DMA((8,))],
        compiler_params=pltpu.CompilerParams(vmem_limit_bytes=56 * 1024 * 1024),
    )(*parts)


def solution(mesh):
    return jax.shard_map(
        body,
        mesh=mesh,
        in_specs=(P("dp", None), P("dp", None)),
        out_specs=(P("dp", "replica"), P("dp", "replica")),
        check_vma=False,
    )
```

```python
import jax
import jax.numpy as jnp
from jax import lax
from jax.experimental import pallas as pl
from jax.experimental.pallas import tpu as pltpu
from jax.sharding import PartitionSpec as P

LAMBDA = 0.0051
EPS = 1e-05
MESH = pl.DeviceIdType.MESH
F32 = jnp.float32
BF16 = jnp.bfloat16
BATCH = 8192

OWN = (2, 3, 10, 11, 8, 9, 12, 13)
STAT_SIB = (2, 3, 4, 5)
STAT_NON = (2, 3, 6, 7)
KB = (2, 3, 6, 7)
AB = (0, 1, 4, 5)

M_Y = 0
M_ST1 = 12
M_ST2 = 17
M_C = 24
M_ZR = 32
M_ZG = 48
M_GD = 64
M_P1 = 84
M_P2O = 96
M_P2R = 100
M_P2L = 104
M_X = 108
M_ALL = 109

HIGH = lax.Precision.HIGHEST


def nt(a, b, precision=None):
    return lax.dot_general(
        a, b, (((1,), (1,)), ((), ())), preferred_element_type=F32, precision=precision
    )


def tn(a, b, precision=None):
    return lax.dot_general(
        a, b, (((0,), (0,)), ((), ())), preferred_element_type=F32, precision=precision
    )


def nn(a, b):
    return lax.dot_general(a, b, (((1,), (0,)), ((), ())), preferred_element_type=F32)


def ab(a):
    return a + 2 * lax.div(a, 2)


def kb(k):
    return k + 2 + 2 * lax.div(k, 2)


def kernel(
    first, second, out1, out2,
    raw, cen, oth, xt, stat, smsg, st1, st2m, st2, fin, scl, fix, nrm, cown, csend, crecv, zs, zr, g,
    acc1, acc2, rsq, csq, rowsq, colsq,
    p1, p1in, p1relay, p2, p2in, p2relay, xs, xr, ob1, ob2, ss, rs, ls, os_,
):
    dp = lax.axis_index("dp")
    rep = lax.axis_index("replica")
    c = lax.rem(dp, 2)
    ylo = lax.rem(lax.div(dp, 2), 2)
    z = lax.div(dp, 4)
    yhi = lax.div(rep, 4)
    x = lax.rem(rep, 4)

    def dev(x_, yhi_, ylo_, z_, c_):
        return (z_ * 4 + ylo_ * 2 + c_, yhi_ * 4 + x_)

    core = dev(x, yhi, ylo, z, 1 - c)
    sib = dev(x, yhi, 1 - ylo, z, c)
    sibc = dev(x, yhi, 1 - ylo, z, 1 - c)
    non = dev(x, 1 - yhi, 1 - ylo, z, c)
    nonc = dev(x, 1 - yhi, 1 - ylo, z, 1 - c)
    right = dev(lax.rem(x + 1, 4), yhi, ylo, z, c)
    left = dev(lax.rem(x + 3, 4), yhi, ylo, z, c)
    zdev = [dev(x, yhi, ylo, lax.rem(z + q, 8), c) for q in range(8)]
    zto = (zdev[1], zdev[7])

    def load(i, ref, col):
        return pltpu.make_async_copy(
            ref.at[:, pl.ds(pl.multiple_of(col, 256), 256)], raw.at[i], ls.at[i]
        )

    pieces = [lax.rem(x + k, 4) * 512 for k in range(4)]
    kz = lax.rem(z, 4)
    iz = lax.div(z, 4)
    seed = lax.rem(x + kz, 4) * 512
    base = yhi * 2048
    other = 2048 - base
    mine = x * 512
    lo = ylo * 256
    hi = 256 - lo
    loads = [
        load(0, second, base + seed + hi),
        load(1, second, other + seed + hi),
        load(2, first, base + mine),
        load(3, first, base + mine + 256),
        load(4, second, base + pieces[0] + hi),
        load(5, second, base + pieces[1] + hi),
        load(6, second, other + pieces[2] + hi),
        load(7, second, other + pieces[3] + hi),
        load(8, first, other + mine),
        load(9, first, other + mine + 256),
    ] + [load(10 + k, second, base + pieces[k] + lo) for k in range(4)]
    for cp in loads:
        cp.start()

    barrier = pltpu.get_barrier_semaphore()
    partners = [core, sib, sibc, non, nonc, right, left] + zdev[1:]
    for d in partners:
        pl.semaphore_signal(barrier, inc=1, device_id=d, device_id_type=MESH)

    def make(i, src, dst, to):
        return pltpu.make_async_remote_copy(
            src_ref=src, dst_ref=dst, send_sem=ss.at[i], recv_sem=rs.at[i], device_id=to, device_id_type=MESH
        )

    sends = []

    def send(i, src, dst, to):
        cp = make(i, src, dst, to)
        cp.start()
        sends.append(cp)
        return cp

    def local_stats(i, carry):
        pltpu.make_async_copy(first.at[:, pl.ds(0, 256)], raw.at[i], ls.at[i]).wait()
        v = raw[i]
        m = jnp.sum(v, 0, keepdims=True) * (1.0 / 256)
        dv = v - m
        r = dv.astype(BF16)
        cen[i] = r
        stat[i, 0:1, :] = m
        stat[i, 1:2, :] = jnp.sum(dv * dv, 0, keepdims=True)
        stat[i, 2:3, :] = jnp.sum(r.astype(F32), 0, keepdims=True)
        stat[i, 3:4, :] = jnp.zeros_like(m)
        return carry

    top, low = pl.ds(0, 128), pl.ds(128, 128)
    k0, k1, k2, k3 = [kb(lax.rem(kz + n, 4)) for n in range(4)]
    lax.fori_loop(0, 2, local_stats, 0)
    pl.semaphore_wait(barrier, len(partners))
    y_top = send(M_Y + 0, cen.at[0, top], oth.at[k0, top], sib)
    y_low = send(M_Y + 1, cen.at[1, low], oth.at[k0, low], non)
    lax.fori_loop(2, 4, local_stats, 0)
    x_in = []
    for n, e in enumerate((1 - iz, iz)):
        x_in.append(
            [
                send(M_Y + 2 + 2 * n, cen.at[2 + e], oth.at[e], sib),
                send(M_Y + 3 + 2 * n, cen.at[2 + e], oth.at[4 + e], non),
            ]
        )
    lax.fori_loop(4, 14, local_stats, 0)

    def comoment(i, j):
        return jnp.sum((raw[i] - stat[i, 0:1, :]) * (raw[j] - stat[j, 0:1, :]), 0, keepdims=True)

    for n in range(4):
        smsg[0, n] = stat[STAT_SIB[n]]
        smsg[1, n] = stat[STAT_NON[n]]
    for b in range(8):
        st1[0, b] = stat[OWN[b]]
    smsg[0, 1 - ylo, 3:4, :] = comoment(3 - ylo, 4)
    st1[0, ylo, 3:4, :] = comoment(2 + ylo, 10)
    st_in = [
        send(M_ST1 + 0, smsg.at[0], st1.at[2, pl.ds(0, 4)], sib),
        send(M_ST1 + 1, smsg.at[1], st1.at[2, pl.ds(4, 4)], non),
        send(M_ST1 + 2, smsg.at[0], st1.at[3, pl.ds(0, 4)], sibc),
        send(M_ST1 + 3, smsg.at[1], st1.at[3, pl.ds(4, 4)], nonc),
        send(M_ST1 + 4, st1.at[0], st1.at[1], core),
    ]
    y_top.wait_recv()
    t1 = send(M_Y + 6, oth.at[k0, top], oth.at[k1, top], left)
    t3 = send(M_Y + 7, oth.at[k0, top], oth.at[k3, top], right)
    y_low.wait_recv()
    l1 = send(M_Y + 8, oth.at[k0, low], oth.at[k1, low], left)
    l3 = send(M_Y + 9, oth.at[k0, low], oth.at[k3, low], right)
    for a in range(4):
        xt[0, a] = cen[OWN[AB[a]]].T
    for cp in st_in:
        cp.wait_recv()

    def merge(rows_of, slots, count):
        devs = []
        res = []
        for b in range(8):
            rows = [rows_of(s, b) for s in range(slots)]
            total = sum(rows[1:], rows[0])
            m = total[0:1] * (1.0 / slots)
            dv = [r[0:1] - m for r in rows]
            m2 = total[1:2] + count * sum([d * d for d in dv[1:]], dv[0] * dv[0])
            devs.append(dv)
            res.append([m, m2, total[2:3], total[3:4]])
        for b in range(2):
            cross = sum([p * q for p, q in zip(devs[b][1:], devs[2][1:])], devs[b][0] * devs[2][0])
            res[b][3] = res[b][3] + count * cross
        return res

    for b, r in enumerate(merge(lambda s, b: st1[s, b], 4, 256.0)):
        for n in range(4):
            st2m[0, b, n : n + 1, :] = r[n]
    for q in range(8):
        zq = lax.rem(z + q, 8)
        fa = ab(2 * c + lax.div(zq, 4))
        fk = kb(lax.rem(zq, 4))
        if q:
            for b in range(8):
                st2m[q, b] = st2m[0, b]
        for s in range(4):
            st2m[q, 8, s : s + 1, :] = st1[s, fa, 0:1, :]
            st2m[q, 9, s : s + 1, :] = st1[s, fk, 0:1, :]
    st2_in = [send(M_ST2 + q - 1, st2m.at[q], st2.at[q - 1], zdev[q]) for q in range(1, 8)]

    for n in range(4):
        acc1[n] = jnp.zeros((512, 256), F32)
        acc2[n] = jnp.zeros((512, 256), F32)
    rsq[...] = jnp.zeros_like(rsq)
    csq[...] = jnp.zeros_like(csq)
    t1.wait_recv()
    yk2 = [send(M_Y + 10, oth.at[k1, top], oth.at[k2, top], left)]
    t3.wait_recv()
    l3.wait_recv()
    yk2.append(send(M_Y + 11, oth.at[k3, low], oth.at[k2, low], right))

    def x_ready(n):
        e = (1 - iz, iz)[n]
        for j in range(2):
            x_in[n][j].wait_recv()
            xt[1, 2 * j + e] = oth[4 * j + e].T

    def corr(s, carry):
        r = jnp.where(lax.rem(s, 2) == 1, 4 - lax.div(s + 1, 2), 4 + lax.div(s, 2))
        d = lax.rem(z + r, 8)
        i = lax.div(d, 4)
        k = lax.rem(d, 4)
        y0 = cen[10 + k]
        y1 = oth[kb(k)]
        a = 2 * (1 - c) + i
        csend[s] = (nn(xt[0, a], y0) + nn(xt[1, a], y1)).astype(BF16)
        make(M_C + s, csend.at[s], crecv.at[s], core).start()
        a = 2 * c + i
        cown[s] = nn(xt[0, a], y0) + nn(xt[1, a], y1)
        return carry

    def c_recv(s):
        make(M_C + s, csend.at[s], crecv.at[s], core).wait_recv()

    def zslot(d, t, u):
        return d * 8 + (t - 1) * 2 + u

    z_in = {}

    def chain(t, far):
        dist = 5 - t
        slot = (7 - 2 * dist, 8 - 2 * dist) if dist < 4 else (0, 0)
        if (t, far) in ((1, True), (2, False), (3, False), (4, False)):
            c_recv(slot[0])
            if t > 1:
                c_recv(slot[1])
        for d in range(2):
            u = d if far else 1 - d
            n = slot[d]
            rows = slice(128 * u, 128 * u + 128)
            v = cown[n, rows] + crecv[n, rows].astype(F32)
            if (d, t - 1, u) in z_in:
                z_in[(d, t - 1, u)].wait_recv()
                v = v + zr[zslot(d, t - 1, u)].astype(F32)
            i = zslot(d, t, u)
            zs[i] = v.astype(BF16)
            z_in[(d, t, u)] = send(M_ZR + i, zs.at[i], zr.at[i], zto[d])

    x_ready(0)
    lax.fori_loop(0, 1, corr, 0)
    x_ready(1)
    l1.wait_recv()
    lax.fori_loop(1, 3, corr, 0)
    chain(1, True)
    chain(2, False)
    for cp in yk2:
        cp.wait_recv()
    lax.fori_loop(3, 5, corr, 0)
    chain(2, True)
    lax.fori_loop(5, 8, corr, 0)
    chain(3, False)

    for cp in st2_in:
        cp.wait_recv()
    whole = merge(lambda s, b: st2m[0, b] if s == 0 else st2[s - 1, b], 8, 1024.0)
    rstds = []
    for b, r in enumerate(whole):
        rstd = lax.rsqrt(r[1] * (1.0 / BATCH) + EPS)
        fin[b, 0:1, :] = r[0] + r[2] * (1.0 / BATCH)
        fin[b, 1:2, :] = rstd
        fin[b, 2:3, :] = r[0]
        fin[b, 3:4, :] = jnp.zeros_like(rstd)
        rstds.append(rstd)
    low_half = ylo == 0
    cii = jnp.where(low_half, whole[0][3] * rstds[0], whole[1][3] * rstds[1]) * rstds[2] * (1.0 / BATCH)
    fin[8, 0:1, :] = cii
    fin[8, 1:2, :] = (-2.0 * (1.0 - cii)).astype(BF16).astype(F32)

    def norm(b, carry):
        for src, slot, o in ((None, 0, 0), (oth, 2, 1)):
            shift = st1[slot, b, 0:1, :] - fin[b, 0:1, :]
            scale = fin[b, 1:2, :]
            for h in range(2):
                rows = slice(128 * h, 128 * h + 128)
                v = own_block(b, h) if o == 0 else oth[b, rows]
                nrm[b, o * 256 + 128 * h : o * 256 + 128 * h + 128, :] = (
                    (v.astype(F32) + shift) * scale
                ).astype(BF16)
        return carry

    def own_block(b, h):
        p = lax.div(b, 4)
        q = lax.rem(b, 4)
        idx = jnp.where(q < 2, 2 + q + 6 * p, 8 + q + 2 * p)
        return cen[idx, 128 * h : 128 * h + 128]

    chain(3, True)
    lax.fori_loop(0, 4, norm, 0)
    chain(4, False)
    lax.fori_loop(4, 8, norm, 0)

    fa = ab(2 * c + lax.div(z, 4))
    fk = kb(lax.rem(z, 4))
    pad = jnp.zeros((7, 256), F32)
    ra = jnp.concatenate([fin[fa, 1:2, :] * (2.0 * LAMBDA / BATCH), pad], 0)
    rk = jnp.concatenate([fin[fk, 1:2, :], pad], 0)
    rows_id = lax.broadcasted_iota(jnp.int32, (256, 256), 0)
    cols_id = lax.broadcasted_iota(jnp.int32, (256, 256), 1)
    off = rows_id + jnp.where((c == 0) & (z == 4 * ylo), 0, 512) != cols_id
    scl[...] = jnp.where(off, tn(ra, rk, HIGH), 0.0)
    mu_a = [(st2m[0, 8] if s == 0 else st2[s - 1, 8]) - fin[fa, 2:3, :] for s in range(8)]
    mu_k = [(st2m[0, 9] if s == 0 else st2[s - 1, 9]) - fin[fk, 2:3, :] for s in range(8)]
    fix[...] = scl[...] * tn(jnp.concatenate(mu_a, 0) * 256.0, jnp.concatenate(mu_k, 0), HIGH)
    chain(4, True)

    c_recv(7)
    for u in range(2):
        rows = slice(128 * u, 128 * u + 128)
        v = cown[7, rows] + crecv[7, rows].astype(F32)
        for d in (1 - u, u):
            z_in[(d, 4, u)].wait_recv()
            v = v + zr[zslot(d, 4, u)].astype(F32)
        g[c, z, u] = (v * scl[rows] + fix[rows]).astype(BF16)
        for d in (u, 1 - u):
            i = zslot(d, 1, u)
            send(M_ZG + i, g.at[c, z, u], g.at[c, z, u], zto[d])
        send(M_GD + u, g.at[c, z, u], g.at[c, z, u], core)

    def arrive(t, far, onward):
        for d in range(2):
            u = d if far else 1 - d
            i = d * 8 + (t - 1) * 2 + u
            source = lax.rem(z + (8 - t if d == 0 else t), 8)
            part = g.at[c, source, u]
            make(M_ZG + i, part, part, zto[d]).wait_recv()
            if onward is not None:
                start = make(M_ZG + i + 2, part, part, zto[d]).start
                if onward is True:
                    start()
                else:
                    pl.when(onward)(start)
            make(M_GD + 4 * t + 2 * d + u, part, part, core).start()

    def use(j, zs_):
        a = 2 * j + lax.div(zs_, 4)
        k = lax.rem(zs_, 4)
        ga = g[j, zs_].reshape(256, 256)
        acc1[a] += nt(nrm[kb(k)], ga)
        acc2[k] += nn(nrm[ab(a)], ga)
        v = ga.astype(F32)
        s = v * v
        rsq[a] += s[:, 0:128] + s[:, 128:256]
        csq[k] += jnp.sum(s.reshape(32, 8, 256), 0)

    def from_core(t, d, u):
        part = g.at[0, 0, 0]
        make(M_GD + 4 * t + 2 * d + u, part, part, core).wait_recv()

    def uses(t, mine_too):
        def one(n, inner):
            if not mine_too:
                for u in range(2):
                    from_core(t, n, u)
            use(c if mine_too else 1 - c, lax.rem(z + (8 - t) + n * 2 * t, 8))
            return inner

        lax.fori_loop(0, jnp.where(t == 0, 1, 2), one, 0)

    uses(0, True)

    def step(t, carry):
        arrive(t, True, True)
        uses(t - 1, False)
        arrive(t, False, t < 3)
        uses(t, True)
        return carry

    def partial1(a, o):
        b = ab(a)
        rows = slice(o * 256, o * 256 + 256)
        f = nrm[b, rows].astype(F32)
        v = acc1[a, rows] - f * rowsq[a, 0:1, :]
        gd = jnp.where(a == ylo, fin[8, 1:2, :], 0.0)
        v = v + (nrm[2, rows].astype(F32) - f * fin[8, 0:1, :]) * gd
        return v * fin[b, 1:2, :]

    def p1_start(ph, e):
        for a in (e, 2 + e):
            rowsq[a] = nt(jnp.ones((8, 128), F32), rsq[a], HIGH) * (0.5 / LAMBDA)
        m = M_P1 + 6 * ph
        p1[ph, 0] = partial1(2 + e, 0).astype(BF16)
        relay = [
            send(m, p1.at[ph, 0, top], p1relay.at[ph, top], sib),
            send(m + 1, p1.at[ph, 0, low], p1relay.at[ph, low], non),
        ]
        p1[ph, 1] = partial1(2 + e, 1).astype(BF16)
        a = send(m + 2, p1.at[ph, 1, low], p1in.at[ph, 1, low], non)
        p1[ph, 2] = partial1(e, 1).astype(BF16)
        b = send(m + 3, p1.at[ph, 2, top], p1in.at[ph, 0, top], sib)
        return relay, [a, b]

    def p1_add(ph, relay):
        m = M_P1 + 6 * ph
        relay[0].wait_recv()
        p1[ph, 1, top] = (p1[ph, 1, top].astype(F32) + p1relay[ph, top].astype(F32)).astype(BF16)
        a = send(m + 4, p1.at[ph, 1, top], p1in.at[ph, 1, top], non)
        relay[1].wait_recv()
        p1[ph, 2, low] = (p1[ph, 2, low].astype(F32) + p1relay[ph, low].astype(F32)).astype(BF16)
        return [a, send(m + 5, p1.at[ph, 2, low], p1in.at[ph, 0, low], sib)]

    lax.fori_loop(1, 4, step, 0)
    uses(3, False)
    relay1, in1 = p1_start(0, iz)
    arrive(4, True, None)

    def final_two(n, carry):
        use(lax.rem(c + n, 2), lax.rem(z + 4, 8))
        return carry

    lax.fori_loop(0, 1, final_two, 0)
    from_core(4, 0, 0)
    from_core(4, 1, 1)
    lax.fori_loop(1, 2, final_two, 0)

    for k in range(4):
        colsq[k] = jnp.sum(csq[k], 0, keepdims=True) * (0.5 / LAMBDA)

    def partial2(k, o):
        b = KB[k]
        rows = slice(o * 256, o * 256 + 256)
        s = nrm[b, rows].astype(F32)
        v = acc2[k, rows] - s * colsq[k]
        if k == 0:
            v = v + (nrm[ylo, rows].astype(F32) - s * fin[8, 0:1, :]) * fin[8, 1:2, :]
        return v * fin[b, 1:2, :]

    def p2_relay(o):
        p2[2, o] = partial2(2, o).astype(BF16)
        return [
            send(M_P2O + 2 * o, p2.at[2, o, top], p2relay.at[o, top], right),
            send(M_P2O + 2 * o + 1, p2.at[2, o, low], p2relay.at[o, low], left),
        ]

    def p2_send(o):
        p2[1, o] = partial2(1, o).astype(BF16)
        a = send(M_P2R + 2 * o, p2.at[1, o, low], p2in.at[0, o, low], right)
        p2[3, o] = partial2(3, o).astype(BF16)
        return [a, send(M_P2L + 2 * o, p2.at[3, o, top], p2in.at[1, o, top], left)]

    def p2_add(o, relay):
        relay[0].wait_recv()
        p2[1, o, top] = (p2[1, o, top].astype(F32) + p2relay[o, top].astype(F32)).astype(BF16)
        a = send(M_P2R + 2 * o + 1, p2.at[1, o, top], p2in.at[0, o, top], right)
        relay[1].wait_recv()
        p2[3, o, low] = (p2[3, o, low].astype(F32) + p2relay[o, low].astype(F32)).astype(BF16)
        return [a, send(M_P2L + 2 * o + 1, p2.at[3, o, low], p2in.at[1, o, low], left)]

    relay2 = p2_relay(1)
    in1 += p1_add(0, relay1)
    in2 = p2_send(1)
    relay1, more = p1_start(1, 1 - iz)
    in1 += more
    relay20 = p2_relay(0)
    in2 += p2_add(1, relay2)
    in20 = p2_send(0)
    ob2[0] = partial2(0, 1)
    ob2[1] = partial2(0, 0)
    in1 += p1_add(1, relay1)
    in20 += p2_add(0, relay20)
    for cp in in2:
        cp.wait_recv()
    xs[...] = (ob2[0] + p2in[0, 1].astype(F32) + p2in[1, 1].astype(F32)).astype(BF16)
    x_last = send(M_X, xs, xr, sib)
    ob1[0] = partial1(iz, 0)
    ob1[1] = partial1(1 - iz, 0)
    outs = []

    def put(src, ref, col, i):
        cp = pltpu.make_async_copy(src, ref.at[:, pl.ds(pl.multiple_of(col, 256), 256)], os_.at[i])
        cp.start()
        outs.append(cp)

    for cp in in20:
        cp.wait_recv()
    ob2[1] = ob2[1] + p2in[0, 0].astype(F32) + p2in[1, 0].astype(F32)
    put(ob2.at[1], out2, lo, 0)
    for cp in in1:
        cp.wait_recv()
    for ph, e in enumerate((iz, 1 - iz)):
        ob1[ph] = ob1[ph] + p1in[ph, 0].astype(F32) + p1in[ph, 1].astype(F32)
        put(ob1.at[ph], out1, e * 256, 1 + ph)
    x_last.wait_recv()
    ob2[0] = xr[...].astype(F32)
    put(ob2.at[0], out2, hi, 3)
    for cp in outs:
        cp.wait()
    for cp in sends:
        cp.wait_send()

    def sent(i, part):
        make(i, part, part, core).wait_send()

    for s in range(8):
        sent(M_C + s, csend.at[s])
    for d in range(2):
        for t in range(1, 5):
            for u in range(2):
                if t > 1 and (t < 4 or u == d):
                    sent(M_ZG + zslot(d, t, u), g.at[0, 0, 0])
                if t < 4 or u == d:
                    sent(M_GD + 4 * t + 2 * d + u, g.at[0, 0, 0])


def write_kernel(a, b, out1, out2, held, sem_in, sem_out):
    cps = []
    for n, (src, dst) in enumerate(((a, out1), (b, out2))):
        for q in range(2):
            i = 2 * n + q
            rows = pl.ds(128 * q, 128)
            come = pltpu.make_async_copy(src.at[rows], held.at[i], sem_in.at[i])
            come.start()
            cps.append((come, pltpu.make_async_copy(held.at[i], dst.at[rows], sem_out.at[i])))
    for come, go in cps:
        come.wait()
        go.start()
    for come, go in cps:
        go.wait()


def body(first, second):
    v = pltpu.VMEM
    out = jax.ShapeDtypeStruct((256, 512), F32)
    anywhere = pl.BlockSpec(memory_space=pl.ANY)
    parts = pl.pallas_call(
        kernel,
        out_shape=(out, out),
        in_specs=[anywhere, anywhere],
        out_specs=(anywhere, anywhere),
        scratch_shapes=[
            v((14, 256, 256), F32),
            v((14, 256, 256), BF16),
            v((8, 256, 256), BF16),
            v((2, 4, 256, 256), BF16),
            v((14, 4, 256), F32),
            v((2, 4, 4, 256), F32),
            v((4, 8, 4, 256), F32),
            v((8, 10, 4, 256), F32),
            v((7, 10, 4, 256), F32),
            v((9, 4, 256), F32),
            v((256, 256), F32),
            v((256, 256), F32),
            v((8, 512, 256), BF16),
            v((8, 256, 256), F32),
            v((8, 256, 256), BF16),
            v((8, 256, 256), BF16),
            v((16, 128, 256), BF16),
            v((16, 128, 256), BF16),
            v((2, 8, 2, 128, 256), BF16),
            v((4, 512, 256), F32),
            v((4, 512, 256), F32),
            v((4, 256, 128), F32),
            v((4, 8, 256), F32),
            v((4, 8, 256), F32),
            v((4, 1, 256), F32),
            v((2, 3, 256, 256), BF16),
            v((2, 2, 256, 256), BF16),
            v((2, 256, 256), BF16),
            v((4, 2, 256, 256), BF16),
            v((2, 2, 256, 256), BF16),
            v((2, 256, 256), BF16),
            v((256, 256), BF16),
            v((256, 256), BF16),
            v((2, 256, 256), F32),
            v((2, 256, 256), F32),
            pltpu.SemaphoreType.DMA((M_ALL,)),
            pltpu.SemaphoreType.DMA((M_ALL,)),
            pltpu.SemaphoreType.DMA((14,)),
            pltpu.SemaphoreType.DMA((4,)),
        ],
        compiler_params=pltpu.CompilerParams(
            collective_id=0, has_side_effects=True, vmem_limit_bytes=56 * 1024 * 1024
        ),
    )(first, second)
    return pl.pallas_call(
        write_kernel,
        out_shape=(out, out),
        in_specs=[anywhere, anywhere],
        out_specs=(anywhere, anywhere),
        scratch_shapes=[v((4, 128, 512), F32), pltpu.SemaphoreType.DMA((4,)), pltpu.SemaphoreType.DMA((4,))],
        compiler_params=pltpu.CompilerParams(vmem_limit_bytes=56 * 1024 * 1024),
    )(*parts)


def solution(mesh):
    return jax.shard_map(
        body,
        mesh=mesh,
        in_specs=(P("dp", None), P("dp", None)),
        out_specs=(P("dp", "replica"), P("dp", "replica")),
        check_vma=False,
    )
```

```python
import jax
import jax.numpy as jnp
from jax import lax
from jax.experimental import pallas as pl
from jax.experimental.pallas import tpu as pltpu
from jax.sharding import PartitionSpec as P

LAMBDA = 0.0051
EPS = 1e-05
MESH = pl.DeviceIdType.MESH
F32 = jnp.float32
BF16 = jnp.bfloat16
BATCH = 8192

OWN = (2, 3, 10, 11, 8, 9, 12, 13)
STAT_SIB = (2, 3, 4, 5)
STAT_NON = (2, 3, 6, 7)
KB = (2, 3, 6, 7)
AB = (0, 1, 4, 5)

M_Y = 0
M_ST1 = 12
M_ST2 = 17
M_ST3 = 24
M_C = 31
M_ZR = 39
M_ZG = 71
M_GD = 103
M_P1 = 123
M_P2O = 135
M_P2R = 139
M_P2L = 143
M_X = 147
M_ALL = 148

HIGH = lax.Precision.HIGHEST


def nt(a, b, precision=None):
    return lax.dot_general(
        a, b, (((1,), (1,)), ((), ())), preferred_element_type=F32, precision=precision
    )


def tn(a, b, precision=None):
    return lax.dot_general(
        a, b, (((0,), (0,)), ((), ())), preferred_element_type=F32, precision=precision
    )


def nn(a, b):
    return lax.dot_general(a, b, (((1,), (0,)), ((), ())), preferred_element_type=F32)


def ab(a):
    return a + 2 * lax.div(a, 2)


def kb(k):
    return k + 2 + 2 * lax.div(k, 2)


def kernel(
    first, second, out1, out2,
    raw, cen, oth, xt, stat, smsg, st1, pst, st2m, st2, fin, dg, scl, fix, nrm, cown, csend, crecv, zs, zr, g,
    acc1, acc2, rsq, csq, rowsq, colsq,
    p1, p1in, p1relay, p2, p2in, p2relay, xs, xr, ob1, ob2, ss, rs, ls, os_,
):
    dp = lax.axis_index("dp")
    rep = lax.axis_index("replica")
    c = lax.rem(dp, 2)
    ylo = lax.rem(lax.div(dp, 2), 2)
    z = lax.div(dp, 4)
    yhi = lax.div(rep, 4)
    x = lax.rem(rep, 4)

    def dev(x_, yhi_, ylo_, z_, c_):
        return (z_ * 4 + ylo_ * 2 + c_, yhi_ * 4 + x_)

    core = dev(x, yhi, ylo, z, 1 - c)
    sib = dev(x, yhi, 1 - ylo, z, c)
    sibc = dev(x, yhi, 1 - ylo, z, 1 - c)
    non = dev(x, 1 - yhi, 1 - ylo, z, c)
    nonc = dev(x, 1 - yhi, 1 - ylo, z, 1 - c)
    right = dev(lax.rem(x + 1, 4), yhi, ylo, z, c)
    left = dev(lax.rem(x + 3, 4), yhi, ylo, z, c)
    zdev = [dev(x, yhi, ylo, lax.rem(z + q, 8), c) for q in range(8)]
    zto = (zdev[1], zdev[7])

    def load(i, ref, col):
        return pltpu.make_async_copy(
            ref.at[:, pl.ds(pl.multiple_of(col, 256), 256)], raw.at[i], ls.at[i]
        )

    pieces = [lax.rem(x + k, 4) * 512 for k in range(4)]
    kz = lax.rem(z, 4)
    iz = lax.div(z, 4)
    seed = lax.rem(x + kz, 4) * 512
    base = yhi * 2048
    other = 2048 - base
    mine = x * 512
    lo = ylo * 256
    hi = 256 - lo
    loads = [
        load(0, second, base + seed + hi),
        load(1, second, other + seed + hi),
        load(2, first, base + mine),
        load(3, first, base + mine + 256),
        load(4, second, base + pieces[0] + hi),
        load(5, second, base + pieces[1] + hi),
        load(6, second, other + pieces[2] + hi),
        load(7, second, other + pieces[3] + hi),
        load(8, first, other + mine),
        load(9, first, other + mine + 256),
    ] + [load(10 + k, second, base + pieces[k] + lo) for k in range(4)]
    for cp in loads:
        cp.start()

    barrier = pltpu.get_barrier_semaphore()
    partners = [core, sib, sibc, non, nonc, right, left] + zdev[1:]
    for d in partners:
        pl.semaphore_signal(barrier, inc=1, device_id=d, device_id_type=MESH)

    def make(i, src, dst, to):
        return pltpu.make_async_remote_copy(
            src_ref=src, dst_ref=dst, send_sem=ss.at[i], recv_sem=rs.at[i], device_id=to, device_id_type=MESH
        )

    sends = []

    def send(i, src, dst, to):
        cp = make(i, src, dst, to)
        cp.start()
        sends.append(cp)
        return cp

    def local_stats(i, carry):
        pltpu.make_async_copy(first.at[:, pl.ds(0, 256)], raw.at[i], ls.at[i]).wait()
        v = raw[i]
        m = jnp.sum(v, 0, keepdims=True) * (1.0 / 256)
        dv = v - m
        r = dv.astype(BF16)
        cen[i] = r
        stat[i, 0:1, :] = m
        stat[i, 1:2, :] = jnp.sum(dv * dv, 0, keepdims=True)
        stat[i, 2:3, :] = jnp.sum(r.astype(F32), 0, keepdims=True)
        stat[i, 3:4, :] = jnp.zeros_like(m)
        return carry

    top, low = pl.ds(0, 128), pl.ds(128, 128)
    k0, k1, k2, k3 = [kb(lax.rem(kz + n, 4)) for n in range(4)]
    lax.fori_loop(0, 2, local_stats, 0)
    pl.semaphore_wait(barrier, len(partners))
    y_top = send(M_Y + 0, cen.at[0, top], oth.at[k0, top], sib)
    y_low = send(M_Y + 1, cen.at[1, low], oth.at[k0, low], non)
    x_in = []
    for n, e in enumerate((1 - iz, iz)):
        lax.fori_loop(2 + e, 3 + e, local_stats, 0)
        xt[0, e] = cen[2 + e].T
        x_in.append(
            [
                send(M_Y + 2 + 2 * n, xt.at[0, e], xt.at[1, e], sib),
                send(M_Y + 3 + 2 * n, xt.at[0, e], xt.at[1, 2 + e], non),
            ]
        )
    lax.fori_loop(4, 14, local_stats, 0)

    def comoment(i, j):
        return jnp.sum((raw[i] - stat[i, 0:1, :]) * (raw[j] - stat[j, 0:1, :]), 0, keepdims=True)

    for n in range(4):
        smsg[0, n] = stat[STAT_SIB[n]]
        smsg[1, n] = stat[STAT_NON[n]]
    for b in range(8):
        st1[0, b] = stat[OWN[b]]
    smsg[0, 1 - ylo, 3:4, :] = comoment(3 - ylo, 4)
    st1[0, ylo, 3:4, :] = comoment(2 + ylo, 10)
    st_in = [
        send(M_ST1 + 0, smsg.at[0], st1.at[2, pl.ds(0, 4)], sib),
        send(M_ST1 + 1, smsg.at[1], st1.at[2, pl.ds(4, 4)], non),
        send(M_ST1 + 2, smsg.at[0], st1.at[3, pl.ds(0, 4)], sibc),
        send(M_ST1 + 3, smsg.at[1], st1.at[3, pl.ds(4, 4)], nonc),
        send(M_ST1 + 4, st1.at[0], st1.at[1], core),
    ]
    y_top.wait_recv()
    t1 = send(M_Y + 6, oth.at[k0, top], oth.at[k1, top], left)
    t3 = send(M_Y + 7, oth.at[k0, top], oth.at[k3, top], right)
    y_low.wait_recv()
    l1 = send(M_Y + 8, oth.at[k0, low], oth.at[k1, low], left)
    l3 = send(M_Y + 9, oth.at[k0, low], oth.at[k3, low], right)
    for a in range(2, 4):
        xt[0, a] = cen[OWN[AB[a]]].T
    for cp in st_in:
        cp.wait_recv()

    def merge(rows, count):
        total = sum(rows[1:], rows[0])
        m = total[0:1] * (1.0 / len(rows))
        dv = [r[0:1] - m for r in rows]
        m2 = total[1:2] + count * sum([d * d for d in dv[1:]], dv[0] * dv[0])
        return m, m2, total[2:3], total[3:4], dv

    def cross(p, q):
        return sum([a * b for a, b in zip(p[1:], q[1:])], p[0] * q[0])

    merged = [merge([st1[s, b] for s in range(4)], 256.0) for b in range(8)]
    for b, (m, m2, r, co, dv) in enumerate(merged):
        if b < 2:
            co = co + 256.0 * cross(dv, merged[2][4])
        for n, row in enumerate((m, m2, r, co)):
            pst[b, n : n + 1, :] = row
    st2_in = []
    for q in range(8):
        zq = lax.rem(z + q, 8)
        fa = ab(2 * c + lax.div(zq, 4))
        fk = kb(lax.rem(zq, 4))
        st2m[q, 0] = pst[zq]
        st2m[q, 3] = pst[2]
        for s in range(4):
            st2m[q, 1, s : s + 1, :] = st1[s, fa, 0:1, :]
            st2m[q, 2, s : s + 1, :] = st1[s, fk, 0:1, :]
        if q:
            st2_in.append(send(M_ST2 + q - 1, st2m.at[q], st2.at[q - 1], zdev[q]))

    t1.wait_recv()
    yk2 = [send(M_Y + 10, oth.at[k1, top], oth.at[k2, top], left)]
    t3.wait_recv()
    l3.wait_recv()
    yk2.append(send(M_Y + 11, oth.at[k3, low], oth.at[k2, low], right))

    def x_ready(n):
        for j in range(2):
            x_in[n][j].wait_recv()

    def corr(s, carry):
        r = jnp.where(lax.rem(s, 2) == 1, 4 - lax.div(s + 1, 2), 4 + lax.div(s, 2))
        d = lax.rem(z + r, 8)
        i = lax.div(d, 4)
        k = lax.rem(d, 4)
        y0 = cen[10 + k]
        y1 = oth[kb(k)]
        a = 2 * (1 - c) + i
        csend[s] = (nn(xt[0, a], y0) + nn(xt[1, a], y1)).astype(BF16)
        make(M_C + s, csend.at[s], crecv.at[s], core).start()
        a = 2 * c + i
        cown[s] = nn(xt[0, a], y0) + nn(xt[1, a], y1)
        return carry

    def c_recv(s):
        make(M_C + s, csend.at[s], crecv.at[s], core).wait_recv()

    def zslot(d, t, u):
        return d * 16 + (t - 1) * 4 + u * 2

    z_in = {}

    def chain(t, far):
        dist = 5 - t
        slot = (7 - 2 * dist, 8 - 2 * dist) if dist < 4 else (0, 0)
        if (t, far) in ((1, True), (2, False), (3, False), (4, False)):
            c_recv(slot[0])
            if t > 1:
                c_recv(slot[1])
        for s in range(2):
            for d in range(2):
                u = d if far else 1 - d
                n = slot[d]
                rows = slice(128 * u + 64 * s, 128 * u + 64 * s + 64)
                v = cown[n, rows] + crecv[n, rows].astype(F32)
                if (d, t - 1, u, s) in z_in:
                    z_in[(d, t - 1, u, s)].wait_recv()
                    v = v + zr[zslot(d, t - 1, u) + s].astype(F32)
                i = zslot(d, t, u) + s
                zs[i] = v.astype(BF16)
                z_in[(d, t, u, s)] = send(M_ZR + i, zs.at[i], zr.at[i], zto[d])

    x_ready(0)
    lax.fori_loop(0, 1, corr, 0)

    def zero(n, carry):
        acc1[n] = jnp.zeros((512, 256), F32)
        acc2[n] = jnp.zeros((512, 256), F32)
        return carry

    lax.fori_loop(0, 4, zero, 0)
    rsq[...] = jnp.zeros_like(rsq)
    csq[...] = jnp.zeros_like(csq)
    x_ready(1)
    chain(1, True)
    l1.wait_recv()
    lax.fori_loop(1, 3, corr, 0)
    for a in range(4):
        oth[AB[a]] = xt[1, a].T
    chain(2, False)
    for cp in yk2:
        cp.wait_recv()
    lax.fori_loop(3, 5, corr, 0)
    chain(2, True)
    lax.fori_loop(5, 8, corr, 0)
    chain(3, False)

    for cp in st2_in:
        cp.wait_recv()
    st2m_all = [st2m[0, 0]] + [st2[s, 0] for s in range(7)]
    k0_means = [st2m[0, 3]] + [st2[s, 3] for s in range(7)]
    m, m2, r, co, dv = merge(st2m_all, 1024.0)
    k0_dv = merge(k0_means, 1024.0)[4]
    fin[z, 0:1, :] = m + r * (1.0 / BATCH)
    fin[z, 1:2, :] = lax.rsqrt(m2 * (1.0 / BATCH) + EPS)
    fin[z, 2:3, :] = m
    fin[z, 3:4, :] = co + 1024.0 * cross(dv, k0_dv)
    fin_in = [send(M_ST3 + q - 1, fin.at[z], fin.at[z], zdev[q]) for q in range(1, 8)]

    def norm(b, carry):
        for src, slot, o in ((None, 0, 0), (oth, 2, 1)):
            shift = st1[slot, b, 0:1, :] - fin[b, 0:1, :]
            scale = fin[b, 1:2, :]
            for h in range(2):
                rows = slice(128 * h, 128 * h + 128)
                v = own_block(b, h) if o == 0 else oth[b, rows]
                nrm[b, o * 256 + 128 * h : o * 256 + 128 * h + 128, :] = (
                    (v.astype(F32) + shift) * scale
                ).astype(BF16)
        return carry

    def own_block(b, h):
        p = lax.div(b, 4)
        q = lax.rem(b, 4)
        idx = jnp.where(q < 2, 2 + q + 6 * p, 8 + q + 2 * p)
        return cen[idx, 128 * h : 128 * h + 128]

    chain(3, True)
    for cp in fin_in:
        cp.wait_recv()
    cii = fin[ylo, 3:4, :] * fin[ylo, 1:2, :] * fin[2, 1:2, :] * (1.0 / BATCH)
    dg[0:1, :] = cii
    dg[1:2, :] = (-2.0 * (1.0 - cii)).astype(BF16).astype(F32)
    lax.fori_loop(0, 4, norm, 0)
    chain(4, False)
    lax.fori_loop(4, 8, norm, 0)

    fa = ab(2 * c + lax.div(z, 4))
    fk = kb(lax.rem(z, 4))
    pad = jnp.zeros((7, 256), F32)
    ra = jnp.concatenate([fin[fa, 1:2, :] * (2.0 * LAMBDA / BATCH), pad], 0)
    rk = jnp.concatenate([fin[fk, 1:2, :], pad], 0)
    rows_id = lax.broadcasted_iota(jnp.int32, (256, 256), 0)
    cols_id = lax.broadcasted_iota(jnp.int32, (256, 256), 1)
    off = rows_id + jnp.where((c == 0) & (z == 4 * ylo), 0, 512) != cols_id
    scl[...] = jnp.where(off, tn(ra, rk, HIGH), 0.0)
    mu_a = [(st2m[0, 1] if s == 0 else st2[s - 1, 1]) - fin[fa, 2:3, :] for s in range(8)]
    mu_k = [(st2m[0, 2] if s == 0 else st2[s - 1, 2]) - fin[fk, 2:3, :] for s in range(8)]
    fix[...] = scl[...] * tn(jnp.concatenate(mu_a, 0) * 256.0, jnp.concatenate(mu_k, 0), HIGH)
    chain(4, True)

    c_recv(7)
    for s in range(2):
        for u in range(2):
            q = 2 * u + s
            rows = slice(64 * q, 64 * q + 64)
            v = cown[7, rows] + crecv[7, rows].astype(F32)
            for d in (1 - u, u):
                z_in[(d, 4, u, s)].wait_recv()
                v = v + zr[zslot(d, 4, u) + s].astype(F32)
            part = g.at[c, z, q]
            g[c, z, q] = (v * scl[rows] + fix[rows]).astype(BF16)
            for d in (u, 1 - u):
                send(M_ZG + zslot(d, 1, u) + s, part, part, zto[d])
    send(M_GD + 0, g.at[c, z, pl.ds(0, 2)], g.at[c, z, pl.ds(0, 2)], core)
    send(M_GD + 1, g.at[c, z, pl.ds(2, 2)], g.at[c, z, pl.ds(2, 2)], core)

    def arrive(t, far, onward):
        for s in range(2):
            for d in range(2):
                u = d if far else 1 - d
                i = d * 16 + (t - 1) * 4 + u * 2 + s
                source = lax.rem(z + (8 - t if d == 0 else t), 8)
                part = g.at[c, source, 2 * u + s]
                make(M_ZG + i, part, part, zto[d]).wait_recv()
                if onward is not None:
                    start = make(M_ZG + i + 4, part, part, zto[d]).start
                    if onward is True:
                        start()
                    else:
                        pl.when(onward)(start)
                if s == 1:
                    both = g.at[c, source, pl.ds(2 * u, 2)]
                    make(M_GD + 4 * t + 2 * d + u, both, both, core).start()

    def use(j, zs_):
        a = 2 * j + lax.div(zs_, 4)
        k = lax.rem(zs_, 4)
        ga = g[j, zs_].reshape(256, 256)
        acc1[a] += nt(nrm[kb(k)], ga)
        acc2[k] += nn(nrm[ab(a)], ga)
        v = ga.astype(F32)
        s = v * v
        rsq[a] += s[:, 0:128] + s[:, 128:256]
        csq[k] += jnp.sum(s.reshape(32, 8, 256), 0)

    def from_core(t, d, u):
        part = g.at[0, 0, pl.ds(0, 2)]
        make(M_GD + 4 * t + 2 * d + u, part, part, core).wait_recv()

    def uses(t, mine_too):
        def one(n, inner):
            if not mine_too:
                for u in range(2):
                    from_core(t, n, u)
            use(c if mine_too else 1 - c, lax.rem(z + (8 - t) + n * 2 * t, 8))
            return inner

        lax.fori_loop(0, jnp.where(t == 0, 1, 2), one, 0)

    uses(0, True)

    def step(t, carry):
        arrive(t, True, True)
        uses(t - 1, False)
        arrive(t, False, t < 3)
        uses(t, True)
        return carry

    def partial1(a, o):
        b = ab(a)
        rows = slice(o * 256, o * 256 + 256)
        f = nrm[b, rows].astype(F32)
        v = acc1[a, rows] - f * rowsq[a, 0:1, :]
        gd = jnp.where(a == ylo, dg[1:2, :], 0.0)
        v = v + (nrm[2, rows].astype(F32) - f * dg[0:1, :]) * gd
        return v * fin[b, 1:2, :]

    def p1_start(ph, e):
        for a in (e, 2 + e):
            rowsq[a] = nt(jnp.ones((8, 128), F32), rsq[a], HIGH) * (0.5 / LAMBDA)
        m = M_P1 + 6 * ph
        p1[ph, 0] = partial1(2 + e, 0).astype(BF16)
        relay = [
            send(m, p1.at[ph, 0, top], p1relay.at[ph, top], sib),
            send(m + 1, p1.at[ph, 0, low], p1relay.at[ph, low], non),
        ]
        p1[ph, 1] = partial1(2 + e, 1).astype(BF16)
        a = send(m + 2, p1.at[ph, 1, low], p1in.at[ph, 1, low], non)
        p1[ph, 2] = partial1(e, 1).astype(BF16)
        b = send(m + 3, p1.at[ph, 2, top], p1in.at[ph, 0, top], sib)
        return relay, [a, b]

    def p1_add(ph, relay):
        m = M_P1 + 6 * ph
        relay[0].wait_recv()
        p1[ph, 1, top] = (p1[ph, 1, top].astype(F32) + p1relay[ph, top].astype(F32)).astype(BF16)
        a = send(m + 4, p1.at[ph, 1, top], p1in.at[ph, 1, top], non)
        relay[1].wait_recv()
        p1[ph, 2, low] = (p1[ph, 2, low].astype(F32) + p1relay[ph, low].astype(F32)).astype(BF16)
        return [a, send(m + 5, p1.at[ph, 2, low], p1in.at[ph, 0, low], sib)]

    lax.fori_loop(1, 4, step, 0)
    uses(3, False)
    relay1, in1 = p1_start(0, iz)
    arrive(4, True, None)

    def final_two(n, carry):
        use(lax.rem(c + n, 2), lax.rem(z + 4, 8))
        return carry

    lax.fori_loop(0, 1, final_two, 0)
    from_core(4, 0, 0)
    from_core(4, 1, 1)
    lax.fori_loop(1, 2, final_two, 0)

    for k in range(4):
        colsq[k] = jnp.sum(csq[k], 0, keepdims=True) * (0.5 / LAMBDA)

    def partial2(k, o):
        b = KB[k]
        rows = slice(o * 256, o * 256 + 256)
        s = nrm[b, rows].astype(F32)
        v = acc2[k, rows] - s * colsq[k]
        if k == 0:
            v = v + (nrm[ylo, rows].astype(F32) - s * dg[0:1, :]) * dg[1:2, :]
        return v * fin[b, 1:2, :]

    def p2_relay(o):
        p2[2, o] = partial2(2, o).astype(BF16)
        return [
            send(M_P2O + 2 * o, p2.at[2, o, top], p2relay.at[o, top], right),
            send(M_P2O + 2 * o + 1, p2.at[2, o, low], p2relay.at[o, low], left),
        ]

    def p2_send(o):
        p2[1, o] = partial2(1, o).astype(BF16)
        a = send(M_P2R + 2 * o, p2.at[1, o, low], p2in.at[0, o, low], right)
        p2[3, o] = partial2(3, o).astype(BF16)
        return [a, send(M_P2L + 2 * o, p2.at[3, o, top], p2in.at[1, o, top], left)]

    def p2_add(o, relay):
        relay[0].wait_recv()
        p2[1, o, top] = (p2[1, o, top].astype(F32) + p2relay[o, top].astype(F32)).astype(BF16)
        a = send(M_P2R + 2 * o + 1, p2.at[1, o, top], p2in.at[0, o, top], right)
        relay[1].wait_recv()
        p2[3, o, low] = (p2[3, o, low].astype(F32) + p2relay[o, low].astype(F32)).astype(BF16)
        return [a, send(M_P2L + 2 * o + 1, p2.at[3, o, low], p2in.at[1, o, low], left)]

    def sent(i, part):
        make(i, part, part, core).wait_send()

    def finish_sends():
        for cp in done:
            cp.wait_send()
        for s in range(8):
            sent(M_C + s, csend.at[s])
        for d in range(2):
            for t in range(1, 5):
                for u in range(2):
                    if t > 1 and (t < 4 or u == d):
                        for s in range(2):
                            sent(M_ZG + zslot(d, t, u) + s, g.at[0, 0, 0])
                    if t < 4 or u == d:
                        sent(M_GD + 4 * t + 2 * d + u, g.at[0, 0, pl.ds(0, 2)])

    done = list(sends)
    relay2 = p2_relay(1)
    in1 += p1_add(0, relay1)
    in2 = p2_send(1)
    relay1, more = p1_start(1, 1 - iz)
    in1 += more
    relay20 = p2_relay(0)
    in2 += p2_add(1, relay2)
    in20 = p2_send(0)
    ob2[0] = partial2(0, 1)
    ob2[1] = partial2(0, 0)
    in1 += p1_add(1, relay1)
    in20 += p2_add(0, relay20)
    finish_sends()
    for cp in in2:
        cp.wait_recv()
    xs[...] = (ob2[0] + p2in[0, 1].astype(F32) + p2in[1, 1].astype(F32)).astype(BF16)
    x_last = send(M_X, xs, xr, sib)
    ob1[0] = partial1(iz, 0)
    ob1[1] = partial1(1 - iz, 0)
    outs = []

    def put(src, ref, col, i):
        cp = pltpu.make_async_copy(src, ref.at[:, pl.ds(pl.multiple_of(col, 256), 256)], os_.at[i])
        cp.start()
        outs.append(cp)

    for cp in in20:
        cp.wait_recv()
    ob2[1] = ob2[1] + p2in[0, 0].astype(F32) + p2in[1, 0].astype(F32)
    put(ob2.at[1], out2, lo, 0)
    for cp in in1:
        cp.wait_recv()
    for ph, e in enumerate((iz, 1 - iz)):
        ob1[ph] = ob1[ph] + p1in[ph, 0].astype(F32) + p1in[ph, 1].astype(F32)
        put(ob1.at[ph], out1, e * 256, 1 + ph)
    x_last.wait_recv()
    ob2[0] = xr[...].astype(F32)
    put(ob2.at[0], out2, hi, 3)
    for cp in outs:
        cp.wait()
    for cp in sends[len(done) :]:
        cp.wait_send()


def write_kernel(a, b, out1, out2, sem):
    cps = []
    for n, (src, dst) in enumerate(((a, out1), (b, out2))):
        for q in range(2):
            rows = pl.ds(128 * q, 128)
            cps.append(pltpu.make_async_copy(src.at[rows], dst.at[rows], sem.at[2 * n + q]))
    for cp in cps:
        cp.start()
    for cp in cps:
        cp.wait()


def body(first, second):
    v = pltpu.VMEM
    out = jax.ShapeDtypeStruct((256, 512), F32)
    anywhere = pl.BlockSpec(memory_space=pl.ANY)
    parts = pl.pallas_call(
        kernel,
        out_shape=(out, out),
        in_specs=[anywhere, anywhere],
        out_specs=(anywhere, anywhere),
        scratch_shapes=[
            v((14, 256, 256), F32),
            v((14, 256, 256), BF16),
            v((8, 256, 256), BF16),
            v((2, 4, 256, 256), BF16),
            v((14, 4, 256), F32),
            v((2, 4, 4, 256), F32),
            v((4, 8, 4, 256), F32),
            v((8, 4, 256), F32),
            v((8, 4, 4, 256), F32),
            v((7, 4, 4, 256), F32),
            v((8, 4, 256), F32),
            v((2, 256), F32),
            v((256, 256), F32),
            v((256, 256), F32),
            v((8, 512, 256), BF16),
            v((8, 256, 256), F32),
            v((8, 256, 256), BF16),
            v((8, 256, 256), BF16),
            v((32, 64, 256), BF16),
            v((32, 64, 256), BF16),
            v((2, 8, 4, 64, 256), BF16),
            v((4, 512, 256), F32),
            v((4, 512, 256), F32),
            v((4, 256, 128), F32),
            v((4, 8, 256), F32),
            v((4, 8, 256), F32),
            v((4, 1, 256), F32),
            v((2, 3, 256, 256), BF16),
            v((2, 2, 256, 256), BF16),
            v((2, 256, 256), BF16),
            v((4, 2, 256, 256), BF16),
            v((2, 2, 256, 256), BF16),
            v((2, 256, 256), BF16),
            v((256, 256), BF16),
            v((256, 256), BF16),
            v((2, 256, 256), F32),
            v((2, 256, 256), F32),
            pltpu.SemaphoreType.DMA((M_ALL,)),
            pltpu.SemaphoreType.DMA((M_ALL,)),
            pltpu.SemaphoreType.DMA((14,)),
            pltpu.SemaphoreType.DMA((4,)),
        ],
        compiler_params=pltpu.CompilerParams(
            collective_id=0, has_side_effects=True, vmem_limit_bytes=51 * 1024 * 1024
        ),
    )(first, second)
    return pl.pallas_call(
        write_kernel,
        out_shape=(out, out),
        in_specs=[pl.BlockSpec(memory_space=pltpu.VMEM)] * 2,
        out_specs=(anywhere, anywhere),
        scratch_shapes=[pltpu.SemaphoreType.DMA((4,))],
        compiler_params=pltpu.CompilerParams(vmem_limit_bytes=8 * 1024 * 1024),
    )(*parts)


def solution(mesh):
    return jax.shard_map(
        body,
        mesh=mesh,
        in_specs=(P("dp", None), P("dp", None)),
        out_specs=(P("dp", "replica"), P("dp", "replica")),
        check_vma=False,
    )
```

```python
import jax
import jax.numpy as jnp
from jax import lax
from jax.experimental import pallas as pl
from jax.experimental.pallas import tpu as pltpu
from jax.sharding import PartitionSpec as P

LAMBDA = 0.0051
EPS = 1e-05
MESH = pl.DeviceIdType.MESH
F32 = jnp.float32
BF16 = jnp.bfloat16
BATCH = 8192

OWN = (2, 3, 10, 11, 8, 9, 12, 13)
STAT_SIB = (2, 3, 4, 5)
STAT_NON = (2, 3, 6, 7)
KB = (2, 3, 6, 7)
AB = (0, 1, 4, 5)

M_Y = 0
M_ST1 = 12
M_ST2 = 17
M_ST3 = 24
M_C = 31
M_ZR = 39
M_ZG = 71
M_GD = 103
M_P1 = 123
M_P2O = 135
M_P2R = 139
M_P2L = 143
M_X = 147
M_ALL = 148

HIGH = lax.Precision.HIGHEST


def nt(a, b, precision=None):
    return lax.dot_general(
        a, b, (((1,), (1,)), ((), ())), preferred_element_type=F32, precision=precision
    )


def tn(a, b, precision=None):
    return lax.dot_general(
        a, b, (((0,), (0,)), ((), ())), preferred_element_type=F32, precision=precision
    )


def nn(a, b):
    return lax.dot_general(a, b, (((1,), (0,)), ((), ())), preferred_element_type=F32)


def ab(a):
    return a + 2 * lax.div(a, 2)


def kb(k):
    return k + 2 + 2 * lax.div(k, 2)


def kernel(
    first, second, out1, out2,
    raw, cen, oth, xt, stat, smsg, st1, pst, st2m, st2, fin, dg, scl, fix, nrm, cown, csend, crecv, zs, zr, g,
    acc1, acc2, rsq, csq, rowsq, colsq,
    p1, p1in, p1relay, p2, p2in, p2relay, xs, xr, ob1, ob2, ss, rs, ls, os_,
):
    dp = lax.axis_index("dp")
    rep = lax.axis_index("replica")
    c = lax.rem(dp, 2)
    ylo = lax.rem(lax.div(dp, 2), 2)
    z = lax.div(dp, 4)
    yhi = lax.div(rep, 4)
    x = lax.rem(rep, 4)

    def dev(x_, yhi_, ylo_, z_, c_):
        return (z_ * 4 + ylo_ * 2 + c_, yhi_ * 4 + x_)

    core = dev(x, yhi, ylo, z, 1 - c)
    sib = dev(x, yhi, 1 - ylo, z, c)
    sibc = dev(x, yhi, 1 - ylo, z, 1 - c)
    non = dev(x, 1 - yhi, 1 - ylo, z, c)
    nonc = dev(x, 1 - yhi, 1 - ylo, z, 1 - c)
    right = dev(lax.rem(x + 1, 4), yhi, ylo, z, c)
    left = dev(lax.rem(x + 3, 4), yhi, ylo, z, c)
    zdev = [dev(x, yhi, ylo, lax.rem(z + q, 8), c) for q in range(8)]
    zto = (zdev[1], zdev[7])
    zto2 = (zdev[2], zdev[6])

    def load(i, ref, col):
        return pltpu.make_async_copy(
            ref.at[:, pl.ds(pl.multiple_of(col, 256), 256)], raw.at[i], ls.at[i]
        )

    pieces = [lax.rem(x + k, 4) * 512 for k in range(4)]
    kz = lax.rem(z, 4)
    iz = lax.div(z, 4)
    seed = lax.rem(x + kz, 4) * 512
    base = yhi * 2048
    other = 2048 - base
    mine = x * 512
    lo = ylo * 256
    hi = 256 - lo
    loads = [
        load(0, second, base + seed + hi),
        load(1, second, other + seed + hi),
        load(2, first, base + mine),
        load(3, first, base + mine + 256),
        load(4, second, base + pieces[0] + hi),
        load(5, second, base + pieces[1] + hi),
        load(6, second, other + pieces[2] + hi),
        load(7, second, other + pieces[3] + hi),
        load(8, first, other + mine),
        load(9, first, other + mine + 256),
    ] + [load(10 + k, second, base + pieces[k] + lo) for k in range(4)]
    for cp in loads:
        cp.start()

    barrier = pltpu.get_barrier_semaphore()
    partners = [core, sib, sibc, non, nonc, right, left] + zdev[1:]
    for d in partners:
        pl.semaphore_signal(barrier, inc=1, device_id=d, device_id_type=MESH)

    def make(i, src, dst, to):
        return pltpu.make_async_remote_copy(
            src_ref=src, dst_ref=dst, send_sem=ss.at[i], recv_sem=rs.at[i], device_id=to, device_id_type=MESH
        )

    sends = []

    def send(i, src, dst, to):
        cp = make(i, src, dst, to)
        cp.start()
        sends.append(cp)
        return cp

    def local_stats(i, carry):
        pltpu.make_async_copy(first.at[:, pl.ds(0, 256)], raw.at[i], ls.at[i]).wait()
        v = raw[i]
        m = jnp.sum(v, 0, keepdims=True) * (1.0 / 256)
        dv = v - m
        r = dv.astype(BF16)
        cen[i] = r
        stat[i, 0:1, :] = m
        stat[i, 1:2, :] = jnp.sum(dv * dv, 0, keepdims=True)
        stat[i, 2:3, :] = jnp.sum(r.astype(F32), 0, keepdims=True)
        stat[i, 3:4, :] = jnp.zeros_like(m)
        return carry

    top, low = pl.ds(0, 128), pl.ds(128, 128)
    k0, k1, k2, k3 = [kb(lax.rem(kz + n, 4)) for n in range(4)]
    lax.fori_loop(0, 2, local_stats, 0)
    pl.semaphore_wait(barrier, len(partners))
    y_top = send(M_Y + 0, cen.at[0, top], oth.at[k0, top], sib)
    y_low = send(M_Y + 1, cen.at[1, low], oth.at[k0, low], non)
    x_in = []
    for n, e in enumerate((1 - iz, iz)):
        lax.fori_loop(2 + e, 3 + e, local_stats, 0)
        xt[0, e] = cen[2 + e].T
        x_in.append(
            [
                send(M_Y + 2 + 2 * n, xt.at[0, e], xt.at[1, e], sib),
                send(M_Y + 3 + 2 * n, xt.at[0, e], xt.at[1, 2 + e], non),
            ]
        )
    lax.fori_loop(4, 14, local_stats, 0)

    def comoment(i, j):
        return jnp.sum((raw[i] - stat[i, 0:1, :]) * (raw[j] - stat[j, 0:1, :]), 0, keepdims=True)

    for n in range(4):
        smsg[0, n] = stat[STAT_SIB[n]]
        smsg[1, n] = stat[STAT_NON[n]]
    for b in range(8):
        st1[0, b] = stat[OWN[b]]
    smsg[0, 1 - ylo, 3:4, :] = comoment(3 - ylo, 4)
    st1[0, ylo, 3:4, :] = comoment(2 + ylo, 10)
    st_in = [
        send(M_ST1 + 0, smsg.at[0], st1.at[2, pl.ds(0, 4)], sib),
        send(M_ST1 + 1, smsg.at[1], st1.at[2, pl.ds(4, 4)], non),
        send(M_ST1 + 2, smsg.at[0], st1.at[3, pl.ds(0, 4)], sibc),
        send(M_ST1 + 3, smsg.at[1], st1.at[3, pl.ds(4, 4)], nonc),
        send(M_ST1 + 4, st1.at[0], st1.at[1], core),
    ]
    y_top.wait_recv()
    t1 = send(M_Y + 6, oth.at[k0, top], oth.at[k1, top], left)
    t3 = send(M_Y + 7, oth.at[k0, top], oth.at[k3, top], right)
    y_low.wait_recv()
    l1 = send(M_Y + 8, oth.at[k0, low], oth.at[k1, low], left)
    l3 = send(M_Y + 9, oth.at[k0, low], oth.at[k3, low], right)
    for a in range(2, 4):
        xt[0, a] = cen[OWN[AB[a]]].T
    for cp in st_in:
        cp.wait_recv()

    def merge(rows, count):
        total = sum(rows[1:], rows[0])
        m = total[0:1] * (1.0 / len(rows))
        dv = [r[0:1] - m for r in rows]
        m2 = total[1:2] + count * sum([d * d for d in dv[1:]], dv[0] * dv[0])
        return m, m2, total[2:3], total[3:4], dv

    def cross(p, q):
        return sum([a * b for a, b in zip(p[1:], q[1:])], p[0] * q[0])

    merged = [merge([st1[s, b] for s in range(4)], 256.0) for b in range(8)]
    for b, (m, m2, r, co, dv) in enumerate(merged):
        if b < 2:
            co = co + 256.0 * cross(dv, merged[2][4])
        for n, row in enumerate((m, m2, r, co)):
            pst[b, n : n + 1, :] = row
    st2_in = []
    for q in range(8):
        zq = lax.rem(z + q, 8)
        fa = ab(2 * c + lax.div(zq, 4))
        fk = kb(lax.rem(zq, 4))
        st2m[q, 0] = pst[zq]
        st2m[q, 3] = pst[2]
        for s in range(4):
            st2m[q, 1, s : s + 1, :] = st1[s, fa, 0:1, :]
            st2m[q, 2, s : s + 1, :] = st1[s, fk, 0:1, :]
        if q:
            st2_in.append(send(M_ST2 + q - 1, st2m.at[q], st2.at[q - 1], zdev[q]))

    t1.wait_recv()
    yk2 = [send(M_Y + 10, oth.at[k1, top], oth.at[k2, top], left)]
    t3.wait_recv()
    l3.wait_recv()
    yk2.append(send(M_Y + 11, oth.at[k3, low], oth.at[k2, low], right))

    def x_ready(n):
        for j in range(2):
            x_in[n][j].wait_recv()

    def corr(s, carry):
        r = jnp.where(lax.rem(s, 2) == 1, 4 - lax.div(s + 1, 2), 4 + lax.div(s, 2))
        d = lax.rem(z + r, 8)
        i = lax.div(d, 4)
        k = lax.rem(d, 4)
        y0 = cen[10 + k]
        y1 = oth[kb(k)]
        a = 2 * (1 - c) + i
        csend[s] = (nn(xt[0, a], y0) + nn(xt[1, a], y1)).astype(BF16)
        make(M_C + s, csend.at[s], crecv.at[s], core).start()
        a = 2 * c + i
        cown[s] = nn(xt[0, a], y0) + nn(xt[1, a], y1)
        return carry

    def c_recv(s):
        make(M_C + s, csend.at[s], crecv.at[s], core).wait_recv()

    def zslot(d, t, u):
        return d * 16 + (t - 1) * 4 + u * 2

    z_in = {}

    def chain(t, far):
        dist = 5 - t
        slot = (7 - 2 * dist, 8 - 2 * dist) if dist < 4 else (0, 0)
        if (t, far) in ((1, True), (2, False), (3, False), (4, False)):
            c_recv(slot[0])
            if t > 1:
                c_recv(slot[1])
        for s in range(2):
            for d in range(2):
                u = d if far else 1 - d
                n = slot[d]
                rows = slice(128 * u + 64 * s, 128 * u + 64 * s + 64)
                v = cown[n, rows] + crecv[n, rows].astype(F32)
                for before in {2: (), 3: (1, 2), 4: (3,)}.get(t, ()) if far else (t - 1,):
                    if (d, before, u, s) in z_in:
                        z_in[(d, before, u, s)].wait_recv()
                        v = v + zr[zslot(d, before, u) + s].astype(F32)
                i = zslot(d, t, u) + s
                zs[i] = v.astype(BF16)
                to = zto2[d] if t == 1 else zto[d]
                z_in[(d, t, u, s)] = send(M_ZR + i, zs.at[i], zr.at[i], to)

    x_ready(0)
    lax.fori_loop(0, 1, corr, 0)

    def zero(n, carry):
        acc1[n] = jnp.zeros((512, 256), F32)
        acc2[n] = jnp.zeros((512, 256), F32)
        return carry

    lax.fori_loop(0, 4, zero, 0)
    rsq[...] = jnp.zeros_like(rsq)
    csq[...] = jnp.zeros_like(csq)
    x_ready(1)
    chain(1, True)
    l1.wait_recv()
    lax.fori_loop(1, 3, corr, 0)
    for a in range(4):
        oth[AB[a]] = xt[1, a].T
    chain(2, False)
    for cp in yk2:
        cp.wait_recv()
    lax.fori_loop(3, 5, corr, 0)
    chain(2, True)
    lax.fori_loop(5, 8, corr, 0)
    chain(3, False)

    for cp in st2_in:
        cp.wait_recv()
    st2m_all = [st2m[0, 0]] + [st2[s, 0] for s in range(7)]
    k0_means = [st2m[0, 3]] + [st2[s, 3] for s in range(7)]
    m, m2, r, co, dv = merge(st2m_all, 1024.0)
    k0_dv = merge(k0_means, 1024.0)[4]
    fin[z, 0:1, :] = m + r * (1.0 / BATCH)
    fin[z, 1:2, :] = lax.rsqrt(m2 * (1.0 / BATCH) + EPS)
    fin[z, 2:3, :] = m
    fin[z, 3:4, :] = co + 1024.0 * cross(dv, k0_dv)
    fin_in = [send(M_ST3 + q - 1, fin.at[z], fin.at[z], zdev[q]) for q in range(1, 8)]

    def norm(b, carry):
        for src, slot, o in ((None, 0, 0), (oth, 2, 1)):
            shift = st1[slot, b, 0:1, :] - fin[b, 0:1, :]
            scale = fin[b, 1:2, :]
            for h in range(2):
                rows = slice(128 * h, 128 * h + 128)
                v = own_block(b, h) if o == 0 else oth[b, rows]
                nrm[b, o * 256 + 128 * h : o * 256 + 128 * h + 128, :] = (
                    (v.astype(F32) + shift) * scale
                ).astype(BF16)
        return carry

    def own_block(b, h):
        p = lax.div(b, 4)
        q = lax.rem(b, 4)
        idx = jnp.where(q < 2, 2 + q + 6 * p, 8 + q + 2 * p)
        return cen[idx, 128 * h : 128 * h + 128]

    chain(3, True)
    for cp in fin_in:
        cp.wait_recv()
    cii = fin[ylo, 3:4, :] * fin[ylo, 1:2, :] * fin[2, 1:2, :] * (1.0 / BATCH)
    dg[0:1, :] = cii
    dg[1:2, :] = (-2.0 * (1.0 - cii)).astype(BF16).astype(F32)
    lax.fori_loop(0, 4, norm, 0)
    chain(4, False)
    lax.fori_loop(4, 8, norm, 0)

    fa = ab(2 * c + lax.div(z, 4))
    fk = kb(lax.rem(z, 4))
    pad = jnp.zeros((7, 256), F32)
    ra = jnp.concatenate([fin[fa, 1:2, :] * (2.0 * LAMBDA / BATCH), pad], 0)
    rk = jnp.concatenate([fin[fk, 1:2, :], pad], 0)
    rows_id = lax.broadcasted_iota(jnp.int32, (256, 256), 0)
    cols_id = lax.broadcasted_iota(jnp.int32, (256, 256), 1)
    off = rows_id + jnp.where((c == 0) & (z == 4 * ylo), 0, 512) != cols_id
    scl[...] = jnp.where(off, tn(ra, rk, HIGH), 0.0)
    mu_a = [(st2m[0, 1] if s == 0 else st2[s - 1, 1]) - fin[fa, 2:3, :] for s in range(8)]
    mu_k = [(st2m[0, 2] if s == 0 else st2[s - 1, 2]) - fin[fk, 2:3, :] for s in range(8)]
    fix[...] = scl[...] * tn(jnp.concatenate(mu_a, 0) * 256.0, jnp.concatenate(mu_k, 0), HIGH)
    chain(4, True)

    c_recv(7)
    for s in range(2):
        for u in range(2):
            q = 2 * u + s
            rows = slice(64 * q, 64 * q + 64)
            v = cown[7, rows] + crecv[7, rows].astype(F32)
            for d in (1 - u, u):
                z_in[(d, 4, u, s)].wait_recv()
                v = v + zr[zslot(d, 4, u) + s].astype(F32)
            part = g.at[c, z, q]
            g[c, z, q] = (v * scl[rows] + fix[rows]).astype(BF16)
            send(M_ZG + zslot(u, 1, u) + s, part, part, zto[u])
            send(M_ZG + zslot(u, 2, u) + s, part, part, zto2[u])
            send(M_ZG + zslot(1 - u, 1, u) + s, part, part, zto[1 - u])
    send(M_GD + 0, g.at[c, z, pl.ds(0, 2)], g.at[c, z, pl.ds(0, 2)], core)
    send(M_GD + 1, g.at[c, z, pl.ds(2, 2)], g.at[c, z, pl.ds(2, 2)], core)

    def arrive(t, far, onward):
        for s in range(2):
            for d in range(2):
                u = d if far else 1 - d
                i = d * 16 + (t - 1) * 4 + u * 2 + s
                source = lax.rem(z + (8 - t if d == 0 else t), 8)
                part = g.at[c, source, 2 * u + s]
                make(M_ZG + i, part, part, zto[d]).wait_recv()
                if onward is not None:
                    start = make(M_ZG + i + 4, part, part, zto[d]).start
                    if onward is True:
                        start()
                    else:
                        pl.when(onward)(start)
                if s == 1:
                    both = g.at[c, source, pl.ds(2 * u, 2)]
                    make(M_GD + 4 * t + 2 * d + u, both, both, core).start()

    def use(j, zs_):
        a = 2 * j + lax.div(zs_, 4)
        k = lax.rem(zs_, 4)
        ga = g[j, zs_].reshape(256, 256)
        acc1[a] += nt(nrm[kb(k)], ga)
        acc2[k] += nn(nrm[ab(a)], ga)
        v = ga.astype(F32)
        s = v * v
        rsq[a] += s[:, 0:128] + s[:, 128:256]
        csq[k] += jnp.sum(s.reshape(32, 8, 256), 0)

    def from_core(t, d, u):
        part = g.at[0, 0, pl.ds(0, 2)]
        make(M_GD + 4 * t + 2 * d + u, part, part, core).wait_recv()

    def uses(t, mine_too):
        def one(n, inner):
            if not mine_too:
                for u in range(2):
                    from_core(t, n, u)
            use(c if mine_too else 1 - c, lax.rem(z + (8 - t) + n * 2 * t, 8))
            return inner

        lax.fori_loop(0, jnp.where(t == 0, 1, 2), one, 0)

    uses(0, True)

    def step(t, carry):
        arrive(t, True, t > 1)
        uses(t - 1, False)
        arrive(t, False, t < 3)
        uses(t, True)
        return carry

    def partial1(a, o):
        b = ab(a)
        rows = slice(o * 256, o * 256 + 256)
        f = nrm[b, rows].astype(F32)
        v = acc1[a, rows] - f * rowsq[a, 0:1, :]
        gd = jnp.where(a == ylo, dg[1:2, :], 0.0)
        v = v + (nrm[2, rows].astype(F32) - f * dg[0:1, :]) * gd
        return v * fin[b, 1:2, :]

    def p1_start(ph, e):
        for a in (e, 2 + e):
            rowsq[a] = nt(jnp.ones((8, 128), F32), rsq[a], HIGH) * (0.5 / LAMBDA)
        m = M_P1 + 6 * ph
        p1[ph, 0] = partial1(2 + e, 0).astype(BF16)
        relay = [
            send(m, p1.at[ph, 0, top], p1relay.at[ph, top], sib),
            send(m + 1, p1.at[ph, 0, low], p1relay.at[ph, low], non),
        ]
        p1[ph, 1] = partial1(2 + e, 1).astype(BF16)
        a = send(m + 2, p1.at[ph, 1, low], p1in.at[ph, 1, low], non)
        p1[ph, 2] = partial1(e, 1).astype(BF16)
        b = send(m + 3, p1.at[ph, 2, top], p1in.at[ph, 0, top], sib)
        return relay, [a, b]

    def p1_add(ph, relay):
        m = M_P1 + 6 * ph
        relay[0].wait_recv()
        p1[ph, 1, top] = (p1[ph, 1, top].astype(F32) + p1relay[ph, top].astype(F32)).astype(BF16)
        a = send(m + 4, p1.at[ph, 1, top], p1in.at[ph, 1, top], non)
        relay[1].wait_recv()
        p1[ph, 2, low] = (p1[ph, 2, low].astype(F32) + p1relay[ph, low].astype(F32)).astype(BF16)
        return [a, send(m + 5, p1.at[ph, 2, low], p1in.at[ph, 0, low], sib)]

    lax.fori_loop(1, 4, step, 0)
    uses(3, False)
    relay1, in1 = p1_start(0, iz)
    arrive(4, True, None)

    def final_two(n, carry):
        use(lax.rem(c + n, 2), lax.rem(z + 4, 8))
        return carry

    lax.fori_loop(0, 1, final_two, 0)
    from_core(4, 0, 0)
    from_core(4, 1, 1)
    lax.fori_loop(1, 2, final_two, 0)

    for k in range(4):
        colsq[k] = jnp.sum(csq[k], 0, keepdims=True) * (0.5 / LAMBDA)

    def partial2(k, o):
        b = KB[k]
        rows = slice(o * 256, o * 256 + 256)
        s = nrm[b, rows].astype(F32)
        v = acc2[k, rows] - s * colsq[k]
        if k == 0:
            v = v + (nrm[ylo, rows].astype(F32) - s * dg[0:1, :]) * dg[1:2, :]
        return v * fin[b, 1:2, :]

    def p2_relay(o):
        p2[2, o] = partial2(2, o).astype(BF16)
        return [
            send(M_P2O + 2 * o, p2.at[2, o, top], p2relay.at[o, top], right),
            send(M_P2O + 2 * o + 1, p2.at[2, o, low], p2relay.at[o, low], left),
        ]

    def p2_send(o):
        p2[1, o] = partial2(1, o).astype(BF16)
        a = send(M_P2R + 2 * o, p2.at[1, o, low], p2in.at[0, o, low], right)
        p2[3, o] = partial2(3, o).astype(BF16)
        return [a, send(M_P2L + 2 * o, p2.at[3, o, top], p2in.at[1, o, top], left)]

    def p2_add(o, relay):
        relay[0].wait_recv()
        p2[1, o, top] = (p2[1, o, top].astype(F32) + p2relay[o, top].astype(F32)).astype(BF16)
        a = send(M_P2R + 2 * o + 1, p2.at[1, o, top], p2in.at[0, o, top], right)
        relay[1].wait_recv()
        p2[3, o, low] = (p2[3, o, low].astype(F32) + p2relay[o, low].astype(F32)).astype(BF16)
        return [a, send(M_P2L + 2 * o + 1, p2.at[3, o, low], p2in.at[1, o, low], left)]

    def sent(i, part):
        make(i, part, part, core).wait_send()

    def finish_sends():
        for cp in done:
            cp.wait_send()
        for s in range(8):
            sent(M_C + s, csend.at[s])
        for d in range(2):
            for t in range(1, 5):
                for u in range(2):
                    if t > 1 and (t < 4 or u == d) and not (t == 2 and u == d):
                        for s in range(2):
                            sent(M_ZG + zslot(d, t, u) + s, g.at[0, 0, 0])
                    if t < 4 or u == d:
                        sent(M_GD + 4 * t + 2 * d + u, g.at[0, 0, pl.ds(0, 2)])

    done = list(sends)
    relay2 = p2_relay(1)
    in1 += p1_add(0, relay1)
    in2 = p2_send(1)
    relay1, more = p1_start(1, 1 - iz)
    in1 += more
    relay20 = p2_relay(0)
    in2 += p2_add(1, relay2)
    in20 = p2_send(0)
    ob2[0] = partial2(0, 1)
    ob2[1] = partial2(0, 0)
    in1 += p1_add(1, relay1)
    in20 += p2_add(0, relay20)
    finish_sends()
    for cp in in2:
        cp.wait_recv()
    xs[...] = (ob2[0] + p2in[0, 1].astype(F32) + p2in[1, 1].astype(F32)).astype(BF16)
    x_last = send(M_X, xs, xr, sib)
    ob1[0] = partial1(iz, 0)
    ob1[1] = partial1(1 - iz, 0)
    outs = []

    def put(src, ref, col, i):
        cp = pltpu.make_async_copy(src, ref.at[:, pl.ds(pl.multiple_of(col, 256), 256)], os_.at[i])
        cp.start()
        outs.append(cp)

    for cp in in20:
        cp.wait_recv()
    ob2[1] = ob2[1] + p2in[0, 0].astype(F32) + p2in[1, 0].astype(F32)
    put(ob2.at[1], out2, lo, 0)
    for cp in in1:
        cp.wait_recv()
    for ph, e in enumerate((iz, 1 - iz)):
        ob1[ph] = ob1[ph] + p1in[ph, 0].astype(F32) + p1in[ph, 1].astype(F32)
        put(ob1.at[ph], out1, e * 256, 1 + ph)
    x_last.wait_recv()
    ob2[0] = xr[...].astype(F32)
    put(ob2.at[0], out2, hi, 3)
    for cp in outs:
        cp.wait()
    for cp in sends[len(done) :]:
        cp.wait_send()


def write_kernel(a, b, out1, out2, sem):
    cps = []
    for n, (src, dst) in enumerate(((a, out1), (b, out2))):
        for q in range(2):
            rows = pl.ds(128 * q, 128)
            cps.append(pltpu.make_async_copy(src.at[rows], dst.at[rows], sem.at[2 * n + q]))
    for cp in cps:
        cp.start()
    for cp in cps:
        cp.wait()


def body(first, second):
    v = pltpu.VMEM
    out = jax.ShapeDtypeStruct((256, 512), F32)
    anywhere = pl.BlockSpec(memory_space=pl.ANY)
    parts = pl.pallas_call(
        kernel,
        out_shape=(out, out),
        in_specs=[anywhere, anywhere],
        out_specs=(anywhere, anywhere),
        scratch_shapes=[
            v((14, 256, 256), F32),
            v((14, 256, 256), BF16),
            v((8, 256, 256), BF16),
            v((2, 4, 256, 256), BF16),
            v((14, 4, 256), F32),
            v((2, 4, 4, 256), F32),
            v((4, 8, 4, 256), F32),
            v((8, 4, 256), F32),
            v((8, 4, 4, 256), F32),
            v((7, 4, 4, 256), F32),
            v((8, 4, 256), F32),
            v((2, 256), F32),
            v((256, 256), F32),
            v((256, 256), F32),
            v((8, 512, 256), BF16),
            v((8, 256, 256), F32),
            v((8, 256, 256), BF16),
            v((8, 256, 256), BF16),
            v((32, 64, 256), BF16),
            v((32, 64, 256), BF16),
            v((2, 8, 4, 64, 256), BF16),
            v((4, 512, 256), F32),
            v((4, 512, 256), F32),
            v((4, 256, 128), F32),
            v((4, 8, 256), F32),
            v((4, 8, 256), F32),
            v((4, 1, 256), F32),
            v((2, 3, 256, 256), BF16),
            v((2, 2, 256, 256), BF16),
            v((2, 256, 256), BF16),
            v((4, 2, 256, 256), BF16),
            v((2, 2, 256, 256), BF16),
            v((2, 256, 256), BF16),
            v((256, 256), BF16),
            v((256, 256), BF16),
            v((2, 256, 256), F32),
            v((2, 256, 256), F32),
            pltpu.SemaphoreType.DMA((M_ALL,)),
            pltpu.SemaphoreType.DMA((M_ALL,)),
            pltpu.SemaphoreType.DMA((14,)),
            pltpu.SemaphoreType.DMA((4,)),
        ],
        compiler_params=pltpu.CompilerParams(
            collective_id=0, has_side_effects=True, vmem_limit_bytes=51 * 1024 * 1024
        ),
    )(first, second)
    return pl.pallas_call(
        write_kernel,
        out_shape=(out, out),
        in_specs=[pl.BlockSpec(memory_space=pltpu.VMEM)] * 2,
        out_specs=(anywhere, anywhere),
        scratch_shapes=[pltpu.SemaphoreType.DMA((4,))],
        compiler_params=pltpu.CompilerParams(vmem_limit_bytes=8 * 1024 * 1024),
    )(*parts)


def solution(mesh):
    return jax.shard_map(
        body,
        mesh=mesh,
        in_specs=(P("dp", None), P("dp", None)),
        out_specs=(P("dp", "replica"), P("dp", "replica")),
        check_vma=False,
    )
```

```python
import jax
import jax.numpy as jnp
from jax import lax
from jax.experimental import pallas as pl
from jax.experimental.pallas import tpu as pltpu
from jax.sharding import PartitionSpec as P

LAMBDA = 0.0051
EPS = 1e-05
MESH = pl.DeviceIdType.MESH
F32 = jnp.float32
BF16 = jnp.bfloat16
BATCH = 8192

OWN = (0, 1, 4, 5, 2, 3, 6, 7)
STAT_SIB = (0, 1, 8, 9)
STAT_NON = (0, 1, 14, 15)
KB = (2, 3, 6, 7)
AB = (0, 1, 4, 5)

M_Y = 0
M_ST1 = 12
M_ST2 = 17
M_ST3 = 24
M_C = 31
M_YP = 39
M_ZR = 55
M_ZG = 87
M_GD = 119
M_P1 = 139
M_P2O = 151
M_P2R = 155
M_P2L = 159
M_X = 163
M_ALL = 164

HIGH = lax.Precision.HIGHEST


def nt(a, b, precision=None):
    return lax.dot_general(
        a, b, (((1,), (1,)), ((), ())), preferred_element_type=F32, precision=precision
    )


def tn(a, b, precision=None):
    return lax.dot_general(
        a, b, (((0,), (0,)), ((), ())), preferred_element_type=F32, precision=precision
    )


def nn(a, b):
    return lax.dot_general(a, b, (((1,), (0,)), ((), ())), preferred_element_type=F32)


def ab(a):
    return a + 2 * lax.div(a, 2)


def kb(k):
    return k + 2 + 2 * lax.div(k, 2)


def kernel(
    first, second, out1, out2,
    raw, cen, oth, xt, stat, smsg, st1, pst, st2m, st2, fin, dg, scl, fix, nrm, cown, ypart, csend, crecv, ys, yr, zs, zr, g,
    acc1, acc2, rsq, csq, rowsq, colsq,
    p1, p1in, p1relay, p2, p2in, p2relay, xs, xr, ob1, ob2, ss, rs, ls, os_,
):
    dp = lax.axis_index("dp")
    rep = lax.axis_index("replica")
    c = lax.rem(dp, 2)
    ylo = lax.rem(lax.div(dp, 2), 2)
    z = lax.div(dp, 4)
    yhi = lax.div(rep, 4)
    x = lax.rem(rep, 4)

    def dev(x_, yhi_, ylo_, z_, c_):
        return (z_ * 4 + ylo_ * 2 + c_, yhi_ * 4 + x_)

    core = dev(x, yhi, ylo, z, 1 - c)
    sib = dev(x, yhi, 1 - ylo, z, c)
    sibc = dev(x, yhi, 1 - ylo, z, 1 - c)
    non = dev(x, 1 - yhi, 1 - ylo, z, c)
    nonc = dev(x, 1 - yhi, 1 - ylo, z, 1 - c)
    right = dev(lax.rem(x + 1, 4), yhi, ylo, z, c)
    left = dev(lax.rem(x + 3, 4), yhi, ylo, z, c)
    zdev = [dev(x, yhi, ylo, lax.rem(z + q, 8), c) for q in range(8)]
    zto = (zdev[1], zdev[7])

    def load(i, ref, col):
        return pltpu.make_async_copy(
            ref.at[:, pl.ds(pl.multiple_of(col, 256), 256)], raw.at[i], ls.at[i]
        )

    kz = lax.rem(z, 4)
    iz = lax.div(z, 4)
    base = yhi * 2048
    other = 2048 - base
    mine = x * 512
    lo = ylo * 256
    hi = 256 - lo
    loads = [load(2 * j + e, first, (base, other)[j] + mine + 256 * e) for j in range(2) for e in range(2)]
    for n in range(4):
        k = lax.rem(kz + n, 4)
        piece = lax.rem(x + k, 4) * 512
        for m, col in enumerate((base + lo, base + hi, other + hi)):
            loads.append(load(4 + 4 * m + k, second, col + piece))
    for cp in loads:
        cp.start()

    barrier = pltpu.get_barrier_semaphore()
    partners = [core, sib, sibc, non, nonc, right, left] + zdev[1:]
    for d in partners:
        pl.semaphore_signal(barrier, inc=1, device_id=d, device_id_type=MESH)

    def make(i, src, dst, to):
        return pltpu.make_async_remote_copy(
            src_ref=src, dst_ref=dst, send_sem=ss.at[i], recv_sem=rs.at[i], device_id=to, device_id_type=MESH
        )

    sends = []

    def send(i, src, dst, to):
        cp = make(i, src, dst, to)
        cp.start()
        sends.append(cp)
        return cp

    def local_stats(i, carry):
        pltpu.make_async_copy(first.at[:, pl.ds(0, 256)], raw.at[i], ls.at[i]).wait()
        v = raw[i]
        m = jnp.sum(v, 0, keepdims=True) * (1.0 / 256)
        dv = v - m
        r = dv.astype(BF16)
        cen[i] = r
        stat[i, 0:1, :] = m
        stat[i, 1:2, :] = jnp.sum(dv * dv, 0, keepdims=True)
        stat[i, 2:3, :] = jnp.sum(r.astype(F32), 0, keepdims=True)
        stat[i, 3:4, :] = jnp.zeros_like(m)
        return carry

    top, low = pl.ds(0, 128), pl.ds(128, 128)
    def blocks_k(m, carry):
        return local_stats(4 + 4 * lax.rem(m, 3) + lax.rem(kz + lax.div(m, 3), 4), carry)

    lax.fori_loop(0, 4, local_stats, 0)

    def turn(a, carry):
        xt[a] = cen[a].T
        return carry

    lax.fori_loop(0, 4, turn, 0)
    lax.fori_loop(0, 3, blocks_k, 0)
    pl.semaphore_wait(barrier, len(partners))

    def corr(s, carry):
        r = jnp.where(lax.rem(s, 2) == 1, 4 - lax.div(s + 1, 2), 4 + lax.div(s, 2))
        d = lax.rem(z + r, 8)
        i = lax.div(d, 4)
        k = lax.rem(d, 4)
        a = 2 * (1 - c) + i
        b = 2 * c + i
        v = nn(jnp.concatenate([xt[a], xt[b]], 0), cen[4 + k])
        csend[s, 0:256] = v[0:256].astype(BF16)
        cown[s] = v[256:512]
        v = nn(jnp.concatenate([xt[a, top], xt[b, top]], 0), cen[8 + k])
        csend[s, 256:384] = v[0:128].astype(BF16)
        ypart[s, 0:128] = v[128:256]
        v = nn(jnp.concatenate([xt[b, low], xt[a, low]], 0), cen[12 + k])
        csend[s, 384:512] = v[0:128].astype(BF16)
        ypart[s, 128:256] = v[128:256]
        make(M_C + s, csend.at[s], crecv.at[s], core).start()
        return carry

    y_sum = []

    def to_y(s):
        make(M_C + s, csend.at[s], crecv.at[s], core).wait_recv()
        ys[s] = (ypart[s] + crecv[s, 256:512].astype(F32)).astype(BF16)
        y_sum.append(
            (
                send(M_YP + 2 * s, ys.at[s, top], yr.at[s, top], sib),
                send(M_YP + 2 * s + 1, ys.at[s, low], yr.at[s, low], non),
            )
        )

    corr(0, 0)
    lax.fori_loop(3, 12, blocks_k, 0)

    def comoment(i, j):
        return jnp.sum((raw[i] - stat[i, 0:1, :]) * (raw[j] - stat[j, 0:1, :]), 0, keepdims=True)

    for n in range(4):
        smsg[0, n] = stat[STAT_SIB[n]]
        smsg[1, n] = stat[STAT_NON[n]]
    for b in range(8):
        st1[0, b] = stat[OWN[b]]
    smsg[0, 1 - ylo, 3:4, :] = comoment(1 - ylo, 8)
    st1[0, ylo, 3:4, :] = comoment(ylo, 4)
    st_in = [
        send(M_ST1 + 0, smsg.at[0], st1.at[2, pl.ds(0, 4)], sib),
        send(M_ST1 + 1, smsg.at[1], st1.at[2, pl.ds(4, 4)], non),
        send(M_ST1 + 2, smsg.at[0], st1.at[3, pl.ds(0, 4)], sibc),
        send(M_ST1 + 3, smsg.at[1], st1.at[3, pl.ds(4, 4)], nonc),
        send(M_ST1 + 4, st1.at[0], st1.at[1], core),
    ]
    to_y(0)
    lax.fori_loop(1, 3, corr, 0)
    to_y(1)
    to_y(2)
    for cp in st_in:
        cp.wait_recv()

    def merge(rows, count):
        total = sum(rows[1:], rows[0])
        m = total[0:1] * (1.0 / len(rows))
        dv = [r[0:1] - m for r in rows]
        m2 = total[1:2] + count * sum([d * d for d in dv[1:]], dv[0] * dv[0])
        return m, m2, total[2:3], total[3:4], dv

    def cross(p, q):
        return sum([a * b for a, b in zip(p[1:], q[1:])], p[0] * q[0])

    merged = [merge([st1[s, b] for s in range(4)], 256.0) for b in range(8)]
    for b, (m, m2, r, co, dv) in enumerate(merged):
        if b < 2:
            co = co + 256.0 * cross(dv, merged[2][4])
        for n, row in enumerate((m, m2, r, co)):
            pst[b, n : n + 1, :] = row
    st2_in = []
    for q in range(8):
        zq = lax.rem(z + q, 8)
        fa = ab(2 * c + lax.div(zq, 4))
        fk = kb(lax.rem(zq, 4))
        st2m[q, 0] = pst[zq]
        st2m[q, 3] = pst[2]
        for s in range(4):
            st2m[q, 1, s : s + 1, :] = st1[s, fa, 0:1, :]
            st2m[q, 2, s : s + 1, :] = st1[s, fk, 0:1, :]
        if q:
            st2_in.append(send(M_ST2 + q - 1, st2m.at[q], st2.at[q - 1], zdev[q]))

    lax.fori_loop(3, 5, corr, 0)

    def zslot(d, t, u):
        return d * 16 + (t - 1) * 4 + u * 2

    z_in = {}

    def chain(t, far):
        dist = 5 - t
        slot = (7 - 2 * dist, 8 - 2 * dist) if dist < 4 else (0, 0)
        if (t, far) in ((1, True), (2, False), (3, False), (4, False)):
            for n in set(slot):
                for cp in y_sum[n]:
                    cp.wait_recv()
        for s in range(2):
            for d in range(2):
                u = d if far else 1 - d
                n = slot[d]
                rows = slice(128 * u + 64 * s, 128 * u + 64 * s + 64)
                v = cown[n, rows] + crecv[n, rows].astype(F32) + yr[n, rows].astype(F32)
                if (d, t - 1, u, s) in z_in:
                    z_in[(d, t - 1, u, s)].wait_recv()
                    v = v + zr[zslot(d, t - 1, u) + s].astype(F32)
                i = zslot(d, t, u) + s
                zs[i] = v.astype(BF16)
                z_in[(d, t, u, s)] = send(M_ZR + i, zs.at[i], zr.at[i], zto[d])

    chain(1, True)
    to_y(3)
    to_y(4)
    lax.fori_loop(5, 8, corr, 0)
    chain(2, False)
    to_y(5)
    to_y(6)
    to_y(7)

    x_in = [
        send(M_Y + 0, cen.at[8, top], oth.at[2, top], sib),
        send(M_Y + 1, cen.at[12, low], oth.at[2, low], non),
        send(M_Y + 2, cen.at[0], oth.at[0], sib),
        send(M_Y + 3, cen.at[0], oth.at[4], non),
        send(M_Y + 4, cen.at[1], oth.at[1], sib),
        send(M_Y + 5, cen.at[1], oth.at[5], non),
    ]
    chain(2, True)

    def zero(n, carry):
        acc1[n] = jnp.zeros((512, 256), F32)
        acc2[n] = jnp.zeros((512, 256), F32)
        return carry

    lax.fori_loop(0, 4, zero, 0)
    rsq[...] = jnp.zeros_like(rsq)
    csq[...] = jnp.zeros_like(csq)
    chain(3, False)

    for cp in st2_in:
        cp.wait_recv()
    st2m_all = [st2m[0, 0]] + [st2[s, 0] for s in range(7)]
    k0_means = [st2m[0, 3]] + [st2[s, 3] for s in range(7)]
    m, m2, r, co, dv = merge(st2m_all, 1024.0)
    k0_dv = merge(k0_means, 1024.0)[4]
    fin[z, 0:1, :] = m + r * (1.0 / BATCH)
    fin[z, 1:2, :] = lax.rsqrt(m2 * (1.0 / BATCH) + EPS)
    fin[z, 2:3, :] = m
    fin[z, 3:4, :] = co + 1024.0 * cross(dv, k0_dv)
    fin_in = [send(M_ST3 + q - 1, fin.at[z], fin.at[z], zdev[q]) for q in range(1, 8)]

    chain(3, True)
    x_in[0].wait_recv()
    x_in[1].wait_recv()
    x_ring = [
        send(M_Y + 6, oth.at[2], oth.at[3], left),
        send(M_Y + 7, oth.at[2], oth.at[7], right),
    ]
    def norm(b, o):
        shift = st1[2 * o, b, 0:1, :] - fin[b, 0:1, :]
        scale = fin[b, 1:2, :]
        q = lax.rem(b, 4)
        idx = jnp.where(q < 2, 0, 2) + q + 2 * lax.div(b, 4)
        for h in range(2):
            rows = slice(128 * h, 128 * h + 128)
            v = cen[idx, rows] if o == 0 else oth[b, rows]
            nrm[b, o * 256 + 128 * h : o * 256 + 128 * h + 128, :] = ((v.astype(F32) + shift) * scale).astype(BF16)

    def norms(o):
        lax.fori_loop(0, 8, lambda b, carry: (norm(b, o), carry)[1], 0)

    chain(4, False)
    for cp in fin_in:
        cp.wait_recv()
    cii = fin[ylo, 3:4, :] * fin[ylo, 1:2, :] * fin[2, 1:2, :] * (1.0 / BATCH)
    dg[0:1, :] = cii
    dg[1:2, :] = (-2.0 * (1.0 - cii)).astype(BF16).astype(F32)
    norms(0)
    chain(4, True)
    x_ring[0].wait_recv()
    x_ring.append(send(M_Y + 8, oth.at[3, top], oth.at[6, top], left))
    x_ring[1].wait_recv()
    x_ring.append(send(M_Y + 9, oth.at[7, low], oth.at[6, low], right))

    fa = ab(2 * c + lax.div(z, 4))
    fk = kb(lax.rem(z, 4))
    pad = jnp.zeros((7, 256), F32)
    ra = jnp.concatenate([fin[fa, 1:2, :] * (2.0 * LAMBDA / BATCH), pad], 0)
    rk = jnp.concatenate([fin[fk, 1:2, :], pad], 0)
    rows_id = lax.broadcasted_iota(jnp.int32, (256, 256), 0)
    cols_id = lax.broadcasted_iota(jnp.int32, (256, 256), 1)
    off = rows_id + jnp.where((c == 0) & (z == 4 * ylo), 0, 512) != cols_id
    scl[...] = jnp.where(off, tn(ra, rk, HIGH), 0.0)
    mu_a = [(st2m[0, 1] if s == 0 else st2[s - 1, 1]) - fin[fa, 2:3, :] for s in range(8)]
    mu_k = [(st2m[0, 2] if s == 0 else st2[s - 1, 2]) - fin[fk, 2:3, :] for s in range(8)]
    fix[...] = scl[...] * tn(jnp.concatenate(mu_a, 0) * 256.0, jnp.concatenate(mu_k, 0), HIGH)
    for cp in y_sum[7]:
        cp.wait_recv()
    for s in range(2):
        for u in range(2):
            q = 2 * u + s
            rows = slice(64 * q, 64 * q + 64)
            v = cown[7, rows] + crecv[7, rows].astype(F32) + yr[7, rows].astype(F32)
            for d in (1 - u, u):
                z_in[(d, 4, u, s)].wait_recv()
                v = v + zr[zslot(d, 4, u) + s].astype(F32)
            part = g.at[c, z, q]
            g[c, z, q] = (v * scl[rows] + fix[rows]).astype(BF16)
            for d in (u, 1 - u):
                send(M_ZG + zslot(d, 1, u) + s, part, part, zto[d])
    send(M_GD + 0, g.at[c, z, pl.ds(0, 2)], g.at[c, z, pl.ds(0, 2)], core)
    send(M_GD + 1, g.at[c, z, pl.ds(2, 2)], g.at[c, z, pl.ds(2, 2)], core)

    def arrive(t, far, onward):
        for s in range(2):
            for d in range(2):
                u = d if far else 1 - d
                i = d * 16 + (t - 1) * 4 + u * 2 + s
                source = lax.rem(z + (8 - t if d == 0 else t), 8)
                part = g.at[c, source, 2 * u + s]
                make(M_ZG + i, part, part, zto[d]).wait_recv()
                if onward is not None:
                    start = make(M_ZG + i + 4, part, part, zto[d]).start
                    if onward is True:
                        start()
                    else:
                        pl.when(onward)(start)
                if s == 1:
                    both = g.at[c, source, pl.ds(2 * u, 2)]
                    make(M_GD + 4 * t + 2 * d + u, both, both, core).start()

    def use(j, zs_):
        a = 2 * j + lax.div(zs_, 4)
        k = lax.rem(zs_, 4)
        ga = g[j, zs_].reshape(256, 256)
        acc1[a] += nt(nrm[kb(k)], ga)
        acc2[k] += nn(nrm[ab(a)], ga)
        v = ga.astype(F32)
        s = v * v
        rsq[a] += s[:, 0:128] + s[:, 128:256]
        csq[k] += jnp.sum(s.reshape(32, 8, 256), 0)

    def from_core(t, d, u):
        part = g.at[0, 0, pl.ds(0, 2)]
        make(M_GD + 4 * t + 2 * d + u, part, part, core).wait_recv()

    def uses(t, mine_too):
        def one(n, inner):
            if not mine_too:
                for u in range(2):
                    from_core(t, n, u)
            use(c if mine_too else 1 - c, lax.rem(z + (8 - t) + n * 2 * t, 8))
            return inner

        lax.fori_loop(0, jnp.where(t == 0, 1, 2), one, 0)

    for cp in x_in[2:] + x_ring[2:]:
        cp.wait_recv()
    norms(1)
    uses(0, True)

    def step(t, carry):
        arrive(t, True, True)
        uses(t - 1, False)
        arrive(t, False, t < 3)
        uses(t, True)
        return carry

    def partial1(a, o):
        b = ab(a)
        rows = slice(o * 256, o * 256 + 256)
        f = nrm[b, rows].astype(F32)
        v = acc1[a, rows] - f * rowsq[a, 0:1, :]
        gd = jnp.where(a == ylo, dg[1:2, :], 0.0)
        v = v + (nrm[2, rows].astype(F32) - f * dg[0:1, :]) * gd
        return v * fin[b, 1:2, :]

    def p1_start(ph, e):
        for a in (e, 2 + e):
            rowsq[a] = nt(jnp.ones((8, 128), F32), rsq[a], HIGH) * (0.5 / LAMBDA)
        m = M_P1 + 6 * ph
        p1[ph, 0] = partial1(2 + e, 0).astype(BF16)
        relay = [
            send(m, p1.at[ph, 0, top], p1relay.at[ph, top], sib),
            send(m + 1, p1.at[ph, 0, low], p1relay.at[ph, low], non),
        ]
        p1[ph, 1] = partial1(2 + e, 1).astype(BF16)
        a = send(m + 2, p1.at[ph, 1, low], p1in.at[ph, 1, low], non)
        p1[ph, 2] = partial1(e, 1).astype(BF16)
        b = send(m + 3, p1.at[ph, 2, top], p1in.at[ph, 0, top], sib)
        return relay, [a, b]

    def p1_add(ph, relay):
        m = M_P1 + 6 * ph
        relay[0].wait_recv()
        p1[ph, 1, top] = (p1[ph, 1, top].astype(F32) + p1relay[ph, top].astype(F32)).astype(BF16)
        a = send(m + 4, p1.at[ph, 1, top], p1in.at[ph, 1, top], non)
        relay[1].wait_recv()
        p1[ph, 2, low] = (p1[ph, 2, low].astype(F32) + p1relay[ph, low].astype(F32)).astype(BF16)
        return [a, send(m + 5, p1.at[ph, 2, low], p1in.at[ph, 0, low], sib)]

    lax.fori_loop(1, 4, step, 0)
    uses(3, False)
    relay1, in1 = p1_start(0, iz)
    arrive(4, True, None)

    def final_two(n, carry):
        use(lax.rem(c + n, 2), lax.rem(z + 4, 8))
        return carry

    lax.fori_loop(0, 1, final_two, 0)
    from_core(4, 0, 0)
    from_core(4, 1, 1)
    lax.fori_loop(1, 2, final_two, 0)

    for k in range(4):
        colsq[k] = jnp.sum(csq[k], 0, keepdims=True) * (0.5 / LAMBDA)

    def partial2(k, o):
        b = KB[k]
        rows = slice(o * 256, o * 256 + 256)
        s = nrm[b, rows].astype(F32)
        v = acc2[k, rows] - s * colsq[k]
        if k == 0:
            v = v + (nrm[ylo, rows].astype(F32) - s * dg[0:1, :]) * dg[1:2, :]
        return v * fin[b, 1:2, :]

    def p2_relay(o):
        p2[2, o] = partial2(2, o).astype(BF16)
        return [
            send(M_P2O + 2 * o, p2.at[2, o, top], p2relay.at[o, top], right),
            send(M_P2O + 2 * o + 1, p2.at[2, o, low], p2relay.at[o, low], left),
        ]

    def p2_send(o):
        p2[1, o] = partial2(1, o).astype(BF16)
        a = send(M_P2R + 2 * o, p2.at[1, o, low], p2in.at[0, o, low], right)
        p2[3, o] = partial2(3, o).astype(BF16)
        return [a, send(M_P2L + 2 * o, p2.at[3, o, top], p2in.at[1, o, top], left)]

    def p2_add(o, relay):
        relay[0].wait_recv()
        p2[1, o, top] = (p2[1, o, top].astype(F32) + p2relay[o, top].astype(F32)).astype(BF16)
        a = send(M_P2R + 2 * o + 1, p2.at[1, o, top], p2in.at[0, o, top], right)
        relay[1].wait_recv()
        p2[3, o, low] = (p2[3, o, low].astype(F32) + p2relay[o, low].astype(F32)).astype(BF16)
        return [a, send(M_P2L + 2 * o + 1, p2.at[3, o, low], p2in.at[1, o, low], left)]

    def sent(i, part):
        make(i, part, part, core).wait_send()

    def finish_sends():
        for cp in done:
            cp.wait_send()
        for s in range(8):
            sent(M_C + s, csend.at[s])
        for d in range(2):
            for t in range(1, 5):
                for u in range(2):
                    if t > 1 and (t < 4 or u == d):
                        for s in range(2):
                            sent(M_ZG + zslot(d, t, u) + s, g.at[0, 0, 0])
                    if t < 4 or u == d:
                        sent(M_GD + 4 * t + 2 * d + u, g.at[0, 0, pl.ds(0, 2)])

    done = list(sends)
    relay2 = p2_relay(1)
    in1 += p1_add(0, relay1)
    in2 = p2_send(1)
    relay1, more = p1_start(1, 1 - iz)
    in1 += more
    relay20 = p2_relay(0)
    in2 += p2_add(1, relay2)
    in20 = p2_send(0)
    ob2[0] = partial2(0, 1)
    ob2[1] = partial2(0, 0)
    in1 += p1_add(1, relay1)
    in20 += p2_add(0, relay20)
    finish_sends()
    for cp in in2:
        cp.wait_recv()
    xs[...] = (ob2[0] + p2in[0, 1].astype(F32) + p2in[1, 1].astype(F32)).astype(BF16)
    x_last = send(M_X, xs, xr, sib)
    ob1[0] = partial1(iz, 0)
    ob1[1] = partial1(1 - iz, 0)
    outs = []

    def put(src, ref, col, i):
        cp = pltpu.make_async_copy(src, ref.at[:, pl.ds(pl.multiple_of(col, 256), 256)], os_.at[i])
        cp.start()
        outs.append(cp)

    for cp in in20:
        cp.wait_recv()
    ob2[1] = ob2[1] + p2in[0, 0].astype(F32) + p2in[1, 0].astype(F32)
    put(ob2.at[1], out2, lo, 0)
    for cp in in1:
        cp.wait_recv()
    for ph, e in enumerate((iz, 1 - iz)):
        ob1[ph] = ob1[ph] + p1in[ph, 0].astype(F32) + p1in[ph, 1].astype(F32)
        put(ob1.at[ph], out1, e * 256, 1 + ph)
    x_last.wait_recv()
    ob2[0] = xr[...].astype(F32)
    put(ob2.at[0], out2, hi, 3)
    for cp in outs:
        cp.wait()
    for cp in sends[len(done) :]:
        cp.wait_send()


def write_kernel(a, b, out1, out2, sem):
    cps = []
    for n, (src, dst) in enumerate(((a, out1), (b, out2))):
        for q in range(2):
            rows = pl.ds(128 * q, 128)
            cps.append(pltpu.make_async_copy(src.at[rows], dst.at[rows], sem.at[2 * n + q]))
    for cp in cps:
        cp.start()
    for cp in cps:
        cp.wait()


def body(first, second):
    v = pltpu.VMEM
    out = jax.ShapeDtypeStruct((256, 512), F32)
    anywhere = pl.BlockSpec(memory_space=pl.ANY)
    parts = pl.pallas_call(
        kernel,
        out_shape=(out, out),
        in_specs=[anywhere, anywhere],
        out_specs=(anywhere, anywhere),
        scratch_shapes=[
            v((16, 256, 256), F32),
            v((16, 256, 256), BF16),
            v((8, 256, 256), BF16),
            v((4, 256, 256), BF16),
            v((16, 4, 256), F32),
            v((2, 4, 4, 256), F32),
            v((4, 8, 4, 256), F32),
            v((8, 4, 256), F32),
            v((8, 4, 4, 256), F32),
            v((7, 4, 4, 256), F32),
            v((8, 4, 256), F32),
            v((2, 256), F32),
            v((256, 256), F32),
            v((256, 256), F32),
            v((8, 512, 256), BF16),
            v((8, 256, 256), F32),
            v((8, 256, 256), F32),
            v((8, 512, 256), BF16),
            v((8, 512, 256), BF16),
            v((8, 256, 256), BF16),
            v((8, 256, 256), BF16),
            v((32, 64, 256), BF16),
            v((32, 64, 256), BF16),
            v((2, 8, 4, 64, 256), BF16),
            v((4, 512, 256), F32),
            v((4, 512, 256), F32),
            v((4, 256, 128), F32),
            v((4, 8, 256), F32),
            v((4, 8, 256), F32),
            v((4, 1, 256), F32),
            v((2, 3, 256, 256), BF16),
            v((2, 2, 256, 256), BF16),
            v((2, 256, 256), BF16),
            v((4, 2, 256, 256), BF16),
            v((2, 2, 256, 256), BF16),
            v((2, 256, 256), BF16),
            v((256, 256), BF16),
            v((256, 256), BF16),
            v((2, 256, 256), F32),
            v((2, 256, 256), F32),
            pltpu.SemaphoreType.DMA((M_ALL,)),
            pltpu.SemaphoreType.DMA((M_ALL,)),
            pltpu.SemaphoreType.DMA((16,)),
            pltpu.SemaphoreType.DMA((4,)),
        ],
        compiler_params=pltpu.CompilerParams(
            collective_id=0, has_side_effects=True, vmem_limit_bytes=51 * 1024 * 1024
        ),
    )(first, second)
    return pl.pallas_call(
        write_kernel,
        out_shape=(out, out),
        in_specs=[pl.BlockSpec(memory_space=pltpu.VMEM)] * 2,
        out_specs=(anywhere, anywhere),
        scratch_shapes=[pltpu.SemaphoreType.DMA((4,))],
        compiler_params=pltpu.CompilerParams(vmem_limit_bytes=8 * 1024 * 1024),
    )(*parts)


def solution(mesh):
    return jax.shard_map(
        body,
        mesh=mesh,
        in_specs=(P("dp", None), P("dp", None)),
        out_specs=(P("dp", "replica"), P("dp", "replica")),
        check_vma=False,
    )
```

```python
import jax
import jax.numpy as jnp
from jax import lax
from jax.experimental import pallas as pl
from jax.experimental.pallas import tpu as pltpu
from jax.sharding import PartitionSpec as P

LAMBDA = 0.0051
EPS = 1e-05
MESH = pl.DeviceIdType.MESH
F32 = jnp.float32
BF16 = jnp.bfloat16
BATCH = 8192

OWN = (0, 1, 4, 5, 2, 3, 6, 7)
STAT_SIB = (0, 1, 8, 9)
STAT_NON = (0, 1, 14, 15)
KB = (2, 3, 6, 7)
AB = (0, 1, 4, 5)

M_Y = 0
M_ST1 = 12
M_ST2 = 17
M_ST3 = 24
M_C = 31
M_YP = 39
M_ZR = 55
M_ZG = 87
M_GD = 119
M_P1 = 139
M_P2O = 151
M_P2R = 155
M_P2L = 159
M_X = 163
M_ALL = 164

HIGH = lax.Precision.HIGHEST


def nt(a, b, precision=None):
    return lax.dot_general(
        a, b, (((1,), (1,)), ((), ())), preferred_element_type=F32, precision=precision
    )


def tn(a, b, precision=None):
    return lax.dot_general(
        a, b, (((0,), (0,)), ((), ())), preferred_element_type=F32, precision=precision
    )


def nn(a, b):
    return lax.dot_general(a, b, (((1,), (0,)), ((), ())), preferred_element_type=F32)


def ab(a):
    return a + 2 * lax.div(a, 2)


def kb(k):
    return k + 2 + 2 * lax.div(k, 2)


def kernel(
    first, second, out1, out2,
    raw, cen, oth, xt, stat, smsg, st1, pst, st2m, st2, fin, dg, scl, fix, nrm, cown, ypart, csend, crecv, ys, yr, zs, zr, g,
    acc1, acc2, rsq, csq, rowsq, colsq,
    p1, p1in, p1relay, p2, p2in, p2relay, xs, xr, ob1, ob2, ss, rs, ls, os_,
):
    dp = lax.axis_index("dp")
    rep = lax.axis_index("replica")
    c = lax.rem(dp, 2)
    ylo = lax.rem(lax.div(dp, 2), 2)
    z = lax.div(dp, 4)
    yhi = lax.div(rep, 4)
    x = lax.rem(rep, 4)

    def dev(x_, yhi_, ylo_, z_, c_):
        return (z_ * 4 + ylo_ * 2 + c_, yhi_ * 4 + x_)

    core = dev(x, yhi, ylo, z, 1 - c)
    sib = dev(x, yhi, 1 - ylo, z, c)
    sibc = dev(x, yhi, 1 - ylo, z, 1 - c)
    non = dev(x, 1 - yhi, 1 - ylo, z, c)
    nonc = dev(x, 1 - yhi, 1 - ylo, z, 1 - c)
    right = dev(lax.rem(x + 1, 4), yhi, ylo, z, c)
    left = dev(lax.rem(x + 3, 4), yhi, ylo, z, c)
    zdev = [dev(x, yhi, ylo, lax.rem(z + q, 8), c) for q in range(8)]
    zto = (zdev[1], zdev[7])

    def load(i, ref, col):
        return pltpu.make_async_copy(
            ref.at[:, pl.ds(pl.multiple_of(col, 256), 256)], raw.at[i], ls.at[i]
        )

    kz = lax.rem(z, 4)
    iz = lax.div(z, 4)
    base = yhi * 2048
    other = 2048 - base
    mine = x * 512
    lo = ylo * 256
    hi = 256 - lo
    def load_first(e):
        for j in range(2):
            load(2 * j + e, first, (base, other)[j] + mine + 256 * e).start()

    def load_second(k):
        piece = lax.rem(x + k, 4) * 512
        for m, col in enumerate((base + lo, base + hi, other + hi)):
            load(4 + 4 * m + k, second, col + piece).start()

    load_first(1 - iz)
    load_second(kz)
    barrier = pltpu.get_barrier_semaphore()
    partners = [core, sib, sibc, non, nonc, right, left] + zdev[1:]
    for d in partners:
        pl.semaphore_signal(barrier, inc=1, device_id=d, device_id_type=MESH)
    load_first(iz)
    for n in (3, 1, 2):
        load_second(lax.rem(kz + n, 4))

    def make(i, src, dst, to):
        return pltpu.make_async_remote_copy(
            src_ref=src, dst_ref=dst, send_sem=ss.at[i], recv_sem=rs.at[i], device_id=to, device_id_type=MESH
        )

    sends = []

    def send(i, src, dst, to):
        cp = make(i, src, dst, to)
        cp.start()
        sends.append(cp)
        return cp

    def local_stats(i, carry):
        pltpu.make_async_copy(first.at[:, pl.ds(0, 256)], raw.at[i], ls.at[i]).wait()
        v = raw[i]
        m = jnp.sum(v, 0, keepdims=True) * (1.0 / 256)
        dv = v - m
        r = dv.astype(BF16)
        cen[i] = r
        stat[i, 0:1, :] = m
        stat[i, 1:2, :] = jnp.sum(dv * dv, 0, keepdims=True)
        stat[i, 2:3, :] = jnp.sum(r.astype(F32), 0, keepdims=True)
        stat[i, 3:4, :] = jnp.zeros_like(m)
        return carry

    top, low = pl.ds(0, 128), pl.ds(128, 128)

    def blocks_k(m, carry):
        return local_stats(4 + 4 * lax.rem(m, 3) + lax.rem(kz + lax.div(m, 3), 4), carry)

    def first_blocks(e):
        def one(j, carry):
            local_stats(2 * j + e, carry)
            xt[2 * j + e] = cen[2 * j + e].T
            return carry

        lax.fori_loop(0, 2, one, 0)

    first_blocks(1 - iz)
    lax.fori_loop(0, 3, blocks_k, 0)
    pl.semaphore_wait(barrier, len(partners))

    def corr(s, carry):
        r = jnp.where(lax.rem(s, 2) == 1, 4 - lax.div(s + 1, 2), 4 + lax.div(s, 2))
        d = lax.rem(z + r, 8)
        i = lax.div(d, 4)
        k = lax.rem(d, 4)
        a = 2 * (1 - c) + i
        b = 2 * c + i
        v = nn(jnp.concatenate([xt[a], xt[b]], 0), cen[4 + k])
        csend[s, 0:256] = v[0:256].astype(BF16)
        cown[s] = v[256:512]
        v = nn(jnp.concatenate([xt[a, top], xt[b, top]], 0), cen[8 + k])
        csend[s, 256:384] = v[0:128].astype(BF16)
        ypart[s, 0:128] = v[128:256]
        v = nn(jnp.concatenate([xt[b, low], xt[a, low]], 0), cen[12 + k])
        csend[s, 384:512] = v[0:128].astype(BF16)
        ypart[s, 128:256] = v[128:256]
        make(M_C + s, csend.at[s], crecv.at[s], core).start()
        return carry

    y_sum = []

    def to_y(s):
        make(M_C + s, csend.at[s], crecv.at[s], core).wait_recv()
        ys[s] = (ypart[s] + crecv[s, 256:512].astype(F32)).astype(BF16)
        y_sum.append(
            (
                send(M_YP + 2 * s, ys.at[s, top], yr.at[s, top], sib),
                send(M_YP + 2 * s + 1, ys.at[s, low], yr.at[s, low], non),
            )
        )

    corr(0, 0)
    first_blocks(iz)
    lax.fori_loop(3, 12, blocks_k, 0)
    to_y(0)
    lax.fori_loop(1, 3, corr, 0)

    def comoment(i, j):
        return jnp.sum((raw[i] - stat[i, 0:1, :]) * (raw[j] - stat[j, 0:1, :]), 0, keepdims=True)

    for n in range(4):
        smsg[0, n] = stat[STAT_SIB[n]]
        smsg[1, n] = stat[STAT_NON[n]]
    for b in range(8):
        st1[0, b] = stat[OWN[b]]
    smsg[0, 1 - ylo, 3:4, :] = comoment(1 - ylo, 8)
    st1[0, ylo, 3:4, :] = comoment(ylo, 4)
    st_in = [
        send(M_ST1 + 0, smsg.at[0], st1.at[2, pl.ds(0, 4)], sib),
        send(M_ST1 + 1, smsg.at[1], st1.at[2, pl.ds(4, 4)], non),
        send(M_ST1 + 2, smsg.at[0], st1.at[3, pl.ds(0, 4)], sibc),
        send(M_ST1 + 3, smsg.at[1], st1.at[3, pl.ds(4, 4)], nonc),
        send(M_ST1 + 4, st1.at[0], st1.at[1], core),
    ]
    to_y(1)
    to_y(2)

    def zslot(d, t, u):
        return d * 16 + (t - 1) * 4 + u * 2

    z_in = {}

    def chain(t, far):
        dist = 5 - t
        slot = (7 - 2 * dist, 8 - 2 * dist) if dist < 4 else (0, 0)
        if (t, far) in ((1, True), (2, False), (3, False), (4, False)):
            for n in set(slot):
                for cp in y_sum[n]:
                    cp.wait_recv()
        for s in range(2):
            for d in range(2):
                u = d if far else 1 - d
                n = slot[d]
                rows = slice(128 * u + 64 * s, 128 * u + 64 * s + 64)
                v = cown[n, rows] + crecv[n, rows].astype(F32) + yr[n, rows].astype(F32)
                if (d, t - 1, u, s) in z_in:
                    z_in[(d, t - 1, u, s)].wait_recv()
                    v = v + zr[zslot(d, t - 1, u) + s].astype(F32)
                i = zslot(d, t, u) + s
                zs[i] = v.astype(BF16)
                z_in[(d, t, u, s)] = send(M_ZR + i, zs.at[i], zr.at[i], zto[d])

    chain(1, True)
    lax.fori_loop(3, 5, corr, 0)
    for cp in st_in:
        cp.wait_recv()

    def merge(rows, count):
        total = sum(rows[1:], rows[0])
        m = total[0:1] * (1.0 / len(rows))
        dv = [r[0:1] - m for r in rows]
        m2 = total[1:2] + count * sum([d * d for d in dv[1:]], dv[0] * dv[0])
        return m, m2, total[2:3], total[3:4], dv

    def cross(p, q):
        return sum([a * b for a, b in zip(p[1:], q[1:])], p[0] * q[0])

    merged = [merge([st1[s, b] for s in range(4)], 256.0) for b in range(8)]
    for b, (m, m2, r, co, dv) in enumerate(merged):
        if b < 2:
            co = co + 256.0 * cross(dv, merged[2][4])
        for n, row in enumerate((m, m2, r, co)):
            pst[b, n : n + 1, :] = row
    st2_in = []
    for q in range(8):
        zq = lax.rem(z + q, 8)
        fa = ab(2 * c + lax.div(zq, 4))
        fk = kb(lax.rem(zq, 4))
        st2m[q, 0] = pst[zq]
        st2m[q, 3] = pst[2]
        for s in range(4):
            st2m[q, 1, s : s + 1, :] = st1[s, fa, 0:1, :]
            st2m[q, 2, s : s + 1, :] = st1[s, fk, 0:1, :]
        if q:
            st2_in.append(send(M_ST2 + q - 1, st2m.at[q], st2.at[q - 1], zdev[q]))

    to_y(3)
    to_y(4)
    chain(2, False)
    chain(2, True)
    lax.fori_loop(5, 8, corr, 0)

    def zero(n, carry):
        acc1[n] = jnp.zeros((512, 256), F32)
        acc2[n] = jnp.zeros((512, 256), F32)
        return carry

    lax.fori_loop(0, 4, zero, 0)
    rsq[...] = jnp.zeros_like(rsq)
    csq[...] = jnp.zeros_like(csq)
    to_y(5)
    to_y(6)
    to_y(7)

    x_in = [
        send(M_Y + 0, cen.at[8, top], oth.at[2, top], sib),
        send(M_Y + 1, cen.at[12, low], oth.at[2, low], non),
        send(M_Y + 2, cen.at[0], oth.at[0], sib),
        send(M_Y + 3, cen.at[0], oth.at[4], non),
        send(M_Y + 4, cen.at[1], oth.at[1], sib),
        send(M_Y + 5, cen.at[1], oth.at[5], non),
    ]
    chain(3, False)

    for cp in st2_in:
        cp.wait_recv()
    st2m_all = [st2m[0, 0]] + [st2[s, 0] for s in range(7)]
    k0_means = [st2m[0, 3]] + [st2[s, 3] for s in range(7)]
    m, m2, r, co, dv = merge(st2m_all, 1024.0)
    k0_dv = merge(k0_means, 1024.0)[4]
    fin[z, 0:1, :] = m + r * (1.0 / BATCH)
    fin[z, 1:2, :] = lax.rsqrt(m2 * (1.0 / BATCH) + EPS)
    fin[z, 2:3, :] = m
    fin[z, 3:4, :] = co + 1024.0 * cross(dv, k0_dv)
    fin_in = [send(M_ST3 + q - 1, fin.at[z], fin.at[z], zdev[q]) for q in range(1, 8)]

    chain(3, True)
    x_in[0].wait_recv()
    x_in[1].wait_recv()
    x_ring = [
        send(M_Y + 6, oth.at[2], oth.at[3], left),
        send(M_Y + 7, oth.at[2], oth.at[7], right),
    ]

    def norm(b, o):
        shift = st1[2 * o, b, 0:1, :] - fin[b, 0:1, :]
        scale = fin[b, 1:2, :]
        q = lax.rem(b, 4)
        idx = jnp.where(q < 2, 0, 2) + q + 2 * lax.div(b, 4)
        for h in range(2):
            rows = slice(128 * h, 128 * h + 128)
            v = cen[idx, rows] if o == 0 else oth[b, rows]
            nrm[b, o * 256 + 128 * h : o * 256 + 128 * h + 128, :] = ((v.astype(F32) + shift) * scale).astype(BF16)

    def norms(o):
        lax.fori_loop(0, 8, lambda b, carry: (norm(b, o), carry)[1], 0)

    chain(4, False)
    for cp in fin_in:
        cp.wait_recv()
    cii = fin[ylo, 3:4, :] * fin[ylo, 1:2, :] * fin[2, 1:2, :] * (1.0 / BATCH)
    dg[0:1, :] = cii
    dg[1:2, :] = (-2.0 * (1.0 - cii)).astype(BF16).astype(F32)
    norms(0)
    chain(4, True)
    x_ring[0].wait_recv()
    x_ring.append(send(M_Y + 8, oth.at[3, top], oth.at[6, top], left))
    x_ring[1].wait_recv()
    x_ring.append(send(M_Y + 9, oth.at[7, low], oth.at[6, low], right))

    fa = ab(2 * c + lax.div(z, 4))
    fk = kb(lax.rem(z, 4))
    pad = jnp.zeros((7, 256), F32)
    ra = jnp.concatenate([fin[fa, 1:2, :] * (2.0 * LAMBDA / BATCH), pad], 0)
    rk = jnp.concatenate([fin[fk, 1:2, :], pad], 0)
    rows_id = lax.broadcasted_iota(jnp.int32, (256, 256), 0)
    cols_id = lax.broadcasted_iota(jnp.int32, (256, 256), 1)
    off = rows_id + jnp.where((c == 0) & (z == 4 * ylo), 0, 512) != cols_id
    scl[...] = jnp.where(off, tn(ra, rk, HIGH), 0.0)
    mu_a = [(st2m[0, 1] if s == 0 else st2[s - 1, 1]) - fin[fa, 2:3, :] for s in range(8)]
    mu_k = [(st2m[0, 2] if s == 0 else st2[s - 1, 2]) - fin[fk, 2:3, :] for s in range(8)]
    fix[...] = scl[...] * tn(jnp.concatenate(mu_a, 0) * 256.0, jnp.concatenate(mu_k, 0), HIGH)

    for cp in y_sum[7]:
        cp.wait_recv()
    for s in range(2):
        for u in range(2):
            q = 2 * u + s
            rows = slice(64 * q, 64 * q + 64)
            v = cown[7, rows] + crecv[7, rows].astype(F32) + yr[7, rows].astype(F32)
            for d in (1 - u, u):
                z_in[(d, 4, u, s)].wait_recv()
                v = v + zr[zslot(d, 4, u) + s].astype(F32)
            part = g.at[c, z, q]
            g[c, z, q] = (v * scl[rows] + fix[rows]).astype(BF16)
            for d in (u, 1 - u):
                send(M_ZG + zslot(d, 1, u) + s, part, part, zto[d])
    send(M_GD + 0, g.at[c, z, pl.ds(0, 2)], g.at[c, z, pl.ds(0, 2)], core)
    send(M_GD + 1, g.at[c, z, pl.ds(2, 2)], g.at[c, z, pl.ds(2, 2)], core)

    def arrive(t, far, onward):
        for s in range(2):
            for d in range(2):
                u = d if far else 1 - d
                i = d * 16 + (t - 1) * 4 + u * 2 + s
                source = lax.rem(z + (8 - t if d == 0 else t), 8)
                part = g.at[c, source, 2 * u + s]
                make(M_ZG + i, part, part, zto[d]).wait_recv()
                if onward is not None:
                    start = make(M_ZG + i + 4, part, part, zto[d]).start
                    if onward is True:
                        start()
                    else:
                        pl.when(onward)(start)
                if s == 1:
                    both = g.at[c, source, pl.ds(2 * u, 2)]
                    make(M_GD + 4 * t + 2 * d + u, both, both, core).start()

    def use(j, zs_):
        a = 2 * j + lax.div(zs_, 4)
        k = lax.rem(zs_, 4)
        ga = g[j, zs_].reshape(256, 256)
        acc1[a] += nt(nrm[kb(k)], ga)
        acc2[k] += nn(nrm[ab(a)], ga)
        v = ga.astype(F32)
        s = v * v
        rsq[a] += s[:, 0:128] + s[:, 128:256]
        csq[k] += jnp.sum(s.reshape(32, 8, 256), 0)

    def from_core(t, d, u):
        part = g.at[0, 0, pl.ds(0, 2)]
        make(M_GD + 4 * t + 2 * d + u, part, part, core).wait_recv()

    def uses(t, mine_too):
        def one(n, inner):
            if not mine_too:
                for u in range(2):
                    from_core(t, n, u)
            use(c if mine_too else 1 - c, lax.rem(z + (8 - t) + n * 2 * t, 8))
            return inner

        lax.fori_loop(0, jnp.where(t == 0, 1, 2), one, 0)

    for cp in x_in[2:] + x_ring[2:]:
        cp.wait_recv()
    norms(1)
    uses(0, True)

    def step(t, carry):
        arrive(t, True, True)
        uses(t - 1, False)
        arrive(t, False, t < 3)
        uses(t, True)
        return carry

    def partial1(a, o):
        b = ab(a)
        rows = slice(o * 256, o * 256 + 256)
        f = nrm[b, rows].astype(F32)
        v = acc1[a, rows] - f * rowsq[a, 0:1, :]
        gd = jnp.where(a == ylo, dg[1:2, :], 0.0)
        v = v + (nrm[2, rows].astype(F32) - f * dg[0:1, :]) * gd
        return v * fin[b, 1:2, :]

    def p1_start(ph, e):
        for a in (e, 2 + e):
            rowsq[a] = nt(jnp.ones((8, 128), F32), rsq[a], HIGH) * (0.5 / LAMBDA)
        m = M_P1 + 6 * ph
        p1[ph, 0] = partial1(2 + e, 0).astype(BF16)
        relay = [
            send(m, p1.at[ph, 0, top], p1relay.at[ph, top], sib),
            send(m + 1, p1.at[ph, 0, low], p1relay.at[ph, low], non),
        ]
        p1[ph, 1] = partial1(2 + e, 1).astype(BF16)
        a = send(m + 2, p1.at[ph, 1, low], p1in.at[ph, 1, low], non)
        p1[ph, 2] = partial1(e, 1).astype(BF16)
        b = send(m + 3, p1.at[ph, 2, top], p1in.at[ph, 0, top], sib)
        return relay, [a, b]

    def p1_add(ph, relay):
        m = M_P1 + 6 * ph
        relay[0].wait_recv()
        p1[ph, 1, top] = (p1[ph, 1, top].astype(F32) + p1relay[ph, top].astype(F32)).astype(BF16)
        a = send(m + 4, p1.at[ph, 1, top], p1in.at[ph, 1, top], non)
        relay[1].wait_recv()
        p1[ph, 2, low] = (p1[ph, 2, low].astype(F32) + p1relay[ph, low].astype(F32)).astype(BF16)
        return [a, send(m + 5, p1.at[ph, 2, low], p1in.at[ph, 0, low], sib)]

    lax.fori_loop(1, 4, step, 0)
    uses(3, False)
    relay1, in1 = p1_start(0, iz)
    arrive(4, True, None)

    def final_two(n, carry):
        use(lax.rem(c + n, 2), lax.rem(z + 4, 8))
        return carry

    lax.fori_loop(0, 1, final_two, 0)
    from_core(4, 0, 0)
    from_core(4, 1, 1)
    lax.fori_loop(1, 2, final_two, 0)

    for k in range(4):
        colsq[k] = jnp.sum(csq[k], 0, keepdims=True) * (0.5 / LAMBDA)

    def partial2(k, o):
        b = KB[k]
        rows = slice(o * 256, o * 256 + 256)
        s = nrm[b, rows].astype(F32)
        v = acc2[k, rows] - s * colsq[k]
        if k == 0:
            v = v + (nrm[ylo, rows].astype(F32) - s * dg[0:1, :]) * dg[1:2, :]
        return v * fin[b, 1:2, :]

    def p2_relay(o):
        p2[2, o] = partial2(2, o).astype(BF16)
        return [
            send(M_P2O + 2 * o, p2.at[2, o, top], p2relay.at[o, top], right),
            send(M_P2O + 2 * o + 1, p2.at[2, o, low], p2relay.at[o, low], left),
        ]

    def p2_send(o):
        p2[1, o] = partial2(1, o).astype(BF16)
        a = send(M_P2R + 2 * o, p2.at[1, o, low], p2in.at[0, o, low], right)
        p2[3, o] = partial2(3, o).astype(BF16)
        return [a, send(M_P2L + 2 * o, p2.at[3, o, top], p2in.at[1, o, top], left)]

    def p2_add(o, relay):
        relay[0].wait_recv()
        p2[1, o, top] = (p2[1, o, top].astype(F32) + p2relay[o, top].astype(F32)).astype(BF16)
        a = send(M_P2R + 2 * o + 1, p2.at[1, o, top], p2in.at[0, o, top], right)
        relay[1].wait_recv()
        p2[3, o, low] = (p2[3, o, low].astype(F32) + p2relay[o, low].astype(F32)).astype(BF16)
        return [a, send(M_P2L + 2 * o + 1, p2.at[3, o, low], p2in.at[1, o, low], left)]

    def sent(i, part):
        make(i, part, part, core).wait_send()

    def finish_sends():
        for cp in done:
            cp.wait_send()
        for s in range(8):
            sent(M_C + s, csend.at[s])
        for d in range(2):
            for t in range(1, 5):
                for u in range(2):
                    if t > 1 and (t < 4 or u == d):
                        for s in range(2):
                            sent(M_ZG + zslot(d, t, u) + s, g.at[0, 0, 0])
                    if t < 4 or u == d:
                        sent(M_GD + 4 * t + 2 * d + u, g.at[0, 0, pl.ds(0, 2)])

    done = list(sends)
    relay2 = p2_relay(1)
    in1 += p1_add(0, relay1)
    in2 = p2_send(1)
    relay1, more = p1_start(1, 1 - iz)
    in1 += more
    relay20 = p2_relay(0)
    in2 += p2_add(1, relay2)
    in20 = p2_send(0)
    ob2[0] = partial2(0, 1)
    ob2[1] = partial2(0, 0)
    in1 += p1_add(1, relay1)
    in20 += p2_add(0, relay20)
    finish_sends()
    for cp in in2:
        cp.wait_recv()
    xs[...] = (ob2[0] + p2in[0, 1].astype(F32) + p2in[1, 1].astype(F32)).astype(BF16)
    x_last = send(M_X, xs, xr, sib)
    ob1[0] = partial1(iz, 0)
    ob1[1] = partial1(1 - iz, 0)
    outs = []

    def put(src, ref, col, i):
        cp = pltpu.make_async_copy(src, ref.at[:, pl.ds(pl.multiple_of(col, 256), 256)], os_.at[i])
        cp.start()
        outs.append(cp)

    for cp in in20:
        cp.wait_recv()
    ob2[1] = ob2[1] + p2in[0, 0].astype(F32) + p2in[1, 0].astype(F32)
    put(ob2.at[1], out2, lo, 0)
    for cp in in1:
        cp.wait_recv()
    for ph, e in enumerate((iz, 1 - iz)):
        ob1[ph] = ob1[ph] + p1in[ph, 0].astype(F32) + p1in[ph, 1].astype(F32)
        put(ob1.at[ph], out1, e * 256, 1 + ph)
    x_last.wait_recv()
    ob2[0] = xr[...].astype(F32)
    put(ob2.at[0], out2, hi, 3)
    for cp in outs:
        cp.wait()
    for cp in sends[len(done) :]:
        cp.wait_send()


def write_kernel(a, b, out1, out2, sem):
    cps = []
    for n, (src, dst) in enumerate(((a, out1), (b, out2))):
        for q in range(2):
            rows = pl.ds(128 * q, 128)
            cps.append(pltpu.make_async_copy(src.at[rows], dst.at[rows], sem.at[2 * n + q]))
    for cp in cps:
        cp.start()
    for cp in cps:
        cp.wait()


def body(first, second):
    v = pltpu.VMEM
    out = jax.ShapeDtypeStruct((256, 512), F32)
    anywhere = pl.BlockSpec(memory_space=pl.ANY)
    parts = pl.pallas_call(
        kernel,
        out_shape=(out, out),
        in_specs=[anywhere, anywhere],
        out_specs=(anywhere, anywhere),
        scratch_shapes=[
            v((16, 256, 256), F32),
            v((16, 256, 256), BF16),
            v((8, 256, 256), BF16),
            v((4, 256, 256), BF16),
            v((16, 4, 256), F32),
            v((2, 4, 4, 256), F32),
            v((4, 8, 4, 256), F32),
            v((8, 4, 256), F32),
            v((8, 4, 4, 256), F32),
            v((7, 4, 4, 256), F32),
            v((8, 4, 256), F32),
            v((2, 256), F32),
            v((256, 256), F32),
            v((256, 256), F32),
            v((8, 512, 256), BF16),
            v((8, 256, 256), F32),
            v((8, 256, 256), F32),
            v((8, 512, 256), BF16),
            v((8, 512, 256), BF16),
            v((8, 256, 256), BF16),
            v((8, 256, 256), BF16),
            v((32, 64, 256), BF16),
            v((32, 64, 256), BF16),
            v((2, 8, 4, 64, 256), BF16),
            v((4, 512, 256), F32),
            v((4, 512, 256), F32),
            v((4, 256, 128), F32),
            v((4, 8, 256), F32),
            v((4, 8, 256), F32),
            v((4, 1, 256), F32),
            v((2, 3, 256, 256), BF16),
            v((2, 2, 256, 256), BF16),
            v((2, 256, 256), BF16),
            v((4, 2, 256, 256), BF16),
            v((2, 2, 256, 256), BF16),
            v((2, 256, 256), BF16),
            v((256, 256), BF16),
            v((256, 256), BF16),
            v((2, 256, 256), F32),
            v((2, 256, 256), F32),
            pltpu.SemaphoreType.DMA((M_ALL,)),
            pltpu.SemaphoreType.DMA((M_ALL,)),
            pltpu.SemaphoreType.DMA((16,)),
            pltpu.SemaphoreType.DMA((4,)),
        ],
        compiler_params=pltpu.CompilerParams(
            collective_id=0, has_side_effects=True, vmem_limit_bytes=51 * 1024 * 1024
        ),
    )(first, second)
    return pl.pallas_call(
        write_kernel,
        out_shape=(out, out),
        in_specs=[pl.BlockSpec(memory_space=pltpu.VMEM)] * 2,
        out_specs=(anywhere, anywhere),
        scratch_shapes=[pltpu.SemaphoreType.DMA((4,))],
        compiler_params=pltpu.CompilerParams(vmem_limit_bytes=8 * 1024 * 1024),
    )(*parts)


def solution(mesh):
    return jax.shard_map(
        body,
        mesh=mesh,
        in_specs=(P("dp", None), P("dp", None)),
        out_specs=(P("dp", "replica"), P("dp", "replica")),
        check_vma=False,
    )
```

```python
import jax
import jax.numpy as jnp
from jax import lax
from jax.experimental import pallas as pl
from jax.experimental.pallas import tpu as pltpu
from jax.sharding import PartitionSpec as P

LAMBDA = 0.0051
EPS = 1e-05
MESH = pl.DeviceIdType.MESH
F32 = jnp.float32
BF16 = jnp.bfloat16
BATCH = 8192

OWN = (0, 1, 4, 5, 2, 3, 6, 7)
STAT_SIB = (0, 1, 8, 9)
STAT_NON = (0, 1, 14, 15)
KB = (2, 3, 6, 7)
AB = (0, 1, 4, 5)

M_Y = 0
M_ST1 = 12
M_ST2 = 17
M_ST3 = 24
M_C = 31
M_YP = 39
M_ZR = 55
M_ZG = 87
M_GD = 119
M_P1 = 139
M_P2O = 151
M_P2R = 155
M_P2L = 159
M_X = 163
M_ALL = 164

HIGH = lax.Precision.HIGHEST


def nt(a, b, precision=None):
    return lax.dot_general(
        a, b, (((1,), (1,)), ((), ())), preferred_element_type=F32, precision=precision
    )


def tn(a, b, precision=None):
    return lax.dot_general(
        a, b, (((0,), (0,)), ((), ())), preferred_element_type=F32, precision=precision
    )


def nn(a, b):
    return lax.dot_general(a, b, (((1,), (0,)), ((), ())), preferred_element_type=F32)


def ab(a):
    return a + 2 * lax.div(a, 2)


def kb(k):
    return k + 2 + 2 * lax.div(k, 2)


def kernel(
    first, second, out1, out2,
    raw, cen, oth, xt, stat, smsg, st1, pst, st2m, st2, fin, dg, scl, fix, nrm, cown, ypart, csend, crecv, ys, yr, zs, zr, g,
    acc1, acc2, rsq, csq, rowsq, colsq,
    p1, p1in, p1relay, p2, p2in, p2relay, xs, xr, ob1, ob2, ss, rs, ls, os_,
):
    dp = lax.axis_index("dp")
    rep = lax.axis_index("replica")
    c = lax.rem(dp, 2)
    ylo = lax.rem(lax.div(dp, 2), 2)
    z = lax.div(dp, 4)
    yhi = lax.div(rep, 4)
    x = lax.rem(rep, 4)

    def dev(x_, yhi_, ylo_, z_, c_):
        return (z_ * 4 + ylo_ * 2 + c_, yhi_ * 4 + x_)

    core = dev(x, yhi, ylo, z, 1 - c)
    sib = dev(x, yhi, 1 - ylo, z, c)
    sibc = dev(x, yhi, 1 - ylo, z, 1 - c)
    non = dev(x, 1 - yhi, 1 - ylo, z, c)
    nonc = dev(x, 1 - yhi, 1 - ylo, z, 1 - c)
    right = dev(lax.rem(x + 1, 4), yhi, ylo, z, c)
    left = dev(lax.rem(x + 3, 4), yhi, ylo, z, c)
    zdev = [dev(x, yhi, ylo, lax.rem(z + q, 8), c) for q in range(8)]
    zto = (zdev[1], zdev[7])

    def load(i, ref, col):
        return pltpu.make_async_copy(
            ref.at[:, pl.ds(pl.multiple_of(col, 256), 256)], raw.at[i], ls.at[i]
        )

    kz = lax.rem(z, 4)
    iz = lax.div(z, 4)
    base = yhi * 2048
    other = 2048 - base
    mine = x * 512
    lo = ylo * 256
    hi = 256 - lo
    def load_first(e):
        for j in range(2):
            load(2 * j + e, first, (base, other)[j] + mine + 256 * e).start()

    def load_second(k):
        piece = lax.rem(x + k, 4) * 512
        for m, col in enumerate((base + lo, base + hi, other + hi)):
            load(4 + 4 * m + k, second, col + piece).start()

    load_first(1 - iz)
    load_second(kz)
    barrier = pltpu.get_barrier_semaphore()
    partners = [core, sib, sibc, non, nonc, right, left] + zdev[1:]
    for d in partners:
        pl.semaphore_signal(barrier, inc=1, device_id=d, device_id_type=MESH)
    load_first(iz)
    for n in (3, 1, 2):
        load_second(lax.rem(kz + n, 4))

    def make(i, src, dst, to):
        return pltpu.make_async_remote_copy(
            src_ref=src, dst_ref=dst, send_sem=ss.at[i], recv_sem=rs.at[i], device_id=to, device_id_type=MESH
        )

    sends = []

    def send(i, src, dst, to):
        cp = make(i, src, dst, to)
        cp.start()
        sends.append(cp)
        return cp

    def local_stats(i, carry):
        pltpu.make_async_copy(first.at[:, pl.ds(0, 256)], raw.at[i], ls.at[i]).wait()
        v = raw[i]
        m = jnp.sum(v, 0, keepdims=True) * (1.0 / 256)
        dv = v - m
        r = dv.astype(BF16)
        cen[i] = r
        stat[i, 0:1, :] = m
        stat[i, 1:2, :] = jnp.sum(dv * dv, 0, keepdims=True)
        stat[i, 2:3, :] = jnp.sum(r.astype(F32), 0, keepdims=True)
        stat[i, 3:4, :] = jnp.zeros_like(m)
        return carry

    top, low = pl.ds(0, 128), pl.ds(128, 128)

    def blocks_k(m, carry):
        return local_stats(4 + 4 * lax.rem(m, 3) + lax.rem(kz + lax.div(m, 3), 4), carry)

    def first_blocks(e):
        def one(j, carry):
            local_stats(2 * j + e, carry)
            xt[2 * j + e] = cen[2 * j + e].T
            return carry

        lax.fori_loop(0, 2, one, 0)

    first_blocks(1 - iz)
    lax.fori_loop(0, 3, blocks_k, 0)
    pl.semaphore_wait(barrier, len(partners))

    def corr(s, carry):
        r = jnp.where(lax.rem(s, 2) == 1, 4 - lax.div(s + 1, 2), 4 + lax.div(s, 2))
        d = lax.rem(z + r, 8)
        i = lax.div(d, 4)
        k = lax.rem(d, 4)
        a = 2 * (1 - c) + i
        b = 2 * c + i
        v = nn(jnp.concatenate([xt[a], xt[b]], 0), cen[4 + k])
        csend[s, 0:256] = v[0:256].astype(BF16)
        cown[s] = v[256:512]
        v = nn(jnp.concatenate([xt[a, top], xt[b, top]], 0), cen[8 + k])
        csend[s, 256:384] = v[0:128].astype(BF16)
        ypart[s, 0:128] = v[128:256]
        v = nn(jnp.concatenate([xt[b, low], xt[a, low]], 0), cen[12 + k])
        csend[s, 384:512] = v[0:128].astype(BF16)
        ypart[s, 128:256] = v[128:256]
        make(M_C + s, csend.at[s], crecv.at[s], core).start()
        return carry

    y_sum = []

    def to_y(s):
        make(M_C + s, csend.at[s], crecv.at[s], core).wait_recv()
        ys[s] = (ypart[s] + crecv[s, 256:512].astype(F32)).astype(BF16)
        y_sum.append(
            (
                send(M_YP + 2 * s, ys.at[s, top], yr.at[s, top], sib),
                send(M_YP + 2 * s + 1, ys.at[s, low], yr.at[s, low], non),
            )
        )

    corr(0, 0)
    first_blocks(iz)
    lax.fori_loop(3, 12, blocks_k, 0)
    def zslot(d, t, u):
        return d * 16 + (t - 1) * 4 + u * 2

    z_in = {}

    def chain(t, far):
        dist = 5 - t
        slot = (7 - 2 * dist, 8 - 2 * dist) if dist < 4 else (0, 0)
        if (t, far) in ((1, True), (2, False), (3, False), (4, False)):
            for n in set(slot):
                for cp in y_sum[n]:
                    cp.wait_recv()
        for s in range(2):
            for d in range(2):
                u = d if far else 1 - d
                n = slot[d]
                rows = slice(128 * u + 64 * s, 128 * u + 64 * s + 64)
                v = cown[n, rows] + crecv[n, rows].astype(F32) + yr[n, rows].astype(F32)
                if (d, t - 1, u, s) in z_in:
                    z_in[(d, t - 1, u, s)].wait_recv()
                    v = v + zr[zslot(d, t - 1, u) + s].astype(F32)
                i = zslot(d, t, u) + s
                zs[i] = v.astype(BF16)
                z_in[(d, t, u, s)] = send(M_ZR + i, zs.at[i], zr.at[i], zto[d])

    to_y(0)
    lax.fori_loop(1, 5, corr, 0)
    to_y(1)
    to_y(2)
    chain(1, True)
    to_y(3)
    to_y(4)

    def comoment(i, j):
        return jnp.sum((raw[i] - stat[i, 0:1, :]) * (raw[j] - stat[j, 0:1, :]), 0, keepdims=True)

    for n in range(4):
        smsg[0, n] = stat[STAT_SIB[n]]
        smsg[1, n] = stat[STAT_NON[n]]
    for b in range(8):
        st1[0, b] = stat[OWN[b]]
    smsg[0, 1 - ylo, 3:4, :] = comoment(1 - ylo, 8)
    st1[0, ylo, 3:4, :] = comoment(ylo, 4)
    st_in = [
        send(M_ST1 + 0, smsg.at[0], st1.at[2, pl.ds(0, 4)], sib),
        send(M_ST1 + 1, smsg.at[1], st1.at[2, pl.ds(4, 4)], non),
        send(M_ST1 + 2, smsg.at[0], st1.at[3, pl.ds(0, 4)], sibc),
        send(M_ST1 + 3, smsg.at[1], st1.at[3, pl.ds(4, 4)], nonc),
        send(M_ST1 + 4, st1.at[0], st1.at[1], core),
    ]
    lax.fori_loop(5, 8, corr, 0)
    chain(2, False)
    to_y(5)
    to_y(6)
    chain(2, True)
    to_y(7)
    for cp in st_in:
        cp.wait_recv()

    def merge(rows, count):
        total = sum(rows[1:], rows[0])
        m = total[0:1] * (1.0 / len(rows))
        dv = [r[0:1] - m for r in rows]
        m2 = total[1:2] + count * sum([d * d for d in dv[1:]], dv[0] * dv[0])
        return m, m2, total[2:3], total[3:4], dv

    def cross(p, q):
        return sum([a * b for a, b in zip(p[1:], q[1:])], p[0] * q[0])

    merged = [merge([st1[s, b] for s in range(4)], 256.0) for b in range(8)]
    for b, (m, m2, r, co, dv) in enumerate(merged):
        if b < 2:
            co = co + 256.0 * cross(dv, merged[2][4])
        for n, row in enumerate((m, m2, r, co)):
            pst[b, n : n + 1, :] = row
    st2_in = []
    for q in range(8):
        zq = lax.rem(z + q, 8)
        fa = ab(2 * c + lax.div(zq, 4))
        fk = kb(lax.rem(zq, 4))
        st2m[q, 0] = pst[zq]
        st2m[q, 3] = pst[2]
        for s in range(4):
            st2m[q, 1, s : s + 1, :] = st1[s, fa, 0:1, :]
            st2m[q, 2, s : s + 1, :] = st1[s, fk, 0:1, :]
        if q:
            st2_in.append(send(M_ST2 + q - 1, st2m.at[q], st2.at[q - 1], zdev[q]))

    x_in = [
        send(M_Y + 0, cen.at[8, top], oth.at[2, top], sib),
        send(M_Y + 1, cen.at[12, low], oth.at[2, low], non),
        send(M_Y + 2, cen.at[0], oth.at[0], sib),
        send(M_Y + 3, cen.at[0], oth.at[4], non),
        send(M_Y + 4, cen.at[1], oth.at[1], sib),
        send(M_Y + 5, cen.at[1], oth.at[5], non),
    ]

    def zero(n, carry):
        acc1[n] = jnp.zeros((512, 256), F32)
        acc2[n] = jnp.zeros((512, 256), F32)
        return carry

    lax.fori_loop(0, 4, zero, 0)
    rsq[...] = jnp.zeros_like(rsq)
    csq[...] = jnp.zeros_like(csq)
    chain(3, False)

    for cp in st2_in:
        cp.wait_recv()
    st2m_all = [st2m[0, 0]] + [st2[s, 0] for s in range(7)]
    k0_means = [st2m[0, 3]] + [st2[s, 3] for s in range(7)]
    m, m2, r, co, dv = merge(st2m_all, 1024.0)
    k0_dv = merge(k0_means, 1024.0)[4]
    fin[z, 0:1, :] = m + r * (1.0 / BATCH)
    fin[z, 1:2, :] = lax.rsqrt(m2 * (1.0 / BATCH) + EPS)
    fin[z, 2:3, :] = m
    fin[z, 3:4, :] = co + 1024.0 * cross(dv, k0_dv)
    fin_in = [send(M_ST3 + q - 1, fin.at[z], fin.at[z], zdev[q]) for q in range(1, 8)]

    chain(3, True)
    x_in[0].wait_recv()
    x_in[1].wait_recv()
    x_ring = [
        send(M_Y + 6, oth.at[2], oth.at[3], left),
        send(M_Y + 7, oth.at[2], oth.at[7], right),
    ]

    def norm(b, o):
        shift = st1[2 * o, b, 0:1, :] - fin[b, 0:1, :]
        scale = fin[b, 1:2, :]
        q = lax.rem(b, 4)
        idx = jnp.where(q < 2, 0, 2) + q + 2 * lax.div(b, 4)
        for h in range(2):
            rows = slice(128 * h, 128 * h + 128)
            v = cen[idx, rows] if o == 0 else oth[b, rows]
            nrm[b, o * 256 + 128 * h : o * 256 + 128 * h + 128, :] = ((v.astype(F32) + shift) * scale).astype(BF16)

    def norms(o):
        lax.fori_loop(0, 8, lambda b, carry: (norm(b, o), carry)[1], 0)

    chain(4, False)
    for cp in fin_in:
        cp.wait_recv()
    cii = fin[ylo, 3:4, :] * fin[ylo, 1:2, :] * fin[2, 1:2, :] * (1.0 / BATCH)
    dg[0:1, :] = cii
    dg[1:2, :] = (-2.0 * (1.0 - cii)).astype(BF16).astype(F32)
    norms(0)
    chain(4, True)
    x_ring[0].wait_recv()
    x_ring.append(send(M_Y + 8, oth.at[3, top], oth.at[6, top], left))
    x_ring[1].wait_recv()
    x_ring.append(send(M_Y + 9, oth.at[7, low], oth.at[6, low], right))

    fa = ab(2 * c + lax.div(z, 4))
    fk = kb(lax.rem(z, 4))
    pad = jnp.zeros((7, 256), F32)
    ra = jnp.concatenate([fin[fa, 1:2, :] * (2.0 * LAMBDA / BATCH), pad], 0)
    rk = jnp.concatenate([fin[fk, 1:2, :], pad], 0)
    rows_id = lax.broadcasted_iota(jnp.int32, (256, 256), 0)
    cols_id = lax.broadcasted_iota(jnp.int32, (256, 256), 1)
    off = rows_id + jnp.where((c == 0) & (z == 4 * ylo), 0, 512) != cols_id
    scl[...] = jnp.where(off, tn(ra, rk, HIGH), 0.0)
    mu_a = [(st2m[0, 1] if s == 0 else st2[s - 1, 1]) - fin[fa, 2:3, :] for s in range(8)]
    mu_k = [(st2m[0, 2] if s == 0 else st2[s - 1, 2]) - fin[fk, 2:3, :] for s in range(8)]
    fix[...] = scl[...] * tn(jnp.concatenate(mu_a, 0) * 256.0, jnp.concatenate(mu_k, 0), HIGH)

    for cp in y_sum[7]:
        cp.wait_recv()
    for s in range(2):
        for u in range(2):
            q = 2 * u + s
            rows = slice(64 * q, 64 * q + 64)
            v = cown[7, rows] + crecv[7, rows].astype(F32) + yr[7, rows].astype(F32)
            for d in (1 - u, u):
                z_in[(d, 4, u, s)].wait_recv()
                v = v + zr[zslot(d, 4, u) + s].astype(F32)
            part = g.at[c, z, q]
            g[c, z, q] = (v * scl[rows] + fix[rows]).astype(BF16)
            for d in (u, 1 - u):
                send(M_ZG + zslot(d, 1, u) + s, part, part, zto[d])
    send(M_GD + 0, g.at[c, z, pl.ds(0, 2)], g.at[c, z, pl.ds(0, 2)], core)
    send(M_GD + 1, g.at[c, z, pl.ds(2, 2)], g.at[c, z, pl.ds(2, 2)], core)

    def arrive(t, far, onward):
        for s in range(2):
            for d in range(2):
                u = d if far else 1 - d
                i = d * 16 + (t - 1) * 4 + u * 2 + s
                source = lax.rem(z + (8 - t if d == 0 else t), 8)
                part = g.at[c, source, 2 * u + s]
                make(M_ZG + i, part, part, zto[d]).wait_recv()
                if onward is not None:
                    start = make(M_ZG + i + 4, part, part, zto[d]).start
                    if onward is True:
                        start()
                    else:
                        pl.when(onward)(start)
                if s == 1:
                    both = g.at[c, source, pl.ds(2 * u, 2)]
                    make(M_GD + 4 * t + 2 * d + u, both, both, core).start()

    def use(j, zs_):
        a = 2 * j + lax.div(zs_, 4)
        k = lax.rem(zs_, 4)
        ga = g[j, zs_].reshape(256, 256)
        acc1[a] += nt(nrm[kb(k)], ga)
        acc2[k] += nn(nrm[ab(a)], ga)
        v = ga.astype(F32)
        s = v * v
        rsq[a] += s[:, 0:128] + s[:, 128:256]
        csq[k] += jnp.sum(s.reshape(32, 8, 256), 0)

    def from_core(t, d, u):
        part = g.at[0, 0, pl.ds(0, 2)]
        make(M_GD + 4 * t + 2 * d + u, part, part, core).wait_recv()

    def uses(t, mine_too):
        def one(n, inner):
            if not mine_too:
                for u in range(2):
                    from_core(t, n, u)
            use(c if mine_too else 1 - c, lax.rem(z + (8 - t) + n * 2 * t, 8))
            return inner

        lax.fori_loop(0, jnp.where(t == 0, 1, 2), one, 0)

    for cp in x_in[2:] + x_ring[2:]:
        cp.wait_recv()
    norms(1)
    uses(0, True)

    def step(t, carry):
        arrive(t, True, True)
        uses(t - 1, False)
        arrive(t, False, t < 3)
        uses(t, True)
        return carry

    def partial1(a, o):
        b = ab(a)
        rows = slice(o * 256, o * 256 + 256)
        f = nrm[b, rows].astype(F32)
        v = acc1[a, rows] - f * rowsq[a, 0:1, :]
        gd = jnp.where(a == ylo, dg[1:2, :], 0.0)
        v = v + (nrm[2, rows].astype(F32) - f * dg[0:1, :]) * gd
        return v * fin[b, 1:2, :]

    def p1_start(ph, e):
        for a in (e, 2 + e):
            rowsq[a] = nt(jnp.ones((8, 128), F32), rsq[a], HIGH) * (0.5 / LAMBDA)
        m = M_P1 + 6 * ph
        p1[ph, 0] = partial1(2 + e, 0).astype(BF16)
        relay = [
            send(m, p1.at[ph, 0, top], p1relay.at[ph, top], sib),
            send(m + 1, p1.at[ph, 0, low], p1relay.at[ph, low], non),
        ]
        p1[ph, 1] = partial1(2 + e, 1).astype(BF16)
        a = send(m + 2, p1.at[ph, 1, low], p1in.at[ph, 1, low], non)
        p1[ph, 2] = partial1(e, 1).astype(BF16)
        b = send(m + 3, p1.at[ph, 2, top], p1in.at[ph, 0, top], sib)
        return relay, [a, b]

    def p1_add(ph, relay):
        m = M_P1 + 6 * ph
        relay[0].wait_recv()
        p1[ph, 1, top] = (p1[ph, 1, top].astype(F32) + p1relay[ph, top].astype(F32)).astype(BF16)
        a = send(m + 4, p1.at[ph, 1, top], p1in.at[ph, 1, top], non)
        relay[1].wait_recv()
        p1[ph, 2, low] = (p1[ph, 2, low].astype(F32) + p1relay[ph, low].astype(F32)).astype(BF16)
        return [a, send(m + 5, p1.at[ph, 2, low], p1in.at[ph, 0, low], sib)]

    lax.fori_loop(1, 4, step, 0)
    uses(3, False)
    relay1, in1 = p1_start(0, iz)
    arrive(4, True, None)

    def final_two(n, carry):
        use(lax.rem(c + n, 2), lax.rem(z + 4, 8))
        return carry

    lax.fori_loop(0, 1, final_two, 0)
    from_core(4, 0, 0)
    from_core(4, 1, 1)
    lax.fori_loop(1, 2, final_two, 0)

    for k in range(4):
        colsq[k] = jnp.sum(csq[k], 0, keepdims=True) * (0.5 / LAMBDA)

    def partial2(k, o):
        b = KB[k]
        rows = slice(o * 256, o * 256 + 256)
        s = nrm[b, rows].astype(F32)
        v = acc2[k, rows] - s * colsq[k]
        if k == 0:
            v = v + (nrm[ylo, rows].astype(F32) - s * dg[0:1, :]) * dg[1:2, :]
        return v * fin[b, 1:2, :]

    def p2_relay(o):
        p2[2, o] = partial2(2, o).astype(BF16)
        return [
            send(M_P2O + 2 * o, p2.at[2, o, top], p2relay.at[o, top], right),
            send(M_P2O + 2 * o + 1, p2.at[2, o, low], p2relay.at[o, low], left),
        ]

    def p2_send(o):
        p2[1, o] = partial2(1, o).astype(BF16)
        a = send(M_P2R + 2 * o, p2.at[1, o, low], p2in.at[0, o, low], right)
        p2[3, o] = partial2(3, o).astype(BF16)
        return [a, send(M_P2L + 2 * o, p2.at[3, o, top], p2in.at[1, o, top], left)]

    def p2_add(o, relay):
        relay[0].wait_recv()
        p2[1, o, top] = (p2[1, o, top].astype(F32) + p2relay[o, top].astype(F32)).astype(BF16)
        a = send(M_P2R + 2 * o + 1, p2.at[1, o, top], p2in.at[0, o, top], right)
        relay[1].wait_recv()
        p2[3, o, low] = (p2[3, o, low].astype(F32) + p2relay[o, low].astype(F32)).astype(BF16)
        return [a, send(M_P2L + 2 * o + 1, p2.at[3, o, low], p2in.at[1, o, low], left)]

    def sent(i, part):
        make(i, part, part, core).wait_send()

    def finish_sends():
        for cp in done:
            cp.wait_send()
        for s in range(8):
            sent(M_C + s, csend.at[s])
        for d in range(2):
            for t in range(1, 5):
                for u in range(2):
                    if t > 1 and (t < 4 or u == d):
                        for s in range(2):
                            sent(M_ZG + zslot(d, t, u) + s, g.at[0, 0, 0])
                    if t < 4 or u == d:
                        sent(M_GD + 4 * t + 2 * d + u, g.at[0, 0, pl.ds(0, 2)])

    done = list(sends)
    relay2 = p2_relay(1)
    in1 += p1_add(0, relay1)
    in2 = p2_send(1)
    relay1, more = p1_start(1, 1 - iz)
    in1 += more
    relay20 = p2_relay(0)
    in2 += p2_add(1, relay2)
    in20 = p2_send(0)
    ob2[0] = partial2(0, 1)
    ob2[1] = partial2(0, 0)
    in1 += p1_add(1, relay1)
    in20 += p2_add(0, relay20)
    finish_sends()
    for cp in in2:
        cp.wait_recv()
    xs[...] = (ob2[0] + p2in[0, 1].astype(F32) + p2in[1, 1].astype(F32)).astype(BF16)
    x_last = send(M_X, xs, xr, sib)
    ob1[0] = partial1(iz, 0)
    ob1[1] = partial1(1 - iz, 0)
    outs = []

    def put(src, ref, col, i):
        cp = pltpu.make_async_copy(src, ref.at[:, pl.ds(pl.multiple_of(col, 256), 256)], os_.at[i])
        cp.start()
        outs.append(cp)

    for cp in in20:
        cp.wait_recv()
    ob2[1] = ob2[1] + p2in[0, 0].astype(F32) + p2in[1, 0].astype(F32)
    put(ob2.at[1], out2, lo, 0)
    for cp in in1:
        cp.wait_recv()
    for ph, e in enumerate((iz, 1 - iz)):
        ob1[ph] = ob1[ph] + p1in[ph, 0].astype(F32) + p1in[ph, 1].astype(F32)
        put(ob1.at[ph], out1, e * 256, 1 + ph)
    x_last.wait_recv()
    ob2[0] = xr[...].astype(F32)
    put(ob2.at[0], out2, hi, 3)
    for cp in outs:
        cp.wait()
    for cp in sends[len(done) :]:
        cp.wait_send()


def write_kernel(a, b, out1, out2, sem):
    cps = []
    for n, (src, dst) in enumerate(((a, out1), (b, out2))):
        for q in range(2):
            rows = pl.ds(128 * q, 128)
            cps.append(pltpu.make_async_copy(src.at[rows], dst.at[rows], sem.at[2 * n + q]))
    for cp in cps:
        cp.start()
    for cp in cps:
        cp.wait()


def body(first, second):
    v = pltpu.VMEM
    out = jax.ShapeDtypeStruct((256, 512), F32)
    anywhere = pl.BlockSpec(memory_space=pl.ANY)
    parts = pl.pallas_call(
        kernel,
        out_shape=(out, out),
        in_specs=[anywhere, anywhere],
        out_specs=(anywhere, anywhere),
        scratch_shapes=[
            v((16, 256, 256), F32),
            v((16, 256, 256), BF16),
            v((8, 256, 256), BF16),
            v((4, 256, 256), BF16),
            v((16, 4, 256), F32),
            v((2, 4, 4, 256), F32),
            v((4, 8, 4, 256), F32),
            v((8, 4, 256), F32),
            v((8, 4, 4, 256), F32),
            v((7, 4, 4, 256), F32),
            v((8, 4, 256), F32),
            v((2, 256), F32),
            v((256, 256), F32),
            v((256, 256), F32),
            v((8, 512, 256), BF16),
            v((8, 256, 256), F32),
            v((8, 256, 256), F32),
            v((8, 512, 256), BF16),
            v((8, 512, 256), BF16),
            v((8, 256, 256), BF16),
            v((8, 256, 256), BF16),
            v((32, 64, 256), BF16),
            v((32, 64, 256), BF16),
            v((2, 8, 4, 64, 256), BF16),
            v((4, 512, 256), F32),
            v((4, 512, 256), F32),
            v((4, 256, 128), F32),
            v((4, 8, 256), F32),
            v((4, 8, 256), F32),
            v((4, 1, 256), F32),
            v((2, 3, 256, 256), BF16),
            v((2, 2, 256, 256), BF16),
            v((2, 256, 256), BF16),
            v((4, 2, 256, 256), BF16),
            v((2, 2, 256, 256), BF16),
            v((2, 256, 256), BF16),
            v((256, 256), BF16),
            v((256, 256), BF16),
            v((2, 256, 256), F32),
            v((2, 256, 256), F32),
            pltpu.SemaphoreType.DMA((M_ALL,)),
            pltpu.SemaphoreType.DMA((M_ALL,)),
            pltpu.SemaphoreType.DMA((16,)),
            pltpu.SemaphoreType.DMA((4,)),
        ],
        compiler_params=pltpu.CompilerParams(
            collective_id=0, has_side_effects=True, vmem_limit_bytes=51 * 1024 * 1024
        ),
    )(first, second)
    return pl.pallas_call(
        write_kernel,
        out_shape=(out, out),
        in_specs=[pl.BlockSpec(memory_space=pltpu.VMEM)] * 2,
        out_specs=(anywhere, anywhere),
        scratch_shapes=[pltpu.SemaphoreType.DMA((4,))],
        compiler_params=pltpu.CompilerParams(vmem_limit_bytes=8 * 1024 * 1024),
    )(*parts)


def solution(mesh):
    return jax.shard_map(
        body,
        mesh=mesh,
        in_specs=(P("dp", None), P("dp", None)),
        out_specs=(P("dp", "replica"), P("dp", "replica")),
        check_vma=False,
    )
```

```python
import jax
import jax.numpy as jnp
from jax import lax
from jax.experimental import pallas as pl
from jax.experimental.pallas import tpu as pltpu
from jax.sharding import PartitionSpec as P

LAMBDA = 0.0051
EPS = 1e-05
MESH = pl.DeviceIdType.MESH
F32 = jnp.float32
BF16 = jnp.bfloat16
BATCH = 8192

OWN = (0, 1, 4, 5, 2, 3, 6, 7)
STAT_SIB = (0, 1, 8, 9)
STAT_NON = (0, 1, 14, 15)
KB = (2, 3, 6, 7)
AB = (0, 1, 4, 5)

M_Y = 0
M_ST1 = 12
M_ST2 = 17
M_ST3 = 24
M_C = 31
M_YP = 39
M_ZR = 55
M_ZG = 87
M_GD = 119
M_P1 = 139
M_P2O = 151
M_P2R = 155
M_P2L = 159
M_X = 163
M_ALL = 164

HIGH = lax.Precision.HIGHEST


def nt(a, b, precision=None):
    return lax.dot_general(
        a, b, (((1,), (1,)), ((), ())), preferred_element_type=F32, precision=precision
    )


def tn(a, b, precision=None):
    return lax.dot_general(
        a, b, (((0,), (0,)), ((), ())), preferred_element_type=F32, precision=precision
    )


def nn(a, b):
    return lax.dot_general(a, b, (((1,), (0,)), ((), ())), preferred_element_type=F32)


def ab(a):
    return a + 2 * lax.div(a, 2)


def kb(k):
    return k + 2 + 2 * lax.div(k, 2)


def kernel(
    first, second, out1, out2,
    raw, cen, oth, xt, stat, smsg, st1, pst, st2m, st2, fin, dg, scl, fix, nrm, cown, ypart, csend, crecv, ys, yr, zs, zr, g,
    acc1, acc2, rsq, csq, rowsq, colsq,
    p1, p1in, p1relay, p2, p2in, p2relay, xs, xr, ob1, ob2, ss, rs, ls, os_,
):
    dp = lax.axis_index("dp")
    rep = lax.axis_index("replica")
    c = lax.rem(dp, 2)
    ylo = lax.rem(lax.div(dp, 2), 2)
    z = lax.div(dp, 4)
    yhi = lax.div(rep, 4)
    x = lax.rem(rep, 4)

    def dev(x_, yhi_, ylo_, z_, c_):
        return (z_ * 4 + ylo_ * 2 + c_, yhi_ * 4 + x_)

    core = dev(x, yhi, ylo, z, 1 - c)
    sib = dev(x, yhi, 1 - ylo, z, c)
    sibc = dev(x, yhi, 1 - ylo, z, 1 - c)
    non = dev(x, 1 - yhi, 1 - ylo, z, c)
    nonc = dev(x, 1 - yhi, 1 - ylo, z, 1 - c)
    right = dev(lax.rem(x + 1, 4), yhi, ylo, z, c)
    left = dev(lax.rem(x + 3, 4), yhi, ylo, z, c)
    zdev = [dev(x, yhi, ylo, lax.rem(z + q, 8), c) for q in range(8)]
    zto = (zdev[1], zdev[7])

    def load(i, ref, col):
        return pltpu.make_async_copy(
            ref.at[:, pl.ds(pl.multiple_of(col, 256), 256)], raw.at[i], ls.at[i]
        )

    kz = lax.rem(z, 4)
    iz = lax.div(z, 4)
    base = yhi * 2048
    other = 2048 - base
    mine = x * 512
    lo = ylo * 256
    hi = 256 - lo
    def load_first(e):
        for j in range(2):
            load(2 * j + e, first, (base, other)[j] + mine + 256 * e).start()

    def load_second(k):
        piece = lax.rem(x + k, 4) * 512
        for m, col in enumerate((base + lo, base + hi, other + hi)):
            load(4 + 4 * m + k, second, col + piece).start()

    load_first(1 - iz)
    load_second(kz)
    barrier = pltpu.get_barrier_semaphore()
    partners = [core, sib, sibc, non, nonc, right, left] + zdev[1:]
    for d in partners:
        pl.semaphore_signal(barrier, inc=1, device_id=d, device_id_type=MESH)
    load_first(iz)
    for n in (3, 1, 2):
        load_second(lax.rem(kz + n, 4))

    def make(i, src, dst, to):
        return pltpu.make_async_remote_copy(
            src_ref=src, dst_ref=dst, send_sem=ss.at[i], recv_sem=rs.at[i], device_id=to, device_id_type=MESH
        )

    sends = []

    def send(i, src, dst, to):
        cp = make(i, src, dst, to)
        cp.start()
        sends.append(cp)
        return cp

    def local_stats(i, carry):
        pltpu.make_async_copy(first.at[:, pl.ds(0, 256)], raw.at[i], ls.at[i]).wait()
        v = raw[i]
        m = jnp.sum(v, 0, keepdims=True) * (1.0 / 256)
        dv = v - m
        r = dv.astype(BF16)
        cen[i] = r
        stat[i, 0:1, :] = m
        stat[i, 1:2, :] = jnp.sum(dv * dv, 0, keepdims=True)
        stat[i, 2:3, :] = jnp.sum(r.astype(F32), 0, keepdims=True)
        stat[i, 3:4, :] = jnp.zeros_like(m)
        return carry

    top, low = pl.ds(0, 128), pl.ds(128, 128)

    def blocks_k(m, carry):
        return local_stats(4 + 4 * lax.rem(m, 3) + lax.rem(kz + lax.div(m, 3), 4), carry)

    def first_blocks(e):
        def one(j, carry):
            local_stats(2 * j + e, carry)
            xt[2 * j + e] = cen[2 * j + e].T
            return carry

        lax.fori_loop(0, 2, one, 0)

    first_blocks(1 - iz)
    lax.fori_loop(0, 3, blocks_k, 0)
    pl.semaphore_wait(barrier, len(partners))

    def corr(s, carry):
        r = jnp.where(lax.rem(s, 2) == 1, 4 - lax.div(s + 1, 2), 4 + lax.div(s, 2))
        d = lax.rem(z + r, 8)
        i = lax.div(d, 4)
        k = lax.rem(d, 4)
        a = 2 * (1 - c) + i
        b = 2 * c + i
        v = nn(jnp.concatenate([xt[a], xt[b]], 0), cen[4 + k])
        csend[s, 0:256] = v[0:256].astype(BF16)
        cown[s] = v[256:512]
        v = nn(jnp.concatenate([xt[a, top], xt[b, top]], 0), cen[8 + k])
        csend[s, 256:384] = v[0:128].astype(BF16)
        ypart[s, 0:128] = v[128:256]
        v = nn(jnp.concatenate([xt[b, low], xt[a, low]], 0), cen[12 + k])
        csend[s, 384:512] = v[0:128].astype(BF16)
        ypart[s, 128:256] = v[128:256]
        make(M_C + s, csend.at[s], crecv.at[s], core).start()
        return carry

    y_sum = []

    def to_y(s):
        make(M_C + s, csend.at[s], crecv.at[s], core).wait_recv()
        ys[s] = (ypart[s] + crecv[s, 256:512].astype(F32)).astype(BF16)
        y_sum.append(
            (
                send(M_YP + 2 * s, ys.at[s, top], yr.at[s, top], sib),
                send(M_YP + 2 * s + 1, ys.at[s, low], yr.at[s, low], non),
            )
        )

    corr(0, 0)
    first_blocks(iz)
    lax.fori_loop(3, 12, blocks_k, 0)
    def zslot(d, t, u):
        return d * 16 + (t - 1) * 4 + u * 2

    z_in = {}

    def chain(t, far):
        dist = 5 - t
        slot = (7 - 2 * dist, 8 - 2 * dist) if dist < 4 else (0, 0)
        if (t, far) in ((1, True), (2, False), (3, False), (4, False)):
            for n in set(slot):
                for cp in y_sum[n]:
                    cp.wait_recv()
        for s in range(2):
            for d in range(2):
                u = d if far else 1 - d
                n = slot[d]
                rows = slice(128 * u + 64 * s, 128 * u + 64 * s + 64)
                v = cown[n, rows] + crecv[n, rows].astype(F32) + yr[n, rows].astype(F32)
                if (d, t - 1, u, s) in z_in:
                    z_in[(d, t - 1, u, s)].wait_recv()
                    v = v + zr[zslot(d, t - 1, u) + s].astype(F32)
                i = zslot(d, t, u) + s
                zs[i] = v.astype(BF16)
                z_in[(d, t, u, s)] = send(M_ZR + i, zs.at[i], zr.at[i], zto[d])

    def comoment(i, j):
        return jnp.sum((raw[i] - stat[i, 0:1, :]) * (raw[j] - stat[j, 0:1, :]), 0, keepdims=True)

    for n in range(4):
        smsg[0, n] = stat[STAT_SIB[n]]
        smsg[1, n] = stat[STAT_NON[n]]
    for b in range(8):
        st1[0, b] = stat[OWN[b]]
    smsg[0, 1 - ylo, 3:4, :] = comoment(1 - ylo, 8)
    st1[0, ylo, 3:4, :] = comoment(ylo, 4)
    st_in = [
        send(M_ST1 + 0, smsg.at[0], st1.at[2, pl.ds(0, 4)], sib),
        send(M_ST1 + 1, smsg.at[1], st1.at[2, pl.ds(4, 4)], non),
        send(M_ST1 + 2, smsg.at[0], st1.at[3, pl.ds(0, 4)], sibc),
        send(M_ST1 + 3, smsg.at[1], st1.at[3, pl.ds(4, 4)], nonc),
        send(M_ST1 + 4, st1.at[0], st1.at[1], core),
    ]
    to_y(0)
    lax.fori_loop(1, 5, corr, 0)
    to_y(1)
    to_y(2)
    for cp in st_in:
        cp.wait_recv()

    def merge(rows, count):
        total = sum(rows[1:], rows[0])
        m = total[0:1] * (1.0 / len(rows))
        dv = [r[0:1] - m for r in rows]
        m2 = total[1:2] + count * sum([d * d for d in dv[1:]], dv[0] * dv[0])
        return m, m2, total[2:3], total[3:4], dv

    def cross(p, q):
        return sum([a * b for a, b in zip(p[1:], q[1:])], p[0] * q[0])

    merged = [merge([st1[s, b] for s in range(4)], 256.0) for b in range(8)]
    for b, (m, m2, r, co, dv) in enumerate(merged):
        if b < 2:
            co = co + 256.0 * cross(dv, merged[2][4])
        for n, row in enumerate((m, m2, r, co)):
            pst[b, n : n + 1, :] = row
    st2_in = []
    for q in range(8):
        zq = lax.rem(z + q, 8)
        fa = ab(2 * c + lax.div(zq, 4))
        fk = kb(lax.rem(zq, 4))
        st2m[q, 0] = pst[zq]
        st2m[q, 3] = pst[2]
        for s in range(4):
            st2m[q, 1, s : s + 1, :] = st1[s, fa, 0:1, :]
            st2m[q, 2, s : s + 1, :] = st1[s, fk, 0:1, :]
        if q:
            st2_in.append(send(M_ST2 + q - 1, st2m.at[q], st2.at[q - 1], zdev[q]))

    to_y(3)
    to_y(4)
    chain(1, True)

    lax.fori_loop(5, 8, corr, 0)
    for cp in st2_in:
        cp.wait_recv()
    st2m_all = [st2m[0, 0]] + [st2[s, 0] for s in range(7)]
    k0_means = [st2m[0, 3]] + [st2[s, 3] for s in range(7)]
    m, m2, r, co, dv = merge(st2m_all, 1024.0)
    k0_dv = merge(k0_means, 1024.0)[4]
    fin[z, 0:1, :] = m + r * (1.0 / BATCH)
    fin[z, 1:2, :] = lax.rsqrt(m2 * (1.0 / BATCH) + EPS)
    fin[z, 2:3, :] = m
    fin[z, 3:4, :] = co + 1024.0 * cross(dv, k0_dv)
    fin_in = [send(M_ST3 + q - 1, fin.at[z], fin.at[z], zdev[q]) for q in range(1, 8)]

    to_y(5)
    to_y(6)
    to_y(7)
    chain(2, False)
    x_in = [
        send(M_Y + 0, cen.at[8, top], oth.at[2, top], sib),
        send(M_Y + 1, cen.at[12, low], oth.at[2, low], non),
        send(M_Y + 2, cen.at[0], oth.at[0], sib),
        send(M_Y + 3, cen.at[0], oth.at[4], non),
        send(M_Y + 4, cen.at[1], oth.at[1], sib),
        send(M_Y + 5, cen.at[1], oth.at[5], non),
    ]
    chain(2, True)

    def zero(n, carry):
        acc1[n] = jnp.zeros((512, 256), F32)
        acc2[n] = jnp.zeros((512, 256), F32)
        return carry

    lax.fori_loop(0, 4, zero, 0)
    rsq[...] = jnp.zeros_like(rsq)
    csq[...] = jnp.zeros_like(csq)
    chain(3, False)

    chain(3, True)
    x_in[0].wait_recv()
    x_in[1].wait_recv()
    x_ring = [
        send(M_Y + 6, oth.at[2], oth.at[3], left),
        send(M_Y + 7, oth.at[2], oth.at[7], right),
    ]

    def norm(b, o):
        shift = st1[2 * o, b, 0:1, :] - fin[b, 0:1, :]
        scale = fin[b, 1:2, :]
        q = lax.rem(b, 4)
        idx = jnp.where(q < 2, 0, 2) + q + 2 * lax.div(b, 4)
        for h in range(2):
            rows = slice(128 * h, 128 * h + 128)
            v = cen[idx, rows] if o == 0 else oth[b, rows]
            nrm[b, o * 256 + 128 * h : o * 256 + 128 * h + 128, :] = ((v.astype(F32) + shift) * scale).astype(BF16)

    def norms(o):
        lax.fori_loop(0, 8, lambda b, carry: (norm(b, o), carry)[1], 0)

    chain(4, False)
    for cp in fin_in:
        cp.wait_recv()
    cii = fin[ylo, 3:4, :] * fin[ylo, 1:2, :] * fin[2, 1:2, :] * (1.0 / BATCH)
    dg[0:1, :] = cii
    dg[1:2, :] = (-2.0 * (1.0 - cii)).astype(BF16).astype(F32)
    norms(0)
    chain(4, True)
    x_ring[0].wait_recv()
    x_ring.append(send(M_Y + 8, oth.at[3, top], oth.at[6, top], left))
    x_ring[1].wait_recv()
    x_ring.append(send(M_Y + 9, oth.at[7, low], oth.at[6, low], right))

    fa = ab(2 * c + lax.div(z, 4))
    fk = kb(lax.rem(z, 4))
    pad = jnp.zeros((7, 256), F32)
    ra = jnp.concatenate([fin[fa, 1:2, :] * (2.0 * LAMBDA / BATCH), pad], 0)
    rk = jnp.concatenate([fin[fk, 1:2, :], pad], 0)
    rows_id = lax.broadcasted_iota(jnp.int32, (256, 256), 0)
    cols_id = lax.broadcasted_iota(jnp.int32, (256, 256), 1)
    off = rows_id + jnp.where((c == 0) & (z == 4 * ylo), 0, 512) != cols_id
    scl[...] = jnp.where(off, tn(ra, rk, HIGH), 0.0)
    mu_a = [(st2m[0, 1] if s == 0 else st2[s - 1, 1]) - fin[fa, 2:3, :] for s in range(8)]
    mu_k = [(st2m[0, 2] if s == 0 else st2[s - 1, 2]) - fin[fk, 2:3, :] for s in range(8)]
    fix[...] = scl[...] * tn(jnp.concatenate(mu_a, 0) * 256.0, jnp.concatenate(mu_k, 0), HIGH)

    for cp in y_sum[7]:
        cp.wait_recv()
    for s in range(2):
        for u in range(2):
            q = 2 * u + s
            rows = slice(64 * q, 64 * q + 64)
            v = cown[7, rows] + crecv[7, rows].astype(F32) + yr[7, rows].astype(F32)
            for d in (1 - u, u):
                z_in[(d, 4, u, s)].wait_recv()
                v = v + zr[zslot(d, 4, u) + s].astype(F32)
            part = g.at[c, z, q]
            g[c, z, q] = (v * scl[rows] + fix[rows]).astype(BF16)
            for d in (u, 1 - u):
                send(M_ZG + zslot(d, 1, u) + s, part, part, zto[d])
    send(M_GD + 0, g.at[c, z, pl.ds(0, 2)], g.at[c, z, pl.ds(0, 2)], core)
    send(M_GD + 1, g.at[c, z, pl.ds(2, 2)], g.at[c, z, pl.ds(2, 2)], core)

    def arrive(t, far, onward):
        for s in range(2):
            for d in range(2):
                u = d if far else 1 - d
                i = d * 16 + (t - 1) * 4 + u * 2 + s
                source = lax.rem(z + (8 - t if d == 0 else t), 8)
                part = g.at[c, source, 2 * u + s]
                make(M_ZG + i, part, part, zto[d]).wait_recv()
                if onward is not None:
                    start = make(M_ZG + i + 4, part, part, zto[d]).start
                    if onward is True:
                        start()
                    else:
                        pl.when(onward)(start)
                if s == 1:
                    both = g.at[c, source, pl.ds(2 * u, 2)]
                    make(M_GD + 4 * t + 2 * d + u, both, both, core).start()

    def use(j, zs_):
        a = 2 * j + lax.div(zs_, 4)
        k = lax.rem(zs_, 4)
        ga = g[j, zs_].reshape(256, 256)
        acc1[a] += nt(nrm[kb(k)], ga)
        acc2[k] += nn(nrm[ab(a)], ga)
        v = ga.astype(F32)
        s = v * v
        rsq[a] += s[:, 0:128] + s[:, 128:256]
        csq[k] += jnp.sum(s.reshape(32, 8, 256), 0)

    def from_core(t, d, u):
        part = g.at[0, 0, pl.ds(0, 2)]
        make(M_GD + 4 * t + 2 * d + u, part, part, core).wait_recv()

    def uses(t, mine_too):
        def one(n, inner):
            if not mine_too:
                for u in range(2):
                    from_core(t, n, u)
            use(c if mine_too else 1 - c, lax.rem(z + (8 - t) + n * 2 * t, 8))
            return inner

        lax.fori_loop(0, jnp.where(t == 0, 1, 2), one, 0)

    for cp in x_in[2:] + x_ring[2:]:
        cp.wait_recv()
    norms(1)
    uses(0, True)

    def step(t, carry):
        arrive(t, True, True)
        uses(t - 1, False)
        arrive(t, False, t < 3)
        uses(t, True)
        return carry

    def partial1(a, o):
        b = ab(a)
        rows = slice(o * 256, o * 256 + 256)
        f = nrm[b, rows].astype(F32)
        v = acc1[a, rows] - f * rowsq[a, 0:1, :]
        gd = jnp.where(a == ylo, dg[1:2, :], 0.0)
        v = v + (nrm[2, rows].astype(F32) - f * dg[0:1, :]) * gd
        return v * fin[b, 1:2, :]

    def p1_start(ph, e):
        for a in (e, 2 + e):
            rowsq[a] = nt(jnp.ones((8, 128), F32), rsq[a], HIGH) * (0.5 / LAMBDA)
        m = M_P1 + 6 * ph
        p1[ph, 0] = partial1(2 + e, 0).astype(BF16)
        relay = [
            send(m, p1.at[ph, 0, top], p1relay.at[ph, top], sib),
            send(m + 1, p1.at[ph, 0, low], p1relay.at[ph, low], non),
        ]
        p1[ph, 1] = partial1(2 + e, 1).astype(BF16)
        a = send(m + 2, p1.at[ph, 1, low], p1in.at[ph, 1, low], non)
        p1[ph, 2] = partial1(e, 1).astype(BF16)
        b = send(m + 3, p1.at[ph, 2, top], p1in.at[ph, 0, top], sib)
        return relay, [a, b]

    def p1_add(ph, relay):
        m = M_P1 + 6 * ph
        relay[0].wait_recv()
        p1[ph, 1, top] = (p1[ph, 1, top].astype(F32) + p1relay[ph, top].astype(F32)).astype(BF16)
        a = send(m + 4, p1.at[ph, 1, top], p1in.at[ph, 1, top], non)
        relay[1].wait_recv()
        p1[ph, 2, low] = (p1[ph, 2, low].astype(F32) + p1relay[ph, low].astype(F32)).astype(BF16)
        return [a, send(m + 5, p1.at[ph, 2, low], p1in.at[ph, 0, low], sib)]

    lax.fori_loop(1, 4, step, 0)
    uses(3, False)
    relay1, in1 = p1_start(0, iz)
    arrive(4, True, None)

    def final_two(n, carry):
        use(lax.rem(c + n, 2), lax.rem(z + 4, 8))
        return carry

    lax.fori_loop(0, 1, final_two, 0)
    from_core(4, 0, 0)
    from_core(4, 1, 1)
    lax.fori_loop(1, 2, final_two, 0)

    for k in range(4):
        colsq[k] = jnp.sum(csq[k], 0, keepdims=True) * (0.5 / LAMBDA)

    def partial2(k, o):
        b = KB[k]
        rows = slice(o * 256, o * 256 + 256)
        s = nrm[b, rows].astype(F32)
        v = acc2[k, rows] - s * colsq[k]
        if k == 0:
            v = v + (nrm[ylo, rows].astype(F32) - s * dg[0:1, :]) * dg[1:2, :]
        return v * fin[b, 1:2, :]

    def p2_relay(o):
        p2[2, o] = partial2(2, o).astype(BF16)
        return [
            send(M_P2O + 2 * o, p2.at[2, o, top], p2relay.at[o, top], right),
            send(M_P2O + 2 * o + 1, p2.at[2, o, low], p2relay.at[o, low], left),
        ]

    def p2_send(o):
        p2[1, o] = partial2(1, o).astype(BF16)
        a = send(M_P2R + 2 * o, p2.at[1, o, low], p2in.at[0, o, low], right)
        p2[3, o] = partial2(3, o).astype(BF16)
        return [a, send(M_P2L + 2 * o, p2.at[3, o, top], p2in.at[1, o, top], left)]

    def p2_add(o, relay):
        relay[0].wait_recv()
        p2[1, o, top] = (p2[1, o, top].astype(F32) + p2relay[o, top].astype(F32)).astype(BF16)
        a = send(M_P2R + 2 * o + 1, p2.at[1, o, top], p2in.at[0, o, top], right)
        relay[1].wait_recv()
        p2[3, o, low] = (p2[3, o, low].astype(F32) + p2relay[o, low].astype(F32)).astype(BF16)
        return [a, send(M_P2L + 2 * o + 1, p2.at[3, o, low], p2in.at[1, o, low], left)]

    def sent(i, part):
        make(i, part, part, core).wait_send()

    def finish_sends():
        for cp in done:
            cp.wait_send()
        for s in range(8):
            sent(M_C + s, csend.at[s])
        for d in range(2):
            for t in range(1, 5):
                for u in range(2):
                    if t > 1 and (t < 4 or u == d):
                        for s in range(2):
                            sent(M_ZG + zslot(d, t, u) + s, g.at[0, 0, 0])
                    if t < 4 or u == d:
                        sent(M_GD + 4 * t + 2 * d + u, g.at[0, 0, pl.ds(0, 2)])

    done = list(sends)
    relay2 = p2_relay(1)
    in1 += p1_add(0, relay1)
    in2 = p2_send(1)
    relay1, more = p1_start(1, 1 - iz)
    in1 += more
    relay20 = p2_relay(0)
    in2 += p2_add(1, relay2)
    in20 = p2_send(0)
    ob2[0] = partial2(0, 1)
    ob2[1] = partial2(0, 0)
    in1 += p1_add(1, relay1)
    in20 += p2_add(0, relay20)
    finish_sends()
    for cp in in2:
        cp.wait_recv()
    xs[...] = (ob2[0] + p2in[0, 1].astype(F32) + p2in[1, 1].astype(F32)).astype(BF16)
    x_last = send(M_X, xs, xr, sib)
    ob1[0] = partial1(iz, 0)
    ob1[1] = partial1(1 - iz, 0)
    outs = []

    def put(src, ref, col, i):
        cp = pltpu.make_async_copy(src, ref.at[:, pl.ds(pl.multiple_of(col, 256), 256)], os_.at[i])
        cp.start()
        outs.append(cp)

    for cp in in20:
        cp.wait_recv()
    ob2[1] = ob2[1] + p2in[0, 0].astype(F32) + p2in[1, 0].astype(F32)
    put(ob2.at[1], out2, lo, 0)
    for cp in in1:
        cp.wait_recv()
    for ph, e in enumerate((iz, 1 - iz)):
        ob1[ph] = ob1[ph] + p1in[ph, 0].astype(F32) + p1in[ph, 1].astype(F32)
        put(ob1.at[ph], out1, e * 256, 1 + ph)
    x_last.wait_recv()
    ob2[0] = xr[...].astype(F32)
    put(ob2.at[0], out2, hi, 3)
    for cp in outs:
        cp.wait()
    for cp in sends[len(done) :]:
        cp.wait_send()


def write_kernel(a, b, out1, out2, sem):
    cps = []
    for n, (src, dst) in enumerate(((a, out1), (b, out2))):
        for q in range(2):
            rows = pl.ds(128 * q, 128)
            cps.append(pltpu.make_async_copy(src.at[rows], dst.at[rows], sem.at[2 * n + q]))
    for cp in cps:
        cp.start()
    for cp in cps:
        cp.wait()


def body(first, second):
    v = pltpu.VMEM
    out = jax.ShapeDtypeStruct((256, 512), F32)
    anywhere = pl.BlockSpec(memory_space=pl.ANY)
    parts = pl.pallas_call(
        kernel,
        out_shape=(out, out),
        in_specs=[anywhere, anywhere],
        out_specs=(anywhere, anywhere),
        scratch_shapes=[
            v((16, 256, 256), F32),
            v((16, 256, 256), BF16),
            v((8, 256, 256), BF16),
            v((4, 256, 256), BF16),
            v((16, 4, 256), F32),
            v((2, 4, 4, 256), F32),
            v((4, 8, 4, 256), F32),
            v((8, 4, 256), F32),
            v((8, 4, 4, 256), F32),
            v((7, 4, 4, 256), F32),
            v((8, 4, 256), F32),
            v((2, 256), F32),
            v((256, 256), F32),
            v((256, 256), F32),
            v((8, 512, 256), BF16),
            v((8, 256, 256), F32),
            v((8, 256, 256), F32),
            v((8, 512, 256), BF16),
            v((8, 512, 256), BF16),
            v((8, 256, 256), BF16),
            v((8, 256, 256), BF16),
            v((32, 64, 256), BF16),
            v((32, 64, 256), BF16),
            v((2, 8, 4, 64, 256), BF16),
            v((4, 512, 256), F32),
            v((4, 512, 256), F32),
            v((4, 256, 128), F32),
            v((4, 8, 256), F32),
            v((4, 8, 256), F32),
            v((4, 1, 256), F32),
            v((2, 3, 256, 256), BF16),
            v((2, 2, 256, 256), BF16),
            v((2, 256, 256), BF16),
            v((4, 2, 256, 256), BF16),
            v((2, 2, 256, 256), BF16),
            v((2, 256, 256), BF16),
            v((256, 256), BF16),
            v((256, 256), BF16),
            v((2, 256, 256), F32),
            v((2, 256, 256), F32),
            pltpu.SemaphoreType.DMA((M_ALL,)),
            pltpu.SemaphoreType.DMA((M_ALL,)),
            pltpu.SemaphoreType.DMA((16,)),
            pltpu.SemaphoreType.DMA((4,)),
        ],
        compiler_params=pltpu.CompilerParams(
            collective_id=0, has_side_effects=True, vmem_limit_bytes=51 * 1024 * 1024
        ),
    )(first, second)
    return pl.pallas_call(
        write_kernel,
        out_shape=(out, out),
        in_specs=[pl.BlockSpec(memory_space=pltpu.VMEM)] * 2,
        out_specs=(anywhere, anywhere),
        scratch_shapes=[pltpu.SemaphoreType.DMA((4,))],
        compiler_params=pltpu.CompilerParams(vmem_limit_bytes=8 * 1024 * 1024),
    )(*parts)


def solution(mesh):
    return jax.shard_map(
        body,
        mesh=mesh,
        in_specs=(P("dp", None), P("dp", None)),
        out_specs=(P("dp", "replica"), P("dp", "replica")),
        check_vma=False,
    )
```

```python
import jax
import jax.numpy as jnp
from jax import lax
from jax.experimental import pallas as pl
from jax.experimental.pallas import tpu as pltpu
from jax.sharding import PartitionSpec as P

LAMBDA = 0.0051
EPS = 1e-05
MESH = pl.DeviceIdType.MESH
F32 = jnp.float32
BF16 = jnp.bfloat16
BATCH = 8192

OWN = (0, 1, 4, 5, 2, 3, 6, 7)
STAT_SIB = (0, 1, 8, 9)
STAT_NON = (0, 1, 14, 15)
KB = (2, 3, 6, 7)
AB = (0, 1, 4, 5)

M_Y = 0
M_ST1 = 12
M_ST2 = 17
M_ST3 = 24
M_C = 31
M_YP = 39
M_ZR = 55
M_ZG = 87
M_GD = 119
M_P1 = 139
M_P2O = 151
M_P2R = 155
M_P2L = 159
M_X = 163
M_ALL = 164

HIGH = lax.Precision.HIGHEST


def nt(a, b, precision=None):
    return lax.dot_general(
        a, b, (((1,), (1,)), ((), ())), preferred_element_type=F32, precision=precision
    )


def tn(a, b, precision=None):
    return lax.dot_general(
        a, b, (((0,), (0,)), ((), ())), preferred_element_type=F32, precision=precision
    )


def nn(a, b):
    return lax.dot_general(a, b, (((1,), (0,)), ((), ())), preferred_element_type=F32)


def ab(a):
    return a + 2 * lax.div(a, 2)


def kb(k):
    return k + 2 + 2 * lax.div(k, 2)


def kernel(
    first, second, out1, out2,
    raw, cen, oth, xt, stat, smsg, st1, pst, st2m, st2, fin, dg, scl, fix, nrm, cown, ypart, csend, crecv, ys, yr, zs, zr, g,
    acc1, acc2, rsq, csq, rowsq, colsq,
    p1, p1in, p1relay, p2, p2in, p2relay, xs, xr, ob1, ob2, ss, rs, ls, os_,
):
    dp = lax.axis_index("dp")
    rep = lax.axis_index("replica")
    c = lax.rem(dp, 2)
    ylo = lax.rem(lax.div(dp, 2), 2)
    z = lax.div(dp, 4)
    yhi = lax.div(rep, 4)
    x = lax.rem(rep, 4)

    def dev(x_, yhi_, ylo_, z_, c_):
        return (z_ * 4 + ylo_ * 2 + c_, yhi_ * 4 + x_)

    core = dev(x, yhi, ylo, z, 1 - c)
    sib = dev(x, yhi, 1 - ylo, z, c)
    sibc = dev(x, yhi, 1 - ylo, z, 1 - c)
    non = dev(x, 1 - yhi, 1 - ylo, z, c)
    nonc = dev(x, 1 - yhi, 1 - ylo, z, 1 - c)
    right = dev(lax.rem(x + 1, 4), yhi, ylo, z, c)
    left = dev(lax.rem(x + 3, 4), yhi, ylo, z, c)
    zdev = [dev(x, yhi, ylo, lax.rem(z + q, 8), c) for q in range(8)]
    zto = (zdev[1], zdev[7])

    def load(i, ref, col):
        return pltpu.make_async_copy(
            ref.at[:, pl.ds(pl.multiple_of(col, 256), 256)], raw.at[i], ls.at[i]
        )

    kz = lax.rem(z, 4)
    iz = lax.div(z, 4)
    base = yhi * 2048
    other = 2048 - base
    mine = x * 512
    lo = ylo * 256
    hi = 256 - lo
    def load_first(e):
        for j in range(2):
            load(2 * j + e, first, (base, other)[j] + mine + 256 * e).start()

    def load_second(k):
        piece = lax.rem(x + k, 4) * 512
        for m, col in enumerate((base + lo, base + hi, other + hi)):
            load(4 + 4 * m + k, second, col + piece).start()

    load_first(1 - iz)
    load_second(kz)
    barrier = pltpu.get_barrier_semaphore()
    partners = [core, sib, sibc, non, nonc, right, left] + zdev[1:]
    for d in partners:
        pl.semaphore_signal(barrier, inc=1, device_id=d, device_id_type=MESH)
    load_first(iz)
    for n in (3, 1, 2):
        load_second(lax.rem(kz + n, 4))

    def make(i, src, dst, to):
        return pltpu.make_async_remote_copy(
            src_ref=src, dst_ref=dst, send_sem=ss.at[i], recv_sem=rs.at[i], device_id=to, device_id_type=MESH
        )

    sends = []

    def send(i, src, dst, to):
        cp = make(i, src, dst, to)
        cp.start()
        sends.append(cp)
        return cp

    def local_stats(i, carry):
        pltpu.make_async_copy(first.at[:, pl.ds(0, 256)], raw.at[i], ls.at[i]).wait()
        v = raw[i]
        m = jnp.sum(v, 0, keepdims=True) * (1.0 / 256)
        dv = v - m
        r = dv.astype(BF16)
        cen[i] = r
        stat[i, 0:1, :] = m
        stat[i, 1:2, :] = jnp.sum(dv * dv, 0, keepdims=True)
        stat[i, 2:3, :] = jnp.sum(r.astype(F32), 0, keepdims=True)
        stat[i, 3:4, :] = jnp.zeros_like(m)
        return carry

    top, low = pl.ds(0, 128), pl.ds(128, 128)

    def blocks_k(m, carry):
        return local_stats(4 + 4 * lax.rem(m, 3) + lax.rem(kz + lax.div(m, 3), 4), carry)

    def first_blocks(e):
        def one(j, carry):
            local_stats(2 * j + e, carry)
            xt[2 * j + e] = cen[2 * j + e].T
            return carry

        lax.fori_loop(0, 2, one, 0)

    first_blocks(1 - iz)
    lax.fori_loop(0, 3, blocks_k, 0)
    pl.semaphore_wait(barrier, len(partners))

    def corr(s, carry):
        r = jnp.where(lax.rem(s, 2) == 1, 4 - lax.div(s + 1, 2), 4 + lax.div(s, 2))
        d = lax.rem(z + r, 8)
        i = lax.div(d, 4)
        k = lax.rem(d, 4)
        a = 2 * (1 - c) + i
        b = 2 * c + i
        v = nn(jnp.concatenate([xt[a], xt[b]], 0), cen[4 + k])
        csend[s, 0:256] = v[0:256].astype(BF16)
        cown[s] = v[256:512]
        v = nn(jnp.concatenate([xt[a, top], xt[b, top]], 0), cen[8 + k])
        csend[s, 256:384] = v[0:128].astype(BF16)
        ypart[s, 0:128] = v[128:256]
        v = nn(jnp.concatenate([xt[b, low], xt[a, low]], 0), cen[12 + k])
        csend[s, 384:512] = v[0:128].astype(BF16)
        ypart[s, 128:256] = v[128:256]
        make(M_C + s, csend.at[s], crecv.at[s], core).start()
        return carry

    y_sum = []

    def to_y(s):
        make(M_C + s, csend.at[s], crecv.at[s], core).wait_recv()
        ys[s] = (ypart[s] + crecv[s, 256:512].astype(F32)).astype(BF16)
        y_sum.append(
            (
                send(M_YP + 2 * s, ys.at[s, top], yr.at[s, top], sib),
                send(M_YP + 2 * s + 1, ys.at[s, low], yr.at[s, low], non),
            )
        )

    corr(0, 0)
    first_blocks(iz)
    lax.fori_loop(3, 12, blocks_k, 0)
    def zslot(d, t, u):
        return d * 16 + (t - 1) * 4 + u * 2

    z_in = {}

    def chain(t, far):
        dist = 5 - t
        slot = (7 - 2 * dist, 8 - 2 * dist) if dist < 4 else (0, 0)
        if (t, far) in ((1, True), (2, False), (3, False), (4, False)):
            for n in set(slot):
                for cp in y_sum[n]:
                    cp.wait_recv()
        for s in range(2):
            for d in range(2):
                u = d if far else 1 - d
                n = slot[d]
                rows = slice(128 * u + 64 * s, 128 * u + 64 * s + 64)
                v = cown[n, rows] + crecv[n, rows].astype(F32) + yr[n, rows].astype(F32)
                if (d, t - 1, u, s) in z_in:
                    z_in[(d, t - 1, u, s)].wait_recv()
                    v = v + zr[zslot(d, t - 1, u) + s].astype(F32)
                i = zslot(d, t, u) + s
                zs[i] = v.astype(BF16)
                z_in[(d, t, u, s)] = send(M_ZR + i, zs.at[i], zr.at[i], zto[d])

    def comoment(i, j):
        return jnp.sum((raw[i] - stat[i, 0:1, :]) * (raw[j] - stat[j, 0:1, :]), 0, keepdims=True)

    for n in range(4):
        smsg[0, n] = stat[STAT_SIB[n]]
        smsg[1, n] = stat[STAT_NON[n]]
    for b in range(8):
        st1[0, b] = stat[OWN[b]]
    smsg[0, 1 - ylo, 3:4, :] = comoment(1 - ylo, 8)
    st1[0, ylo, 3:4, :] = comoment(ylo, 4)
    st_in = [
        send(M_ST1 + 0, smsg.at[0], st1.at[2, pl.ds(0, 4)], sib),
        send(M_ST1 + 1, smsg.at[1], st1.at[2, pl.ds(4, 4)], non),
        send(M_ST1 + 2, smsg.at[0], st1.at[3, pl.ds(0, 4)], sibc),
        send(M_ST1 + 3, smsg.at[1], st1.at[3, pl.ds(4, 4)], nonc),
        send(M_ST1 + 4, st1.at[0], st1.at[1], core),
    ]
    to_y(0)
    lax.fori_loop(1, 5, corr, 0)
    to_y(1)
    to_y(2)
    for cp in st_in:
        cp.wait_recv()

    def merge(rows, count):
        total = sum(rows[1:], rows[0])
        m = total[0:1] * (1.0 / len(rows))
        dv = [r[0:1] - m for r in rows]
        m2 = total[1:2] + count * sum([d * d for d in dv[1:]], dv[0] * dv[0])
        return m, m2, total[2:3], total[3:4], dv

    def cross(p, q):
        return sum([a * b for a, b in zip(p[1:], q[1:])], p[0] * q[0])

    merged = [merge([st1[s, b] for s in range(4)], 256.0) for b in range(8)]
    for b, (m, m2, r, co, dv) in enumerate(merged):
        if b < 2:
            co = co + 256.0 * cross(dv, merged[2][4])
        for n, row in enumerate((m, m2, r, co)):
            pst[b, n : n + 1, :] = row
    st2_in = []
    for q in range(8):
        zq = lax.rem(z + q, 8)
        fa = ab(2 * c + lax.div(zq, 4))
        fk = kb(lax.rem(zq, 4))
        st2m[q, 0] = pst[zq]
        st2m[q, 3] = pst[2]
        for s in range(4):
            st2m[q, 1, s : s + 1, :] = st1[s, fa, 0:1, :]
            st2m[q, 2, s : s + 1, :] = st1[s, fk, 0:1, :]
        if q:
            st2_in.append(send(M_ST2 + q - 1, st2m.at[q], st2.at[q - 1], zdev[q]))

    to_y(3)
    to_y(4)
    chain(1, True)

    lax.fori_loop(5, 8, corr, 0)
    chain(2, False)
    to_y(5)
    to_y(6)
    to_y(7)
    x_in = [
        send(M_Y + 0, cen.at[8, top], oth.at[2, top], sib),
        send(M_Y + 1, cen.at[12, low], oth.at[2, low], non),
        send(M_Y + 2, cen.at[0], oth.at[0], sib),
        send(M_Y + 3, cen.at[0], oth.at[4], non),
        send(M_Y + 4, cen.at[1], oth.at[1], sib),
        send(M_Y + 5, cen.at[1], oth.at[5], non),
    ]
    chain(2, True)

    def zero(n, carry):
        acc1[n] = jnp.zeros((512, 256), F32)
        acc2[n] = jnp.zeros((512, 256), F32)
        return carry

    lax.fori_loop(0, 4, zero, 0)
    rsq[...] = jnp.zeros_like(rsq)
    csq[...] = jnp.zeros_like(csq)
    for cp in st2_in:
        cp.wait_recv()
    st2m_all = [st2m[0, 0]] + [st2[s, 0] for s in range(7)]
    k0_means = [st2m[0, 3]] + [st2[s, 3] for s in range(7)]
    m, m2, r, co, dv = merge(st2m_all, 1024.0)
    k0_dv = merge(k0_means, 1024.0)[4]
    fin[z, 0:1, :] = m + r * (1.0 / BATCH)
    fin[z, 1:2, :] = lax.rsqrt(m2 * (1.0 / BATCH) + EPS)
    fin[z, 2:3, :] = m
    fin[z, 3:4, :] = co + 1024.0 * cross(dv, k0_dv)
    fin_in = [send(M_ST3 + q - 1, fin.at[z], fin.at[z], zdev[q]) for q in range(1, 8)]

    chain(3, False)

    chain(3, True)
    x_in[0].wait_recv()
    x_in[1].wait_recv()
    x_ring = [
        send(M_Y + 6, oth.at[2], oth.at[3], left),
        send(M_Y + 7, oth.at[2], oth.at[7], right),
    ]

    def norm(b, o):
        shift = st1[2 * o, b, 0:1, :] - fin[b, 0:1, :]
        scale = fin[b, 1:2, :]
        q = lax.rem(b, 4)
        idx = jnp.where(q < 2, 0, 2) + q + 2 * lax.div(b, 4)
        for h in range(2):
            rows = slice(128 * h, 128 * h + 128)
            v = cen[idx, rows] if o == 0 else oth[b, rows]
            nrm[b, o * 256 + 128 * h : o * 256 + 128 * h + 128, :] = ((v.astype(F32) + shift) * scale).astype(BF16)

    def norms(o):
        lax.fori_loop(0, 8, lambda b, carry: (norm(b, o), carry)[1], 0)

    chain(4, False)
    for cp in fin_in:
        cp.wait_recv()
    cii = fin[ylo, 3:4, :] * fin[ylo, 1:2, :] * fin[2, 1:2, :] * (1.0 / BATCH)
    dg[0:1, :] = cii
    dg[1:2, :] = (-2.0 * (1.0 - cii)).astype(BF16).astype(F32)
    norms(0)
    chain(4, True)
    x_ring[0].wait_recv()
    x_ring.append(send(M_Y + 8, oth.at[3, top], oth.at[6, top], left))
    x_ring[1].wait_recv()
    x_ring.append(send(M_Y + 9, oth.at[7, low], oth.at[6, low], right))

    fa = ab(2 * c + lax.div(z, 4))
    fk = kb(lax.rem(z, 4))
    pad = jnp.zeros((7, 256), F32)
    ra = jnp.concatenate([fin[fa, 1:2, :] * (2.0 * LAMBDA / BATCH), pad], 0)
    rk = jnp.concatenate([fin[fk, 1:2, :], pad], 0)
    rows_id = lax.broadcasted_iota(jnp.int32, (256, 256), 0)
    cols_id = lax.broadcasted_iota(jnp.int32, (256, 256), 1)
    off = rows_id + jnp.where((c == 0) & (z == 4 * ylo), 0, 512) != cols_id
    scl[...] = jnp.where(off, tn(ra, rk, HIGH), 0.0)
    mu_a = [(st2m[0, 1] if s == 0 else st2[s - 1, 1]) - fin[fa, 2:3, :] for s in range(8)]
    mu_k = [(st2m[0, 2] if s == 0 else st2[s - 1, 2]) - fin[fk, 2:3, :] for s in range(8)]
    fix[...] = scl[...] * tn(jnp.concatenate(mu_a, 0) * 256.0, jnp.concatenate(mu_k, 0), HIGH)

    for cp in y_sum[7]:
        cp.wait_recv()
    for s in range(2):
        for u in range(2):
            q = 2 * u + s
            rows = slice(64 * q, 64 * q + 64)
            v = cown[7, rows] + crecv[7, rows].astype(F32) + yr[7, rows].astype(F32)
            for d in (1 - u, u):
                z_in[(d, 4, u, s)].wait_recv()
                v = v + zr[zslot(d, 4, u) + s].astype(F32)
            part = g.at[c, z, q]
            g[c, z, q] = (v * scl[rows] + fix[rows]).astype(BF16)
            for d in (u, 1 - u):
                send(M_ZG + zslot(d, 1, u) + s, part, part, zto[d])
    send(M_GD + 0, g.at[c, z, pl.ds(0, 2)], g.at[c, z, pl.ds(0, 2)], core)
    send(M_GD + 1, g.at[c, z, pl.ds(2, 2)], g.at[c, z, pl.ds(2, 2)], core)

    def arrive(t, far, onward):
        for s in range(2):
            for d in range(2):
                u = d if far else 1 - d
                i = d * 16 + (t - 1) * 4 + u * 2 + s
                source = lax.rem(z + (8 - t if d == 0 else t), 8)
                part = g.at[c, source, 2 * u + s]
                make(M_ZG + i, part, part, zto[d]).wait_recv()
                if onward is not None:
                    start = make(M_ZG + i + 4, part, part, zto[d]).start
                    if onward is True:
                        start()
                    else:
                        pl.when(onward)(start)
                if s == 1:
                    both = g.at[c, source, pl.ds(2 * u, 2)]
                    make(M_GD + 4 * t + 2 * d + u, both, both, core).start()

    def use(j, zs_):
        a = 2 * j + lax.div(zs_, 4)
        k = lax.rem(zs_, 4)
        ga = g[j, zs_].reshape(256, 256)
        acc1[a] += nt(nrm[kb(k)], ga)
        acc2[k] += nn(nrm[ab(a)], ga)
        v = ga.astype(F32)
        s = v * v
        rsq[a] += s[:, 0:128] + s[:, 128:256]
        csq[k] += jnp.sum(s.reshape(32, 8, 256), 0)

    def from_core(t, d, u):
        part = g.at[0, 0, pl.ds(0, 2)]
        make(M_GD + 4 * t + 2 * d + u, part, part, core).wait_recv()

    def uses(t, mine_too):
        def one(n, inner):
            if not mine_too:
                for u in range(2):
                    from_core(t, n, u)
            use(c if mine_too else 1 - c, lax.rem(z + (8 - t) + n * 2 * t, 8))
            return inner

        lax.fori_loop(0, jnp.where(t == 0, 1, 2), one, 0)

    for cp in x_in[2:] + x_ring[2:]:
        cp.wait_recv()
    norms(1)
    uses(0, True)

    def step(t, carry):
        arrive(t, True, True)
        uses(t - 1, False)
        arrive(t, False, t < 3)
        uses(t, True)
        return carry

    def partial1(a, o):
        b = ab(a)
        rows = slice(o * 256, o * 256 + 256)
        f = nrm[b, rows].astype(F32)
        v = acc1[a, rows] - f * rowsq[a, 0:1, :]
        gd = jnp.where(a == ylo, dg[1:2, :], 0.0)
        v = v + (nrm[2, rows].astype(F32) - f * dg[0:1, :]) * gd
        return v * fin[b, 1:2, :]

    def p1_start(ph, e):
        for a in (e, 2 + e):
            rowsq[a] = nt(jnp.ones((8, 128), F32), rsq[a], HIGH) * (0.5 / LAMBDA)
        m = M_P1 + 6 * ph
        p1[ph, 0] = partial1(2 + e, 0).astype(BF16)
        relay = [
            send(m, p1.at[ph, 0, top], p1relay.at[ph, top], sib),
            send(m + 1, p1.at[ph, 0, low], p1relay.at[ph, low], non),
        ]
        p1[ph, 1] = partial1(2 + e, 1).astype(BF16)
        a = send(m + 2, p1.at[ph, 1, low], p1in.at[ph, 1, low], non)
        p1[ph, 2] = partial1(e, 1).astype(BF16)
        b = send(m + 3, p1.at[ph, 2, top], p1in.at[ph, 0, top], sib)
        return relay, [a, b]

    def p1_add(ph, relay):
        m = M_P1 + 6 * ph
        relay[0].wait_recv()
        p1[ph, 1, top] = (p1[ph, 1, top].astype(F32) + p1relay[ph, top].astype(F32)).astype(BF16)
        a = send(m + 4, p1.at[ph, 1, top], p1in.at[ph, 1, top], non)
        relay[1].wait_recv()
        p1[ph, 2, low] = (p1[ph, 2, low].astype(F32) + p1relay[ph, low].astype(F32)).astype(BF16)
        return [a, send(m + 5, p1.at[ph, 2, low], p1in.at[ph, 0, low], sib)]

    lax.fori_loop(1, 4, step, 0)
    uses(3, False)
    relay1, in1 = p1_start(0, iz)
    arrive(4, True, None)

    def final_two(n, carry):
        use(lax.rem(c + n, 2), lax.rem(z + 4, 8))
        return carry

    lax.fori_loop(0, 1, final_two, 0)
    from_core(4, 0, 0)
    from_core(4, 1, 1)
    lax.fori_loop(1, 2, final_two, 0)

    for k in range(4):
        colsq[k] = jnp.sum(csq[k], 0, keepdims=True) * (0.5 / LAMBDA)

    def partial2(k, o):
        b = KB[k]
        rows = slice(o * 256, o * 256 + 256)
        s = nrm[b, rows].astype(F32)
        v = acc2[k, rows] - s * colsq[k]
        if k == 0:
            v = v + (nrm[ylo, rows].astype(F32) - s * dg[0:1, :]) * dg[1:2, :]
        return v * fin[b, 1:2, :]

    def p2_relay(o):
        p2[2, o] = partial2(2, o).astype(BF16)
        return [
            send(M_P2O + 2 * o, p2.at[2, o, top], p2relay.at[o, top], right),
            send(M_P2O + 2 * o + 1, p2.at[2, o, low], p2relay.at[o, low], left),
        ]

    def p2_send(o):
        p2[1, o] = partial2(1, o).astype(BF16)
        a = send(M_P2R + 2 * o, p2.at[1, o, low], p2in.at[0, o, low], right)
        p2[3, o] = partial2(3, o).astype(BF16)
        return [a, send(M_P2L + 2 * o, p2.at[3, o, top], p2in.at[1, o, top], left)]

    def p2_add(o, relay):
        relay[0].wait_recv()
        p2[1, o, top] = (p2[1, o, top].astype(F32) + p2relay[o, top].astype(F32)).astype(BF16)
        a = send(M_P2R + 2 * o + 1, p2.at[1, o, top], p2in.at[0, o, top], right)
        relay[1].wait_recv()
        p2[3, o, low] = (p2[3, o, low].astype(F32) + p2relay[o, low].astype(F32)).astype(BF16)
        return [a, send(M_P2L + 2 * o + 1, p2.at[3, o, low], p2in.at[1, o, low], left)]

    def sent(i, part):
        make(i, part, part, core).wait_send()

    def finish_sends():
        for cp in done:
            cp.wait_send()
        for s in range(8):
            sent(M_C + s, csend.at[s])
        for d in range(2):
            for t in range(1, 5):
                for u in range(2):
                    if t > 1 and (t < 4 or u == d):
                        for s in range(2):
                            sent(M_ZG + zslot(d, t, u) + s, g.at[0, 0, 0])
                    if t < 4 or u == d:
                        sent(M_GD + 4 * t + 2 * d + u, g.at[0, 0, pl.ds(0, 2)])

    done = list(sends)
    relay2 = p2_relay(1)
    in1 += p1_add(0, relay1)
    in2 = p2_send(1)
    relay1, more = p1_start(1, 1 - iz)
    in1 += more
    relay20 = p2_relay(0)
    in2 += p2_add(1, relay2)
    in20 = p2_send(0)
    ob2[0] = partial2(0, 1)
    ob2[1] = partial2(0, 0)
    in1 += p1_add(1, relay1)
    in20 += p2_add(0, relay20)
    finish_sends()
    for cp in in2:
        cp.wait_recv()
    xs[...] = (ob2[0] + p2in[0, 1].astype(F32) + p2in[1, 1].astype(F32)).astype(BF16)
    x_last = send(M_X, xs, xr, sib)
    ob1[0] = partial1(iz, 0)
    ob1[1] = partial1(1 - iz, 0)
    outs = []

    def put(src, ref, col, i):
        cp = pltpu.make_async_copy(src, ref.at[:, pl.ds(pl.multiple_of(col, 256), 256)], os_.at[i])
        cp.start()
        outs.append(cp)

    for cp in in20:
        cp.wait_recv()
    ob2[1] = ob2[1] + p2in[0, 0].astype(F32) + p2in[1, 0].astype(F32)
    put(ob2.at[1], out2, lo, 0)
    for cp in in1:
        cp.wait_recv()
    for ph, e in enumerate((iz, 1 - iz)):
        ob1[ph] = ob1[ph] + p1in[ph, 0].astype(F32) + p1in[ph, 1].astype(F32)
        put(ob1.at[ph], out1, e * 256, 1 + ph)
    x_last.wait_recv()
    ob2[0] = xr[...].astype(F32)
    put(ob2.at[0], out2, hi, 3)
    for cp in outs:
        cp.wait()
    for cp in sends[len(done) :]:
        cp.wait_send()


def write_kernel(a, b, out1, out2, sem):
    cps = []
    for n, (src, dst) in enumerate(((a, out1), (b, out2))):
        for q in range(2):
            rows = pl.ds(128 * q, 128)
            cps.append(pltpu.make_async_copy(src.at[rows], dst.at[rows], sem.at[2 * n + q]))
    for cp in cps:
        cp.start()
    for cp in cps:
        cp.wait()


def body(first, second):
    v = pltpu.VMEM
    out = jax.ShapeDtypeStruct((256, 512), F32)
    anywhere = pl.BlockSpec(memory_space=pl.ANY)
    parts = pl.pallas_call(
        kernel,
        out_shape=(out, out),
        in_specs=[anywhere, anywhere],
        out_specs=(anywhere, anywhere),
        scratch_shapes=[
            v((16, 256, 256), F32),
            v((16, 256, 256), BF16),
            v((8, 256, 256), BF16),
            v((4, 256, 256), BF16),
            v((16, 4, 256), F32),
            v((2, 4, 4, 256), F32),
            v((4, 8, 4, 256), F32),
            v((8, 4, 256), F32),
            v((8, 4, 4, 256), F32),
            v((7, 4, 4, 256), F32),
            v((8, 4, 256), F32),
            v((2, 256), F32),
            v((256, 256), F32),
            v((256, 256), F32),
            v((8, 512, 256), BF16),
            v((8, 256, 256), F32),
            v((8, 256, 256), F32),
            v((8, 512, 256), BF16),
            v((8, 512, 256), BF16),
            v((8, 256, 256), BF16),
            v((8, 256, 256), BF16),
            v((32, 64, 256), BF16),
            v((32, 64, 256), BF16),
            v((2, 8, 4, 64, 256), BF16),
            v((4, 512, 256), F32),
            v((4, 512, 256), F32),
            v((4, 256, 128), F32),
            v((4, 8, 256), F32),
            v((4, 8, 256), F32),
            v((4, 1, 256), F32),
            v((2, 3, 256, 256), BF16),
            v((2, 2, 256, 256), BF16),
            v((2, 256, 256), BF16),
            v((4, 2, 256, 256), BF16),
            v((2, 2, 256, 256), BF16),
            v((2, 256, 256), BF16),
            v((256, 256), BF16),
            v((256, 256), BF16),
            v((2, 256, 256), F32),
            v((2, 256, 256), F32),
            pltpu.SemaphoreType.DMA((M_ALL,)),
            pltpu.SemaphoreType.DMA((M_ALL,)),
            pltpu.SemaphoreType.DMA((16,)),
            pltpu.SemaphoreType.DMA((4,)),
        ],
        compiler_params=pltpu.CompilerParams(
            collective_id=0, has_side_effects=True, vmem_limit_bytes=51 * 1024 * 1024
        ),
    )(first, second)
    return pl.pallas_call(
        write_kernel,
        out_shape=(out, out),
        in_specs=[pl.BlockSpec(memory_space=pltpu.VMEM)] * 2,
        out_specs=(anywhere, anywhere),
        scratch_shapes=[pltpu.SemaphoreType.DMA((4,))],
        compiler_params=pltpu.CompilerParams(vmem_limit_bytes=8 * 1024 * 1024),
    )(*parts)


def solution(mesh):
    return jax.shard_map(
        body,
        mesh=mesh,
        in_specs=(P("dp", None), P("dp", None)),
        out_specs=(P("dp", "replica"), P("dp", "replica")),
        check_vma=False,
    )
```

```python
import jax
import jax.numpy as jnp
from jax import lax
from jax.experimental import pallas as pl
from jax.experimental.pallas import tpu as pltpu
from jax.sharding import PartitionSpec as P

LAMBDA = 0.0051
EPS = 1e-05
MESH = pl.DeviceIdType.MESH
F32 = jnp.float32
BF16 = jnp.bfloat16
BATCH = 8192

OWN = (0, 1, 4, 5, 2, 3, 6, 7)
STAT_SIB = (0, 1, 8, 9)
STAT_NON = (0, 1, 14, 15)
KB = (2, 3, 6, 7)
AB = (0, 1, 4, 5)

M_Y = 0
M_ST1 = 12
M_ST2 = 17
M_ST3 = 24
M_C = 31
M_YP = 39
M_ZR = 55
M_ZG = 87
M_GD = 119
M_P1 = 139
M_P2O = 151
M_P2R = 155
M_P2L = 159
M_X = 163
M_ALL = 164

HIGH = lax.Precision.HIGHEST


def nt(a, b, precision=None):
    return lax.dot_general(
        a, b, (((1,), (1,)), ((), ())), preferred_element_type=F32, precision=precision
    )


def tn(a, b, precision=None):
    return lax.dot_general(
        a, b, (((0,), (0,)), ((), ())), preferred_element_type=F32, precision=precision
    )


def nn(a, b):
    return lax.dot_general(a, b, (((1,), (0,)), ((), ())), preferred_element_type=F32)


def ab(a):
    return a + 2 * lax.div(a, 2)


def kb(k):
    return k + 2 + 2 * lax.div(k, 2)


def kernel(
    first, second, out1, out2,
    raw, cen, oth, xt, stat, smsg, st1, pst, st2m, st2, fin, dg, scl, fix, nrm, cown, ypart, csend, crecv, ys, yr, zs, zr, g,
    acc1, acc2, rsq, csq, rowsq, colsq,
    p1, p1in, p1relay, p2, p2in, p2relay, xs, xr, ob1, ob2, ss, rs, ls, os_,
):
    dp = lax.axis_index("dp")
    rep = lax.axis_index("replica")
    c = lax.rem(dp, 2)
    ylo = lax.rem(lax.div(dp, 2), 2)
    z = lax.div(dp, 4)
    yhi = lax.div(rep, 4)
    x = lax.rem(rep, 4)

    def dev(x_, yhi_, ylo_, z_, c_):
        return (z_ * 4 + ylo_ * 2 + c_, yhi_ * 4 + x_)

    core = dev(x, yhi, ylo, z, 1 - c)
    sib = dev(x, yhi, 1 - ylo, z, c)
    sibc = dev(x, yhi, 1 - ylo, z, 1 - c)
    non = dev(x, 1 - yhi, 1 - ylo, z, c)
    nonc = dev(x, 1 - yhi, 1 - ylo, z, 1 - c)
    right = dev(lax.rem(x + 1, 4), yhi, ylo, z, c)
    left = dev(lax.rem(x + 3, 4), yhi, ylo, z, c)
    zdev = [dev(x, yhi, ylo, lax.rem(z + q, 8), c) for q in range(8)]
    zto = (zdev[1], zdev[7])

    def load(i, ref, col):
        return pltpu.make_async_copy(
            ref.at[:, pl.ds(pl.multiple_of(col, 256), 256)], raw.at[i], ls.at[i]
        )

    kz = lax.rem(z, 4)
    iz = lax.div(z, 4)
    base = yhi * 2048
    other = 2048 - base
    mine = x * 512
    lo = ylo * 256
    hi = 256 - lo
    def load_first(e):
        for j in range(2):
            load(2 * j + e, first, (base, other)[j] + mine + 256 * e).start()

    def load_second(k):
        piece = lax.rem(x + k, 4) * 512
        for m, col in enumerate((base + lo, base + hi, other + hi)):
            load(4 + 4 * m + k, second, col + piece).start()

    load_first(1 - iz)
    load_second(kz)
    barrier = pltpu.get_barrier_semaphore()
    partners = [core, sib, sibc, non, nonc, right, left] + zdev[1:]
    for d in partners:
        pl.semaphore_signal(barrier, inc=1, device_id=d, device_id_type=MESH)
    load_first(iz)
    for n in (3, 1, 2):
        load_second(lax.rem(kz + n, 4))

    def make(i, src, dst, to):
        return pltpu.make_async_remote_copy(
            src_ref=src, dst_ref=dst, send_sem=ss.at[i], recv_sem=rs.at[i], device_id=to, device_id_type=MESH
        )

    sends = []

    def send(i, src, dst, to):
        cp = make(i, src, dst, to)
        cp.start()
        sends.append(cp)
        return cp

    def local_stats(i, carry):
        pltpu.make_async_copy(first.at[:, pl.ds(0, 256)], raw.at[i], ls.at[i]).wait()
        v = raw[i]
        m = jnp.sum(v, 0, keepdims=True) * (1.0 / 256)
        dv = v - m
        r = dv.astype(BF16)
        cen[i] = r
        stat[i, 0:1, :] = m
        stat[i, 1:2, :] = jnp.sum(dv * dv, 0, keepdims=True)
        stat[i, 2:3, :] = jnp.sum(r.astype(F32), 0, keepdims=True)
        stat[i, 3:4, :] = jnp.zeros_like(m)
        return carry

    top, low = pl.ds(0, 128), pl.ds(128, 128)

    def blocks_k(m, carry):
        return local_stats(4 + 4 * lax.rem(m, 3) + lax.rem(kz + lax.div(m, 3), 4), carry)

    def first_blocks(e):
        def one(j, carry):
            local_stats(2 * j + e, carry)
            xt[2 * j + e] = cen[2 * j + e].T
            return carry

        lax.fori_loop(0, 2, one, 0)

    first_blocks(1 - iz)
    lax.fori_loop(0, 3, blocks_k, 0)
    pl.semaphore_wait(barrier, len(partners))

    def corr(s, carry):
        r = jnp.where(lax.rem(s, 2) == 1, 4 - lax.div(s + 1, 2), 4 + lax.div(s, 2))
        d = lax.rem(z + r, 8)
        i = lax.div(d, 4)
        k = lax.rem(d, 4)
        a = 2 * (1 - c) + i
        b = 2 * c + i
        v = nn(jnp.concatenate([xt[a], xt[b]], 0), cen[4 + k])
        csend[s, 0:256] = v[0:256].astype(BF16)
        cown[s] = v[256:512]
        v = nn(jnp.concatenate([xt[a, top], xt[b, top]], 0), cen[8 + k])
        csend[s, 256:384] = v[0:128].astype(BF16)
        ypart[s, 0:128] = v[128:256]
        v = nn(jnp.concatenate([xt[b, low], xt[a, low]], 0), cen[12 + k])
        csend[s, 384:512] = v[0:128].astype(BF16)
        ypart[s, 128:256] = v[128:256]
        make(M_C + s, csend.at[s], crecv.at[s], core).start()
        return carry

    y_sum = []

    def to_y(s):
        make(M_C + s, csend.at[s], crecv.at[s], core).wait_recv()
        ys[s] = (ypart[s] + crecv[s, 256:512].astype(F32)).astype(BF16)
        y_sum.append(
            (
                send(M_YP + 2 * s, ys.at[s, top], yr.at[s, top], sib),
                send(M_YP + 2 * s + 1, ys.at[s, low], yr.at[s, low], non),
            )
        )

    corr(0, 0)
    first_blocks(iz)
    lax.fori_loop(3, 12, blocks_k, 0)
    def zslot(d, t, u):
        return d * 16 + (t - 1) * 4 + u * 2

    z_in = {}

    def chain(t, far):
        dist = 5 - t
        slot = (7 - 2 * dist, 8 - 2 * dist) if dist < 4 else (0, 0)
        if (t, far) in ((1, True), (2, False), (3, False), (4, False)):
            for n in set(slot):
                for cp in y_sum[n]:
                    cp.wait_recv()
        for s in range(2):
            for d in range(2):
                u = d if far else 1 - d
                n = slot[d]
                rows = slice(128 * u + 64 * s, 128 * u + 64 * s + 64)
                v = cown[n, rows] + crecv[n, rows].astype(F32) + yr[n, rows].astype(F32)
                if (d, t - 1, u, s) in z_in:
                    z_in[(d, t - 1, u, s)].wait_recv()
                    v = v + zr[zslot(d, t - 1, u) + s].astype(F32)
                i = zslot(d, t, u) + s
                zs[i] = v.astype(BF16)
                z_in[(d, t, u, s)] = send(M_ZR + i, zs.at[i], zr.at[i], zto[d])

    def comoment(i, j):
        return jnp.sum((raw[i] - stat[i, 0:1, :]) * (raw[j] - stat[j, 0:1, :]), 0, keepdims=True)

    for n in range(4):
        smsg[0, n] = stat[STAT_SIB[n]]
        smsg[1, n] = stat[STAT_NON[n]]
    for b in range(8):
        st1[0, b] = stat[OWN[b]]
    smsg[0, 1 - ylo, 3:4, :] = comoment(1 - ylo, 8)
    st1[0, ylo, 3:4, :] = comoment(ylo, 4)
    st_in = [
        send(M_ST1 + 0, smsg.at[0], st1.at[2, pl.ds(0, 4)], sib),
        send(M_ST1 + 1, smsg.at[1], st1.at[2, pl.ds(4, 4)], non),
        send(M_ST1 + 2, smsg.at[0], st1.at[3, pl.ds(0, 4)], sibc),
        send(M_ST1 + 3, smsg.at[1], st1.at[3, pl.ds(4, 4)], nonc),
        send(M_ST1 + 4, st1.at[0], st1.at[1], core),
    ]
    to_y(0)
    lax.fori_loop(1, 5, corr, 0)
    to_y(1)
    to_y(2)
    for cp in st_in:
        cp.wait_recv()

    def merge(rows, count):
        total = sum(rows[1:], rows[0])
        m = total[0:1] * (1.0 / len(rows))
        dv = [r[0:1] - m for r in rows]
        m2 = total[1:2] + count * sum([d * d for d in dv[1:]], dv[0] * dv[0])
        return m, m2, total[2:3], total[3:4], dv

    def cross(p, q):
        return sum([a * b for a, b in zip(p[1:], q[1:])], p[0] * q[0])

    merged = [merge([st1[s, b] for s in range(4)], 256.0) for b in range(8)]
    for b, (m, m2, r, co, dv) in enumerate(merged):
        if b < 2:
            co = co + 256.0 * cross(dv, merged[2][4])
        for n, row in enumerate((m, m2, r, co)):
            pst[b, n : n + 1, :] = row
    st2_in = []
    for q in range(8):
        zq = lax.rem(z + q, 8)
        fa = ab(2 * c + lax.div(zq, 4))
        fk = kb(lax.rem(zq, 4))
        st2m[q, 0] = pst[zq]
        st2m[q, 3] = pst[2]
        for s in range(4):
            st2m[q, 1, s : s + 1, :] = st1[s, fa, 0:1, :]
            st2m[q, 2, s : s + 1, :] = st1[s, fk, 0:1, :]
        if q:
            st2_in.append(send(M_ST2 + q - 1, st2m.at[q], st2.at[q - 1], zdev[q]))

    to_y(3)
    to_y(4)
    x_in = [
        send(M_Y + 0, cen.at[8, top], oth.at[2, top], sib),
        send(M_Y + 1, cen.at[12, low], oth.at[2, low], non),
    ]
    chain(1, True)

    lax.fori_loop(5, 8, corr, 0)
    chain(2, False)
    to_y(5)
    to_y(6)
    to_y(7)
    x_in += [
        send(M_Y + 2, cen.at[0], oth.at[0], sib),
        send(M_Y + 3, cen.at[0], oth.at[4], non),
        send(M_Y + 4, cen.at[1], oth.at[1], sib),
        send(M_Y + 5, cen.at[1], oth.at[5], non),
    ]
    chain(2, True)

    def zero(n, carry):
        acc1[n] = jnp.zeros((512, 256), F32)
        acc2[n] = jnp.zeros((512, 256), F32)
        return carry

    lax.fori_loop(0, 4, zero, 0)
    rsq[...] = jnp.zeros_like(rsq)
    csq[...] = jnp.zeros_like(csq)
    x_in[0].wait_recv()
    x_in[1].wait_recv()
    x_ring = [
        send(M_Y + 6, oth.at[2], oth.at[3], left),
        send(M_Y + 7, oth.at[2], oth.at[7], right),
    ]
    for cp in st2_in:
        cp.wait_recv()
    st2m_all = [st2m[0, 0]] + [st2[s, 0] for s in range(7)]
    k0_means = [st2m[0, 3]] + [st2[s, 3] for s in range(7)]
    m, m2, r, co, dv = merge(st2m_all, 1024.0)
    k0_dv = merge(k0_means, 1024.0)[4]
    fin[z, 0:1, :] = m + r * (1.0 / BATCH)
    fin[z, 1:2, :] = lax.rsqrt(m2 * (1.0 / BATCH) + EPS)
    fin[z, 2:3, :] = m
    fin[z, 3:4, :] = co + 1024.0 * cross(dv, k0_dv)
    fin_in = [send(M_ST3 + q - 1, fin.at[z], fin.at[z], zdev[q]) for q in range(1, 8)]

    chain(3, False)

    chain(3, True)

    def norm(b, o):
        shift = st1[2 * o, b, 0:1, :] - fin[b, 0:1, :]
        scale = fin[b, 1:2, :]
        q = lax.rem(b, 4)
        idx = jnp.where(q < 2, 0, 2) + q + 2 * lax.div(b, 4)
        for h in range(2):
            rows = slice(128 * h, 128 * h + 128)
            v = cen[idx, rows] if o == 0 else oth[b, rows]
            nrm[b, o * 256 + 128 * h : o * 256 + 128 * h + 128, :] = ((v.astype(F32) + shift) * scale).astype(BF16)

    def norms(o):
        lax.fori_loop(0, 8, lambda b, carry: (norm(b, o), carry)[1], 0)

    x_ring[0].wait_recv()
    x_ring.append(send(M_Y + 8, oth.at[3, top], oth.at[6, top], left))
    x_ring[1].wait_recv()
    x_ring.append(send(M_Y + 9, oth.at[7, low], oth.at[6, low], right))
    chain(4, False)
    for cp in fin_in:
        cp.wait_recv()
    cii = fin[ylo, 3:4, :] * fin[ylo, 1:2, :] * fin[2, 1:2, :] * (1.0 / BATCH)
    dg[0:1, :] = cii
    dg[1:2, :] = (-2.0 * (1.0 - cii)).astype(BF16).astype(F32)
    norms(0)
    chain(4, True)

    fa = ab(2 * c + lax.div(z, 4))
    fk = kb(lax.rem(z, 4))
    pad = jnp.zeros((7, 256), F32)
    ra = jnp.concatenate([fin[fa, 1:2, :] * (2.0 * LAMBDA / BATCH), pad], 0)
    rk = jnp.concatenate([fin[fk, 1:2, :], pad], 0)
    rows_id = lax.broadcasted_iota(jnp.int32, (256, 256), 0)
    cols_id = lax.broadcasted_iota(jnp.int32, (256, 256), 1)
    off = rows_id + jnp.where((c == 0) & (z == 4 * ylo), 0, 512) != cols_id
    scl[...] = jnp.where(off, tn(ra, rk, HIGH), 0.0)
    mu_a = [(st2m[0, 1] if s == 0 else st2[s - 1, 1]) - fin[fa, 2:3, :] for s in range(8)]
    mu_k = [(st2m[0, 2] if s == 0 else st2[s - 1, 2]) - fin[fk, 2:3, :] for s in range(8)]
    fix[...] = scl[...] * tn(jnp.concatenate(mu_a, 0) * 256.0, jnp.concatenate(mu_k, 0), HIGH)

    for cp in y_sum[7]:
        cp.wait_recv()
    for s in range(2):
        for u in range(2):
            q = 2 * u + s
            rows = slice(64 * q, 64 * q + 64)
            v = cown[7, rows] + crecv[7, rows].astype(F32) + yr[7, rows].astype(F32)
            for d in (1 - u, u):
                z_in[(d, 4, u, s)].wait_recv()
                v = v + zr[zslot(d, 4, u) + s].astype(F32)
            part = g.at[c, z, q]
            g[c, z, q] = (v * scl[rows] + fix[rows]).astype(BF16)
            for d in (u, 1 - u):
                send(M_ZG + zslot(d, 1, u) + s, part, part, zto[d])
    send(M_GD + 0, g.at[c, z, pl.ds(0, 2)], g.at[c, z, pl.ds(0, 2)], core)
    send(M_GD + 1, g.at[c, z, pl.ds(2, 2)], g.at[c, z, pl.ds(2, 2)], core)

    def arrive(t, far, onward):
        for s in range(2):
            for d in range(2):
                u = d if far else 1 - d
                i = d * 16 + (t - 1) * 4 + u * 2 + s
                source = lax.rem(z + (8 - t if d == 0 else t), 8)
                part = g.at[c, source, 2 * u + s]
                make(M_ZG + i, part, part, zto[d]).wait_recv()
                if onward is not None:
                    start = make(M_ZG + i + 4, part, part, zto[d]).start
                    if onward is True:
                        start()
                    else:
                        pl.when(onward)(start)
                if s == 1:
                    both = g.at[c, source, pl.ds(2 * u, 2)]
                    make(M_GD + 4 * t + 2 * d + u, both, both, core).start()

    def use(j, zs_):
        a = 2 * j + lax.div(zs_, 4)
        k = lax.rem(zs_, 4)
        ga = g[j, zs_].reshape(256, 256)
        acc1[a] += nt(nrm[kb(k)], ga)
        acc2[k] += nn(nrm[ab(a)], ga)
        v = ga.astype(F32)
        s = v * v
        rsq[a] += s[:, 0:128] + s[:, 128:256]
        csq[k] += jnp.sum(s.reshape(32, 8, 256), 0)

    def from_core(t, d, u):
        part = g.at[0, 0, pl.ds(0, 2)]
        make(M_GD + 4 * t + 2 * d + u, part, part, core).wait_recv()

    def uses(t, mine_too):
        def one(n, inner):
            if not mine_too:
                for u in range(2):
                    from_core(t, n, u)
            use(c if mine_too else 1 - c, lax.rem(z + (8 - t) + n * 2 * t, 8))
            return inner

        lax.fori_loop(0, jnp.where(t == 0, 1, 2), one, 0)

    arrive(1, True, True)
    arrive(1, False, True)
    for cp in x_in[2:] + x_ring[2:]:
        cp.wait_recv()
    norms(1)
    uses(0, True)
    uses(0, False)
    uses(1, True)

    def step(t, carry):
        arrive(t, True, True)
        uses(t - 1, False)
        arrive(t, False, t < 3)
        uses(t, True)
        return carry

    def partial1(a, o):
        b = ab(a)
        rows = slice(o * 256, o * 256 + 256)
        f = nrm[b, rows].astype(F32)
        v = acc1[a, rows] - f * rowsq[a, 0:1, :]
        gd = jnp.where(a == ylo, dg[1:2, :], 0.0)
        v = v + (nrm[2, rows].astype(F32) - f * dg[0:1, :]) * gd
        return v * fin[b, 1:2, :]

    def p1_start(ph, e):
        for a in (e, 2 + e):
            rowsq[a] = nt(jnp.ones((8, 128), F32), rsq[a], HIGH) * (0.5 / LAMBDA)
        m = M_P1 + 6 * ph
        p1[ph, 0] = partial1(2 + e, 0).astype(BF16)
        relay = [
            send(m, p1.at[ph, 0, top], p1relay.at[ph, top], sib),
            send(m + 1, p1.at[ph, 0, low], p1relay.at[ph, low], non),
        ]
        p1[ph, 1] = partial1(2 + e, 1).astype(BF16)
        a = send(m + 2, p1.at[ph, 1, low], p1in.at[ph, 1, low], non)
        p1[ph, 2] = partial1(e, 1).astype(BF16)
        b = send(m + 3, p1.at[ph, 2, top], p1in.at[ph, 0, top], sib)
        return relay, [a, b]

    def p1_add(ph, relay):
        m = M_P1 + 6 * ph
        relay[0].wait_recv()
        p1[ph, 1, top] = (p1[ph, 1, top].astype(F32) + p1relay[ph, top].astype(F32)).astype(BF16)
        a = send(m + 4, p1.at[ph, 1, top], p1in.at[ph, 1, top], non)
        relay[1].wait_recv()
        p1[ph, 2, low] = (p1[ph, 2, low].astype(F32) + p1relay[ph, low].astype(F32)).astype(BF16)
        return [a, send(m + 5, p1.at[ph, 2, low], p1in.at[ph, 0, low], sib)]

    lax.fori_loop(2, 4, step, 0)
    uses(3, False)
    relay1, in1 = p1_start(0, iz)
    arrive(4, True, None)

    def final_two(n, carry):
        use(lax.rem(c + n, 2), lax.rem(z + 4, 8))
        return carry

    lax.fori_loop(0, 1, final_two, 0)
    from_core(4, 0, 0)
    from_core(4, 1, 1)
    lax.fori_loop(1, 2, final_two, 0)

    for k in range(4):
        colsq[k] = jnp.sum(csq[k], 0, keepdims=True) * (0.5 / LAMBDA)

    def partial2(k, o):
        b = KB[k]
        rows = slice(o * 256, o * 256 + 256)
        s = nrm[b, rows].astype(F32)
        v = acc2[k, rows] - s * colsq[k]
        if k == 0:
            v = v + (nrm[ylo, rows].astype(F32) - s * dg[0:1, :]) * dg[1:2, :]
        return v * fin[b, 1:2, :]

    def p2_relay(o):
        p2[2, o] = partial2(2, o).astype(BF16)
        return [
            send(M_P2O + 2 * o, p2.at[2, o, top], p2relay.at[o, top], right),
            send(M_P2O + 2 * o + 1, p2.at[2, o, low], p2relay.at[o, low], left),
        ]

    def p2_send(o):
        p2[1, o] = partial2(1, o).astype(BF16)
        a = send(M_P2R + 2 * o, p2.at[1, o, low], p2in.at[0, o, low], right)
        p2[3, o] = partial2(3, o).astype(BF16)
        return [a, send(M_P2L + 2 * o, p2.at[3, o, top], p2in.at[1, o, top], left)]

    def p2_add(o, relay):
        relay[0].wait_recv()
        p2[1, o, top] = (p2[1, o, top].astype(F32) + p2relay[o, top].astype(F32)).astype(BF16)
        a = send(M_P2R + 2 * o + 1, p2.at[1, o, top], p2in.at[0, o, top], right)
        relay[1].wait_recv()
        p2[3, o, low] = (p2[3, o, low].astype(F32) + p2relay[o, low].astype(F32)).astype(BF16)
        return [a, send(M_P2L + 2 * o + 1, p2.at[3, o, low], p2in.at[1, o, low], left)]

    def sent(i, part):
        make(i, part, part, core).wait_send()

    def finish_sends():
        for cp in done:
            cp.wait_send()
        for s in range(8):
            sent(M_C + s, csend.at[s])
        for d in range(2):
            for t in range(1, 5):
                for u in range(2):
                    if t > 1 and (t < 4 or u == d):
                        for s in range(2):
                            sent(M_ZG + zslot(d, t, u) + s, g.at[0, 0, 0])
                    if t < 4 or u == d:
                        sent(M_GD + 4 * t + 2 * d + u, g.at[0, 0, pl.ds(0, 2)])

    done = list(sends)
    relay2 = p2_relay(1)
    in1 += p1_add(0, relay1)
    in2 = p2_send(1)
    relay1, more = p1_start(1, 1 - iz)
    in1 += more
    relay20 = p2_relay(0)
    in2 += p2_add(1, relay2)
    in20 = p2_send(0)
    ob2[0] = partial2(0, 1)
    ob2[1] = partial2(0, 0)
    in1 += p1_add(1, relay1)
    in20 += p2_add(0, relay20)
    finish_sends()
    for cp in in2:
        cp.wait_recv()
    xs[...] = (ob2[0] + p2in[0, 1].astype(F32) + p2in[1, 1].astype(F32)).astype(BF16)
    x_last = send(M_X, xs, xr, sib)
    ob1[0] = partial1(iz, 0)
    ob1[1] = partial1(1 - iz, 0)
    outs = []

    def put(src, ref, col, i):
        cp = pltpu.make_async_copy(src, ref.at[:, pl.ds(pl.multiple_of(col, 256), 256)], os_.at[i])
        cp.start()
        outs.append(cp)

    for cp in in20:
        cp.wait_recv()
    ob2[1] = ob2[1] + p2in[0, 0].astype(F32) + p2in[1, 0].astype(F32)
    put(ob2.at[1], out2, lo, 0)
    for cp in in1:
        cp.wait_recv()
    for ph, e in enumerate((iz, 1 - iz)):
        ob1[ph] = ob1[ph] + p1in[ph, 0].astype(F32) + p1in[ph, 1].astype(F32)
        put(ob1.at[ph], out1, e * 256, 1 + ph)
    x_last.wait_recv()
    ob2[0] = xr[...].astype(F32)
    put(ob2.at[0], out2, hi, 3)
    for cp in outs:
        cp.wait()
    for cp in sends[len(done) :]:
        cp.wait_send()


def write_kernel(a, b, out1, out2, sem):
    cps = []
    for n, (src, dst) in enumerate(((a, out1), (b, out2))):
        for q in range(2):
            rows = pl.ds(128 * q, 128)
            cps.append(pltpu.make_async_copy(src.at[rows], dst.at[rows], sem.at[2 * n + q]))
    for cp in cps:
        cp.start()
    for cp in cps:
        cp.wait()


def body(first, second):
    v = pltpu.VMEM
    out = jax.ShapeDtypeStruct((256, 512), F32)
    anywhere = pl.BlockSpec(memory_space=pl.ANY)
    parts = pl.pallas_call(
        kernel,
        out_shape=(out, out),
        in_specs=[anywhere, anywhere],
        out_specs=(anywhere, anywhere),
        scratch_shapes=[
            v((16, 256, 256), F32),
            v((16, 256, 256), BF16),
            v((8, 256, 256), BF16),
            v((4, 256, 256), BF16),
            v((16, 4, 256), F32),
            v((2, 4, 4, 256), F32),
            v((4, 8, 4, 256), F32),
            v((8, 4, 256), F32),
            v((8, 4, 4, 256), F32),
            v((7, 4, 4, 256), F32),
            v((8, 4, 256), F32),
            v((2, 256), F32),
            v((256, 256), F32),
            v((256, 256), F32),
            v((8, 512, 256), BF16),
            v((8, 256, 256), F32),
            v((8, 256, 256), F32),
            v((8, 512, 256), BF16),
            v((8, 512, 256), BF16),
            v((8, 256, 256), BF16),
            v((8, 256, 256), BF16),
            v((32, 64, 256), BF16),
            v((32, 64, 256), BF16),
            v((2, 8, 4, 64, 256), BF16),
            v((4, 512, 256), F32),
            v((4, 512, 256), F32),
            v((4, 256, 128), F32),
            v((4, 8, 256), F32),
            v((4, 8, 256), F32),
            v((4, 1, 256), F32),
            v((2, 3, 256, 256), BF16),
            v((2, 2, 256, 256), BF16),
            v((2, 256, 256), BF16),
            v((4, 2, 256, 256), BF16),
            v((2, 2, 256, 256), BF16),
            v((2, 256, 256), BF16),
            v((256, 256), BF16),
            v((256, 256), BF16),
            v((2, 256, 256), F32),
            v((2, 256, 256), F32),
            pltpu.SemaphoreType.DMA((M_ALL,)),
            pltpu.SemaphoreType.DMA((M_ALL,)),
            pltpu.SemaphoreType.DMA((16,)),
            pltpu.SemaphoreType.DMA((4,)),
        ],
        compiler_params=pltpu.CompilerParams(
            collective_id=0, has_side_effects=True, vmem_limit_bytes=51 * 1024 * 1024
        ),
    )(first, second)
    return pl.pallas_call(
        write_kernel,
        out_shape=(out, out),
        in_specs=[pl.BlockSpec(memory_space=pltpu.VMEM)] * 2,
        out_specs=(anywhere, anywhere),
        scratch_shapes=[pltpu.SemaphoreType.DMA((4,))],
        compiler_params=pltpu.CompilerParams(vmem_limit_bytes=8 * 1024 * 1024),
    )(*parts)


def solution(mesh):
    return jax.shard_map(
        body,
        mesh=mesh,
        in_specs=(P("dp", None), P("dp", None)),
        out_specs=(P("dp", "replica"), P("dp", "replica")),
        check_vma=False,
    )
```

```python
import jax
import jax.numpy as jnp
from jax import lax
from jax.experimental import pallas as pl
from jax.experimental.pallas import tpu as pltpu
from jax.sharding import PartitionSpec as P

LAMBDA = 0.0051
EPS = 1e-05
MESH = pl.DeviceIdType.MESH
F32 = jnp.float32
BF16 = jnp.bfloat16
BATCH = 8192

OWN = (0, 1, 4, 5, 2, 3, 6, 7)
STAT_SIB = (0, 1, 8, 9)
STAT_NON = (0, 1, 14, 15)
KB = (2, 3, 6, 7)
AB = (0, 1, 4, 5)

M_Y = 0
M_ST1 = 12
M_ST2 = 17
M_ST3 = 24
M_C = 31
M_YP = 39
M_ZR = 55
M_ZG = 87
M_GD = 119
M_P1 = 139
M_P2O = 151
M_P2R = 155
M_P2L = 159
M_X = 163
M_ALL = 164

HIGH = lax.Precision.HIGHEST


def nt(a, b, precision=None):
    return lax.dot_general(
        a, b, (((1,), (1,)), ((), ())), preferred_element_type=F32, precision=precision
    )


def tn(a, b, precision=None):
    return lax.dot_general(
        a, b, (((0,), (0,)), ((), ())), preferred_element_type=F32, precision=precision
    )


def nn(a, b):
    return lax.dot_general(a, b, (((1,), (0,)), ((), ())), preferred_element_type=F32)


def ab(a):
    return a + 2 * lax.div(a, 2)


def kb(k):
    return k + 2 + 2 * lax.div(k, 2)


def kernel(
    first, second, out1, out2,
    raw, cen, oth, xt, stat, smsg, st1, pst, st2m, st2, fin, dg, scl, fix, nrm, cown, ypart, csend, crecv, ys, yr, zs, zr, g,
    acc1, acc2, rsq, csq, rowsq, colsq,
    p1, p1in, p1relay, p2, p2in, p2relay, xs, xr, ob1, ob2, ss, rs, ls, os_,
):
    dp = lax.axis_index("dp")
    rep = lax.axis_index("replica")
    c = lax.rem(dp, 2)
    ylo = lax.rem(lax.div(dp, 2), 2)
    z = lax.div(dp, 4)
    yhi = lax.div(rep, 4)
    x = lax.rem(rep, 4)

    def dev(x_, yhi_, ylo_, z_, c_):
        return (z_ * 4 + ylo_ * 2 + c_, yhi_ * 4 + x_)

    core = dev(x, yhi, ylo, z, 1 - c)
    sib = dev(x, yhi, 1 - ylo, z, c)
    sibc = dev(x, yhi, 1 - ylo, z, 1 - c)
    non = dev(x, 1 - yhi, 1 - ylo, z, c)
    nonc = dev(x, 1 - yhi, 1 - ylo, z, 1 - c)
    right = dev(lax.rem(x + 1, 4), yhi, ylo, z, c)
    left = dev(lax.rem(x + 3, 4), yhi, ylo, z, c)
    zdev = [dev(x, yhi, ylo, lax.rem(z + q, 8), c) for q in range(8)]
    zto = (zdev[1], zdev[7])

    def load(i, ref, col):
        return pltpu.make_async_copy(
            ref.at[:, pl.ds(pl.multiple_of(col, 256), 256)], raw.at[i], ls.at[i]
        )

    kz = lax.rem(z, 4)
    iz = lax.div(z, 4)
    base = yhi * 2048
    other = 2048 - base
    mine = x * 512
    lo = ylo * 256
    hi = 256 - lo
    def load_first(e):
        for j in range(2):
            load(2 * j + e, first, (base, other)[j] + mine + 256 * e).start()

    def load_second(k):
        piece = lax.rem(x + k, 4) * 512
        for m, col in enumerate((base + lo, base + hi, other + hi)):
            load(4 + 4 * m + k, second, col + piece).start()

    load_first(1 - iz)
    load_second(kz)
    barrier = pltpu.get_barrier_semaphore()
    partners = [core, sib, sibc, non, nonc, right, left] + zdev[1:]
    for d in partners:
        pl.semaphore_signal(barrier, inc=1, device_id=d, device_id_type=MESH)
    load_first(iz)
    for n in (3, 1, 2):
        load_second(lax.rem(kz + n, 4))

    def make(i, src, dst, to):
        return pltpu.make_async_remote_copy(
            src_ref=src, dst_ref=dst, send_sem=ss.at[i], recv_sem=rs.at[i], device_id=to, device_id_type=MESH
        )

    sends = []

    def send(i, src, dst, to):
        cp = make(i, src, dst, to)
        cp.start()
        sends.append(cp)
        return cp

    def local_stats(i, carry):
        pltpu.make_async_copy(first.at[:, pl.ds(0, 256)], raw.at[i], ls.at[i]).wait()
        v = raw[i]
        m = jnp.sum(v, 0, keepdims=True) * (1.0 / 256)
        dv = v - m
        r = dv.astype(BF16)
        cen[i] = r
        stat[i, 0:1, :] = m
        stat[i, 1:2, :] = jnp.sum(dv * dv, 0, keepdims=True)
        stat[i, 2:3, :] = jnp.sum(r.astype(F32), 0, keepdims=True)
        stat[i, 3:4, :] = jnp.zeros_like(m)
        return carry

    top, low = pl.ds(0, 128), pl.ds(128, 128)

    def blocks_k(m, carry):
        return local_stats(4 + 4 * lax.rem(m, 3) + lax.rem(kz + lax.div(m, 3), 4), carry)

    def first_blocks(e):
        def one(j, carry):
            local_stats(2 * j + e, carry)
            xt[2 * j + e] = cen[2 * j + e].T
            return carry

        lax.fori_loop(0, 2, one, 0)

    first_blocks(1 - iz)
    lax.fori_loop(0, 3, blocks_k, 0)
    pl.semaphore_wait(barrier, len(partners))

    def corr(s, carry):
        r = jnp.where(lax.rem(s, 2) == 1, 4 - lax.div(s + 1, 2), 4 + lax.div(s, 2))
        d = lax.rem(z + r, 8)
        i = lax.div(d, 4)
        k = lax.rem(d, 4)
        a = 2 * (1 - c) + i
        b = 2 * c + i
        v = nn(jnp.concatenate([xt[a], xt[b]], 0), cen[4 + k])
        csend[s, 0:256] = v[0:256].astype(BF16)
        cown[s] = v[256:512]
        v = nn(jnp.concatenate([xt[a, top], xt[b, top]], 0), cen[8 + k])
        csend[s, 256:384] = v[0:128].astype(BF16)
        ypart[s, 0:128] = v[128:256]
        v = nn(jnp.concatenate([xt[b, low], xt[a, low]], 0), cen[12 + k])
        csend[s, 384:512] = v[0:128].astype(BF16)
        ypart[s, 128:256] = v[128:256]
        make(M_C + s, csend.at[s], crecv.at[s], core).start()
        return carry

    y_sum = []

    def to_y(s):
        make(M_C + s, csend.at[s], crecv.at[s], core).wait_recv()
        ys[s] = (ypart[s] + crecv[s, 256:512].astype(F32)).astype(BF16)
        y_sum.append(
            (
                send(M_YP + 2 * s, ys.at[s, top], yr.at[s, top], sib),
                send(M_YP + 2 * s + 1, ys.at[s, low], yr.at[s, low], non),
            )
        )

    corr(0, 0)
    first_blocks(iz)
    lax.fori_loop(3, 12, blocks_k, 0)
    def zslot(d, t, u):
        return d * 16 + (t - 1) * 4 + u * 2

    z_in = {}

    def chain(t, far):
        dist = 5 - t
        slot = (7 - 2 * dist, 8 - 2 * dist) if dist < 4 else (0, 0)
        if (t, far) in ((1, True), (2, False), (3, False), (4, False)):
            for n in set(slot):
                for cp in y_sum[n]:
                    cp.wait_recv()
        for s in range(2):
            for d in range(2):
                u = d if far else 1 - d
                n = slot[d]
                rows = slice(128 * u + 64 * s, 128 * u + 64 * s + 64)
                v = cown[n, rows] + crecv[n, rows].astype(F32) + yr[n, rows].astype(F32)
                if (d, t - 1, u, s) in z_in:
                    z_in[(d, t - 1, u, s)].wait_recv()
                    v = v + zr[zslot(d, t - 1, u) + s].astype(F32)
                i = zslot(d, t, u) + s
                zs[i] = v.astype(BF16)
                z_in[(d, t, u, s)] = send(M_ZR + i, zs.at[i], zr.at[i], zto[d])

    def comoment(i, j):
        return jnp.sum((raw[i] - stat[i, 0:1, :]) * (raw[j] - stat[j, 0:1, :]), 0, keepdims=True)

    for n in range(4):
        smsg[0, n] = stat[STAT_SIB[n]]
        smsg[1, n] = stat[STAT_NON[n]]
    for b in range(8):
        st1[0, b] = stat[OWN[b]]
    smsg[0, 1 - ylo, 3:4, :] = comoment(1 - ylo, 8)
    st1[0, ylo, 3:4, :] = comoment(ylo, 4)
    st_in = [
        send(M_ST1 + 0, smsg.at[0], st1.at[2, pl.ds(0, 4)], sib),
        send(M_ST1 + 1, smsg.at[1], st1.at[2, pl.ds(4, 4)], non),
        send(M_ST1 + 2, smsg.at[0], st1.at[3, pl.ds(0, 4)], sibc),
        send(M_ST1 + 3, smsg.at[1], st1.at[3, pl.ds(4, 4)], nonc),
        send(M_ST1 + 4, st1.at[0], st1.at[1], core),
    ]
    to_y(0)
    lax.fori_loop(1, 5, corr, 0)
    to_y(1)
    to_y(2)
    for cp in st_in:
        cp.wait_recv()

    def merge(rows, count):
        total = sum(rows[1:], rows[0])
        m = total[0:1] * (1.0 / len(rows))
        dv = [r[0:1] - m for r in rows]
        m2 = total[1:2] + count * sum([d * d for d in dv[1:]], dv[0] * dv[0])
        return m, m2, total[2:3], total[3:4], dv

    def cross(p, q):
        return sum([a * b for a, b in zip(p[1:], q[1:])], p[0] * q[0])

    merged = [merge([st1[s, b] for s in range(4)], 256.0) for b in range(8)]
    for b, (m, m2, r, co, dv) in enumerate(merged):
        if b < 2:
            co = co + 256.0 * cross(dv, merged[2][4])
        for n, row in enumerate((m, m2, r, co)):
            pst[b, n : n + 1, :] = row
    st2_in = []
    for q in range(8):
        zq = lax.rem(z + q, 8)
        fa = ab(2 * c + lax.div(zq, 4))
        fk = kb(lax.rem(zq, 4))
        st2m[q, 0] = pst[zq]
        st2m[q, 3] = pst[2]
        for s in range(4):
            st2m[q, 1, s : s + 1, :] = st1[s, fa, 0:1, :]
            st2m[q, 2, s : s + 1, :] = st1[s, fk, 0:1, :]
        if q:
            st2_in.append(send(M_ST2 + q - 1, st2m.at[q], st2.at[q - 1], zdev[q]))

    to_y(3)
    to_y(4)
    x_in = [
        send(M_Y + 0, cen.at[8, top], oth.at[2, top], sib),
        send(M_Y + 1, cen.at[12, low], oth.at[2, low], non),
    ]
    chain(1, True)

    lax.fori_loop(5, 8, corr, 0)
    chain(2, False)
    to_y(5)
    to_y(6)
    to_y(7)
    x_in += [
        send(M_Y + 2, cen.at[0], oth.at[0], sib),
        send(M_Y + 3, cen.at[0], oth.at[4], non),
        send(M_Y + 4, cen.at[1], oth.at[1], sib),
        send(M_Y + 5, cen.at[1], oth.at[5], non),
    ]
    chain(2, True)

    def zero(n, carry):
        acc1[n] = jnp.zeros((512, 256), F32)
        acc2[n] = jnp.zeros((512, 256), F32)
        return carry

    lax.fori_loop(0, 4, zero, 0)
    rsq[...] = jnp.zeros_like(rsq)
    csq[...] = jnp.zeros_like(csq)
    x_in[0].wait_recv()
    x_in[1].wait_recv()
    x_ring = [
        send(M_Y + 6, oth.at[2], oth.at[3], left),
        send(M_Y + 7, oth.at[2], oth.at[7], right),
    ]
    for cp in st2_in:
        cp.wait_recv()
    st2m_all = [st2m[0, 0]] + [st2[s, 0] for s in range(7)]
    k0_means = [st2m[0, 3]] + [st2[s, 3] for s in range(7)]
    m, m2, r, co, dv = merge(st2m_all, 1024.0)
    k0_dv = merge(k0_means, 1024.0)[4]
    fin[z, 0:1, :] = m + r * (1.0 / BATCH)
    fin[z, 1:2, :] = lax.rsqrt(m2 * (1.0 / BATCH) + EPS)
    fin[z, 2:3, :] = m
    fin[z, 3:4, :] = co + 1024.0 * cross(dv, k0_dv)
    fin_in = [send(M_ST3 + q - 1, fin.at[z], fin.at[z], zdev[q]) for q in range(1, 8)]

    chain(3, False)

    chain(3, True)

    def norm(b, o):
        shift = st1[2 * o, b, 0:1, :] - fin[b, 0:1, :]
        scale = fin[b, 1:2, :]
        q = lax.rem(b, 4)
        idx = jnp.where(q < 2, 0, 2) + q + 2 * lax.div(b, 4)
        for h in range(2):
            rows = slice(128 * h, 128 * h + 128)
            v = cen[idx, rows] if o == 0 else oth[b, rows]
            nrm[b, o * 256 + 128 * h : o * 256 + 128 * h + 128, :] = ((v.astype(F32) + shift) * scale).astype(BF16)

    def norms(o):
        lax.fori_loop(0, 8, lambda b, carry: (norm(b, o), carry)[1], 0)

    x_ring[0].wait_recv()
    x_ring.append(send(M_Y + 8, oth.at[3, top], oth.at[6, top], left))
    x_ring[1].wait_recv()
    x_ring.append(send(M_Y + 9, oth.at[7, low], oth.at[6, low], right))
    chain(4, False)
    for cp in fin_in:
        cp.wait_recv()
    cii = fin[ylo, 3:4, :] * fin[ylo, 1:2, :] * fin[2, 1:2, :] * (1.0 / BATCH)
    dg[0:1, :] = cii
    dg[1:2, :] = (-2.0 * (1.0 - cii)).astype(BF16).astype(F32)
    norms(0)
    chain(4, True)

    fa = ab(2 * c + lax.div(z, 4))
    fk = kb(lax.rem(z, 4))
    pad = jnp.zeros((7, 256), F32)
    ra = jnp.concatenate([fin[fa, 1:2, :] * (2.0 * LAMBDA / BATCH), pad], 0)
    rk = jnp.concatenate([fin[fk, 1:2, :], pad], 0)
    rows_id = lax.broadcasted_iota(jnp.int32, (256, 256), 0)
    cols_id = lax.broadcasted_iota(jnp.int32, (256, 256), 1)
    off = rows_id + jnp.where((c == 0) & (z == 4 * ylo), 0, 512) != cols_id
    scl[...] = jnp.where(off, tn(ra, rk, HIGH), 0.0)
    mu_a = [(st2m[0, 1] if s == 0 else st2[s - 1, 1]) - fin[fa, 2:3, :] for s in range(8)]
    mu_k = [(st2m[0, 2] if s == 0 else st2[s - 1, 2]) - fin[fk, 2:3, :] for s in range(8)]
    fix[...] = scl[...] * tn(jnp.concatenate(mu_a, 0) * 256.0, jnp.concatenate(mu_k, 0), HIGH)

    for cp in y_sum[7]:
        cp.wait_recv()
    for s in range(2):
        for u in range(2):
            q = 2 * u + s
            rows = slice(64 * q, 64 * q + 64)
            v = cown[7, rows] + crecv[7, rows].astype(F32) + yr[7, rows].astype(F32)
            for d in (1 - u, u):
                z_in[(d, 4, u, s)].wait_recv()
                v = v + zr[zslot(d, 4, u) + s].astype(F32)
            part = g.at[c, z, q]
            g[c, z, q] = (v * scl[rows] + fix[rows]).astype(BF16)
            for d in (u, 1 - u):
                send(M_ZG + zslot(d, 1, u) + s, part, part, zto[d])
    send(M_GD + 0, g.at[c, z, pl.ds(0, 2)], g.at[c, z, pl.ds(0, 2)], core)
    send(M_GD + 1, g.at[c, z, pl.ds(2, 2)], g.at[c, z, pl.ds(2, 2)], core)

    def arrive(t, far, onward):
        for s in range(2):
            for d in range(2):
                u = d if far else 1 - d
                i = d * 16 + (t - 1) * 4 + u * 2 + s
                source = lax.rem(z + (8 - t if d == 0 else t), 8)
                part = g.at[c, source, 2 * u + s]
                make(M_ZG + i, part, part, zto[d]).wait_recv()
                if onward is not None:
                    start = make(M_ZG + i + 4, part, part, zto[d]).start
                    if onward is True:
                        start()
                    else:
                        pl.when(onward)(start)
                if s == 1:
                    both = g.at[c, source, pl.ds(2 * u, 2)]
                    make(M_GD + 4 * t + 2 * d + u, both, both, core).start()

    def use(zs_):
        i = lax.div(zs_, 4)
        k = lax.rem(zs_, 4)
        ga = jnp.concatenate([g[0, zs_].reshape(256, 256), g[1, zs_].reshape(256, 256)], 0)
        v = nt(nrm[kb(k)], ga)
        acc1[i] += v[:, 0:256]
        acc1[2 + i] += v[:, 256:512]
        acc2[k] += nn(jnp.concatenate([nrm[i], nrm[4 + i]], 1), ga)
        v = ga.astype(F32)
        s = v * v
        part = s[:, 0:128] + s[:, 128:256]
        rsq[i] += part[0:256]
        rsq[2 + i] += part[256:512]
        csq[k] += jnp.sum(s.reshape(64, 8, 256), 0)

    def from_core(t, d, u):
        part = g.at[0, 0, pl.ds(0, 2)]
        make(M_GD + 4 * t + 2 * d + u, part, part, core).wait_recv()

    def uses(t, n):
        for u in range(2):
            from_core(t, n, u)
        use(lax.rem(z + (8 - t) + n * 2 * t, 8))

    arrive(1, True, True)
    arrive(1, False, True)
    for cp in x_in[2:] + x_ring[2:]:
        cp.wait_recv()
    norms(1)
    uses(0, 0)

    def step(t, carry):
        arrive(t, True, True)
        uses(t - 1, 0)
        arrive(t, False, t < 3)
        uses(t - 1, 1)
        return carry

    def partial1(a, o):
        b = ab(a)
        rows = slice(o * 256, o * 256 + 256)
        f = nrm[b, rows].astype(F32)
        v = acc1[a, rows] - f * rowsq[a, 0:1, :]
        gd = jnp.where(a == ylo, dg[1:2, :], 0.0)
        v = v + (nrm[2, rows].astype(F32) - f * dg[0:1, :]) * gd
        return v * fin[b, 1:2, :]

    def p1_start(ph, e):
        for a in (e, 2 + e):
            rowsq[a] = nt(jnp.ones((8, 128), F32), rsq[a], HIGH) * (0.5 / LAMBDA)
        m = M_P1 + 6 * ph
        p1[ph, 0] = partial1(2 + e, 0).astype(BF16)
        relay = [
            send(m, p1.at[ph, 0, top], p1relay.at[ph, top], sib),
            send(m + 1, p1.at[ph, 0, low], p1relay.at[ph, low], non),
        ]
        p1[ph, 1] = partial1(2 + e, 1).astype(BF16)
        a = send(m + 2, p1.at[ph, 1, low], p1in.at[ph, 1, low], non)
        p1[ph, 2] = partial1(e, 1).astype(BF16)
        b = send(m + 3, p1.at[ph, 2, top], p1in.at[ph, 0, top], sib)
        return relay, [a, b]

    def p1_add(ph, relay):
        m = M_P1 + 6 * ph
        relay[0].wait_recv()
        p1[ph, 1, top] = (p1[ph, 1, top].astype(F32) + p1relay[ph, top].astype(F32)).astype(BF16)
        a = send(m + 4, p1.at[ph, 1, top], p1in.at[ph, 1, top], non)
        relay[1].wait_recv()
        p1[ph, 2, low] = (p1[ph, 2, low].astype(F32) + p1relay[ph, low].astype(F32)).astype(BF16)
        return [a, send(m + 5, p1.at[ph, 2, low], p1in.at[ph, 0, low], sib)]

    lax.fori_loop(2, 4, step, 0)
    lax.fori_loop(0, 2, lambda n, carry: (uses(3, n), carry)[1], 0)
    relay1, in1 = p1_start(0, iz)
    arrive(4, True, None)
    from_core(4, 0, 0)
    from_core(4, 1, 1)
    use(lax.rem(z + 4, 8))

    for k in range(4):
        colsq[k] = jnp.sum(csq[k], 0, keepdims=True) * (0.5 / LAMBDA)

    def partial2(k, o):
        b = KB[k]
        rows = slice(o * 256, o * 256 + 256)
        s = nrm[b, rows].astype(F32)
        v = acc2[k, rows] - s * colsq[k]
        if k == 0:
            v = v + (nrm[ylo, rows].astype(F32) - s * dg[0:1, :]) * dg[1:2, :]
        return v * fin[b, 1:2, :]

    def p2_relay(o):
        p2[2, o] = partial2(2, o).astype(BF16)
        return [
            send(M_P2O + 2 * o, p2.at[2, o, top], p2relay.at[o, top], right),
            send(M_P2O + 2 * o + 1, p2.at[2, o, low], p2relay.at[o, low], left),
        ]

    def p2_send(o):
        p2[1, o] = partial2(1, o).astype(BF16)
        a = send(M_P2R + 2 * o, p2.at[1, o, low], p2in.at[0, o, low], right)
        p2[3, o] = partial2(3, o).astype(BF16)
        return [a, send(M_P2L + 2 * o, p2.at[3, o, top], p2in.at[1, o, top], left)]

    def p2_add(o, relay):
        relay[0].wait_recv()
        p2[1, o, top] = (p2[1, o, top].astype(F32) + p2relay[o, top].astype(F32)).astype(BF16)
        a = send(M_P2R + 2 * o + 1, p2.at[1, o, top], p2in.at[0, o, top], right)
        relay[1].wait_recv()
        p2[3, o, low] = (p2[3, o, low].astype(F32) + p2relay[o, low].astype(F32)).astype(BF16)
        return [a, send(M_P2L + 2 * o + 1, p2.at[3, o, low], p2in.at[1, o, low], left)]

    def sent(i, part):
        make(i, part, part, core).wait_send()

    def finish_sends():
        for cp in done:
            cp.wait_send()
        for s in range(8):
            sent(M_C + s, csend.at[s])
        for d in range(2):
            for t in range(1, 5):
                for u in range(2):
                    if t > 1 and (t < 4 or u == d):
                        for s in range(2):
                            sent(M_ZG + zslot(d, t, u) + s, g.at[0, 0, 0])
                    if t < 4 or u == d:
                        sent(M_GD + 4 * t + 2 * d + u, g.at[0, 0, pl.ds(0, 2)])

    done = list(sends)
    relay2 = p2_relay(1)
    in1 += p1_add(0, relay1)
    in2 = p2_send(1)
    relay1, more = p1_start(1, 1 - iz)
    in1 += more
    relay20 = p2_relay(0)
    in2 += p2_add(1, relay2)
    in20 = p2_send(0)
    ob2[0] = partial2(0, 1)
    ob2[1] = partial2(0, 0)
    in1 += p1_add(1, relay1)
    in20 += p2_add(0, relay20)
    finish_sends()
    for cp in in2:
        cp.wait_recv()
    xs[...] = (ob2[0] + p2in[0, 1].astype(F32) + p2in[1, 1].astype(F32)).astype(BF16)
    x_last = send(M_X, xs, xr, sib)
    ob1[0] = partial1(iz, 0)
    ob1[1] = partial1(1 - iz, 0)
    outs = []

    def put(src, ref, col, i):
        cp = pltpu.make_async_copy(src, ref.at[:, pl.ds(pl.multiple_of(col, 256), 256)], os_.at[i])
        cp.start()
        outs.append(cp)

    for cp in in20:
        cp.wait_recv()
    ob2[1] = ob2[1] + p2in[0, 0].astype(F32) + p2in[1, 0].astype(F32)
    put(ob2.at[1], out2, lo, 0)
    for cp in in1:
        cp.wait_recv()
    for ph, e in enumerate((iz, 1 - iz)):
        ob1[ph] = ob1[ph] + p1in[ph, 0].astype(F32) + p1in[ph, 1].astype(F32)
        put(ob1.at[ph], out1, e * 256, 1 + ph)
    x_last.wait_recv()
    ob2[0] = xr[...].astype(F32)
    put(ob2.at[0], out2, hi, 3)
    for cp in outs:
        cp.wait()
    for cp in sends[len(done) :]:
        cp.wait_send()


def write_kernel(a, b, out1, out2, sem):
    cps = []
    for n, (src, dst) in enumerate(((a, out1), (b, out2))):
        for q in range(2):
            rows = pl.ds(128 * q, 128)
            cps.append(pltpu.make_async_copy(src.at[rows], dst.at[rows], sem.at[2 * n + q]))
    for cp in cps:
        cp.start()
    for cp in cps:
        cp.wait()


def body(first, second):
    v = pltpu.VMEM
    out = jax.ShapeDtypeStruct((256, 512), F32)
    anywhere = pl.BlockSpec(memory_space=pl.ANY)
    parts = pl.pallas_call(
        kernel,
        out_shape=(out, out),
        in_specs=[anywhere, anywhere],
        out_specs=(anywhere, anywhere),
        scratch_shapes=[
            v((16, 256, 256), F32),
            v((16, 256, 256), BF16),
            v((8, 256, 256), BF16),
            v((4, 256, 256), BF16),
            v((16, 4, 256), F32),
            v((2, 4, 4, 256), F32),
            v((4, 8, 4, 256), F32),
            v((8, 4, 256), F32),
            v((8, 4, 4, 256), F32),
            v((7, 4, 4, 256), F32),
            v((8, 4, 256), F32),
            v((2, 256), F32),
            v((256, 256), F32),
            v((256, 256), F32),
            v((8, 512, 256), BF16),
            v((8, 256, 256), F32),
            v((8, 256, 256), F32),
            v((8, 512, 256), BF16),
            v((8, 512, 256), BF16),
            v((8, 256, 256), BF16),
            v((8, 256, 256), BF16),
            v((32, 64, 256), BF16),
            v((32, 64, 256), BF16),
            v((2, 8, 4, 64, 256), BF16),
            v((4, 512, 256), F32),
            v((4, 512, 256), F32),
            v((4, 256, 128), F32),
            v((4, 8, 256), F32),
            v((4, 8, 256), F32),
            v((4, 1, 256), F32),
            v((2, 3, 256, 256), BF16),
            v((2, 2, 256, 256), BF16),
            v((2, 256, 256), BF16),
            v((4, 2, 256, 256), BF16),
            v((2, 2, 256, 256), BF16),
            v((2, 256, 256), BF16),
            v((256, 256), BF16),
            v((256, 256), BF16),
            v((2, 256, 256), F32),
            v((2, 256, 256), F32),
            pltpu.SemaphoreType.DMA((M_ALL,)),
            pltpu.SemaphoreType.DMA((M_ALL,)),
            pltpu.SemaphoreType.DMA((16,)),
            pltpu.SemaphoreType.DMA((4,)),
        ],
        compiler_params=pltpu.CompilerParams(
            collective_id=0, has_side_effects=True, vmem_limit_bytes=51 * 1024 * 1024
        ),
    )(first, second)
    return pl.pallas_call(
        write_kernel,
        out_shape=(out, out),
        in_specs=[pl.BlockSpec(memory_space=pltpu.VMEM)] * 2,
        out_specs=(anywhere, anywhere),
        scratch_shapes=[pltpu.SemaphoreType.DMA((4,))],
        compiler_params=pltpu.CompilerParams(vmem_limit_bytes=8 * 1024 * 1024),
    )(*parts)


def solution(mesh):
    return jax.shard_map(
        body,
        mesh=mesh,
        in_specs=(P("dp", None), P("dp", None)),
        out_specs=(P("dp", "replica"), P("dp", "replica")),
        check_vma=False,
    )
```

```python
import jax
import jax.numpy as jnp
from jax import lax
from jax.experimental import pallas as pl
from jax.experimental.pallas import tpu as pltpu
from jax.sharding import PartitionSpec as P

LAMBDA = 0.0051
EPS = 1e-05
MESH = pl.DeviceIdType.MESH
F32 = jnp.float32
BF16 = jnp.bfloat16
BATCH = 8192

OWN = (0, 1, 4, 5, 2, 3, 6, 7)
STAT_SIB = (0, 1, 8, 9)
STAT_NON = (0, 1, 14, 15)
KB = (2, 3, 6, 7)
AB = (0, 1, 4, 5)

M_Y = 0
M_ST1 = 12
M_ST2 = 17
M_ST3 = 24
M_C = 31
M_YP = 39
M_ZR = 55
M_ZG = 87
M_GD = 119
M_P1 = 139
M_P2O = 151
M_P2R = 155
M_P2L = 159
M_X = 163
M_ALL = 164

HIGH = lax.Precision.HIGHEST


def nt(a, b, precision=None):
    return lax.dot_general(
        a, b, (((1,), (1,)), ((), ())), preferred_element_type=F32, precision=precision
    )


def tn(a, b, precision=None):
    return lax.dot_general(
        a, b, (((0,), (0,)), ((), ())), preferred_element_type=F32, precision=precision
    )


def nn(a, b):
    return lax.dot_general(a, b, (((1,), (0,)), ((), ())), preferred_element_type=F32)


def ab(a):
    return a + 2 * lax.div(a, 2)


def kb(k):
    return k + 2 + 2 * lax.div(k, 2)


def kernel(
    first, second, out1, out2,
    raw, cen, oth, xt, stat, smsg, st1, pst, st2m, st2, fin, dg, scl, fix, nrm, cown, ypart, csend, crecv, ys, yr, zs, zr, g,
    acc1, acc2, rsq, csq, rowsq, colsq,
    p1, p1in, p1relay, p2, p2in, p2relay, xs, xr, ob1, ob2, ss, rs, ls, os_,
):
    dp = lax.axis_index("dp")
    rep = lax.axis_index("replica")
    c = lax.rem(dp, 2)
    ylo = lax.rem(lax.div(dp, 2), 2)
    z = lax.div(dp, 4)
    yhi = lax.div(rep, 4)
    x = lax.rem(rep, 4)

    def dev(x_, yhi_, ylo_, z_, c_):
        return (z_ * 4 + ylo_ * 2 + c_, yhi_ * 4 + x_)

    core = dev(x, yhi, ylo, z, 1 - c)
    sib = dev(x, yhi, 1 - ylo, z, c)
    sibc = dev(x, yhi, 1 - ylo, z, 1 - c)
    non = dev(x, 1 - yhi, 1 - ylo, z, c)
    nonc = dev(x, 1 - yhi, 1 - ylo, z, 1 - c)
    right = dev(lax.rem(x + 1, 4), yhi, ylo, z, c)
    left = dev(lax.rem(x + 3, 4), yhi, ylo, z, c)
    zdev = [dev(x, yhi, ylo, lax.rem(z + q, 8), c) for q in range(8)]
    zto = (zdev[1], zdev[7])

    def load(i, ref, col):
        return pltpu.make_async_copy(
            ref.at[:, pl.ds(pl.multiple_of(col, 256), 256)], raw.at[i], ls.at[i]
        )

    kz = lax.rem(z, 4)
    iz = lax.div(z, 4)
    base = yhi * 2048
    other = 2048 - base
    mine = x * 512
    lo = ylo * 256
    hi = 256 - lo
    def load_first(e):
        for j in range(2):
            load(2 * j + e, first, (base, other)[j] + mine + 256 * e).start()

    def load_second(k):
        piece = lax.rem(x + k, 4) * 512
        for m, col in enumerate((base + lo, base + hi, other + hi)):
            load(4 + 4 * m + k, second, col + piece).start()

    load_first(1 - iz)
    load_second(kz)
    barrier = pltpu.get_barrier_semaphore()
    partners = [core, sib, sibc, non, nonc, right, left] + zdev[1:]
    for d in partners:
        pl.semaphore_signal(barrier, inc=1, device_id=d, device_id_type=MESH)
    load_first(iz)
    for n in (3, 1, 2):
        load_second(lax.rem(kz + n, 4))

    def make(i, src, dst, to):
        return pltpu.make_async_remote_copy(
            src_ref=src, dst_ref=dst, send_sem=ss.at[i], recv_sem=rs.at[i], device_id=to, device_id_type=MESH
        )

    sends = []

    def send(i, src, dst, to):
        cp = make(i, src, dst, to)
        cp.start()
        sends.append(cp)
        return cp

    def local_stats(i, carry):
        pltpu.make_async_copy(first.at[:, pl.ds(0, 256)], raw.at[i], ls.at[i]).wait()
        v = raw[i]
        m = jnp.sum(v, 0, keepdims=True) * (1.0 / 256)
        dv = v - m
        r = dv.astype(BF16)
        cen[i] = r
        stat[i, 0:1, :] = m
        stat[i, 1:2, :] = jnp.sum(dv * dv, 0, keepdims=True)
        stat[i, 2:3, :] = jnp.sum(r.astype(F32), 0, keepdims=True)
        stat[i, 3:4, :] = jnp.zeros_like(m)
        return carry

    top, low = pl.ds(0, 128), pl.ds(128, 128)

    def blocks_k(m, carry):
        return local_stats(4 + 4 * lax.rem(m, 3) + lax.rem(kz + lax.div(m, 3), 4), carry)

    def first_blocks(e):
        def one(j, carry):
            local_stats(2 * j + e, carry)
            xt[2 * j + e] = cen[2 * j + e].T
            return carry

        lax.fori_loop(0, 2, one, 0)

    first_blocks(1 - iz)
    lax.fori_loop(0, 3, blocks_k, 0)
    pl.semaphore_wait(barrier, len(partners))

    def corr(s, carry):
        r = jnp.where(lax.rem(s, 2) == 1, 4 - lax.div(s + 1, 2), 4 + lax.div(s, 2))
        d = lax.rem(z + r, 8)
        i = lax.div(d, 4)
        k = lax.rem(d, 4)
        a = 2 * (1 - c) + i
        b = 2 * c + i
        v = nn(jnp.concatenate([xt[a], xt[b]], 0), cen[4 + k])
        csend[s, 0:256] = v[0:256].astype(BF16)
        cown[s] = v[256:512]
        v = nn(jnp.concatenate([xt[a, top], xt[b, top]], 0), cen[8 + k])
        csend[s, 256:384] = v[0:128].astype(BF16)
        ypart[s, 0:128] = v[128:256]
        v = nn(jnp.concatenate([xt[b, low], xt[a, low]], 0), cen[12 + k])
        csend[s, 384:512] = v[0:128].astype(BF16)
        ypart[s, 128:256] = v[128:256]
        make(M_C + s, csend.at[s], crecv.at[s], core).start()
        return carry

    y_sum = []

    def to_y(s):
        make(M_C + s, csend.at[s], crecv.at[s], core).wait_recv()
        ys[s] = (ypart[s] + crecv[s, 256:512].astype(F32)).astype(BF16)
        y_sum.append(
            (
                send(M_YP + 2 * s, ys.at[s, top], yr.at[s, top], sib),
                send(M_YP + 2 * s + 1, ys.at[s, low], yr.at[s, low], non),
            )
        )

    corr(0, 0)
    first_blocks(iz)
    lax.fori_loop(3, 12, blocks_k, 0)
    def zslot(d, t, u):
        return d * 16 + (t - 1) * 4 + u * 2

    z_in = {}

    def chain(t, far):
        dist = 5 - t
        slot = (7 - 2 * dist, 8 - 2 * dist) if dist < 4 else (0, 0)
        if (t, far) in ((1, True), (2, False), (3, False), (4, False)):
            for n in set(slot):
                for cp in y_sum[n]:
                    cp.wait_recv()
        for s in range(2):
            for d in range(2):
                u = d if far else 1 - d
                n = slot[d]
                rows = slice(128 * u + 64 * s, 128 * u + 64 * s + 64)
                v = cown[n, rows] + crecv[n, rows].astype(F32) + yr[n, rows].astype(F32)
                if (d, t - 1, u, s) in z_in:
                    z_in[(d, t - 1, u, s)].wait_recv()
                    v = v + zr[zslot(d, t - 1, u) + s].astype(F32)
                i = zslot(d, t, u) + s
                zs[i] = v.astype(BF16)
                z_in[(d, t, u, s)] = send(M_ZR + i, zs.at[i], zr.at[i], zto[d])

    def comoment(i, j):
        return jnp.sum((raw[i] - stat[i, 0:1, :]) * (raw[j] - stat[j, 0:1, :]), 0, keepdims=True)

    for n in range(4):
        smsg[0, n] = stat[STAT_SIB[n]]
        smsg[1, n] = stat[STAT_NON[n]]
    for b in range(8):
        st1[0, b] = stat[OWN[b]]
    smsg[0, 1 - ylo, 3:4, :] = comoment(1 - ylo, 8)
    st1[0, ylo, 3:4, :] = comoment(ylo, 4)
    st_in = [
        send(M_ST1 + 0, smsg.at[0], st1.at[2, pl.ds(0, 4)], sib),
        send(M_ST1 + 1, smsg.at[1], st1.at[2, pl.ds(4, 4)], non),
        send(M_ST1 + 2, smsg.at[0], st1.at[3, pl.ds(0, 4)], sibc),
        send(M_ST1 + 3, smsg.at[1], st1.at[3, pl.ds(4, 4)], nonc),
        send(M_ST1 + 4, st1.at[0], st1.at[1], core),
    ]
    to_y(0)
    lax.fori_loop(1, 5, corr, 0)
    to_y(1)
    to_y(2)
    for cp in st_in:
        cp.wait_recv()

    def merge(rows, count):
        total = sum(rows[1:], rows[0])
        m = total[0:1] * (1.0 / len(rows))
        dv = [r[0:1] - m for r in rows]
        m2 = total[1:2] + count * sum([d * d for d in dv[1:]], dv[0] * dv[0])
        return m, m2, total[2:3], total[3:4], dv

    def cross(p, q):
        return sum([a * b for a, b in zip(p[1:], q[1:])], p[0] * q[0])

    merged = [merge([st1[s, b] for s in range(4)], 256.0) for b in range(8)]
    for b, (m, m2, r, co, dv) in enumerate(merged):
        if b < 2:
            co = co + 256.0 * cross(dv, merged[2][4])
        for n, row in enumerate((m, m2, r, co)):
            pst[b, n : n + 1, :] = row
    st2_in = []
    for q in range(8):
        zq = lax.rem(z + q, 8)
        fa = ab(2 * c + lax.div(zq, 4))
        fk = kb(lax.rem(zq, 4))
        st2m[q, 0] = pst[zq]
        st2m[q, 3] = pst[2]
        for s in range(4):
            st2m[q, 1, s : s + 1, :] = st1[s, fa, 0:1, :]
            st2m[q, 2, s : s + 1, :] = st1[s, fk, 0:1, :]
        if q:
            st2_in.append(send(M_ST2 + q - 1, st2m.at[q], st2.at[q - 1], zdev[q]))

    to_y(3)
    to_y(4)
    x_in = [
        send(M_Y + 0, cen.at[8, top], oth.at[2, top], sib),
        send(M_Y + 1, cen.at[12, low], oth.at[2, low], non),
    ]
    chain(1, True)

    lax.fori_loop(5, 8, corr, 0)
    chain(2, False)
    to_y(5)
    to_y(6)
    to_y(7)
    x_in += [
        send(M_Y + 2, cen.at[0], oth.at[0], sib),
        send(M_Y + 3, cen.at[0], oth.at[4], non),
        send(M_Y + 4, cen.at[1], oth.at[1], sib),
        send(M_Y + 5, cen.at[1], oth.at[5], non),
    ]
    chain(2, True)

    def zero(n, carry):
        acc1[n] = jnp.zeros((512, 256), F32)
        acc2[n] = jnp.zeros((512, 256), F32)
        return carry

    lax.fori_loop(0, 4, zero, 0)
    rsq[...] = jnp.zeros_like(rsq)
    csq[...] = jnp.zeros_like(csq)
    x_in[0].wait_recv()
    x_in[1].wait_recv()
    x_ring = [
        send(M_Y + 6, oth.at[2], oth.at[3], left),
        send(M_Y + 7, oth.at[2], oth.at[7], right),
    ]
    for cp in st2_in:
        cp.wait_recv()
    st2m_all = [st2m[0, 0]] + [st2[s, 0] for s in range(7)]
    k0_means = [st2m[0, 3]] + [st2[s, 3] for s in range(7)]
    m, m2, r, co, dv = merge(st2m_all, 1024.0)
    k0_dv = merge(k0_means, 1024.0)[4]
    fin[z, 0:1, :] = m + r * (1.0 / BATCH)
    fin[z, 1:2, :] = lax.rsqrt(m2 * (1.0 / BATCH) + EPS)
    fin[z, 2:3, :] = m
    fin[z, 3:4, :] = co + 1024.0 * cross(dv, k0_dv)
    fin_in = [send(M_ST3 + q - 1, fin.at[z], fin.at[z], zdev[q]) for q in range(1, 8)]

    chain(3, False)

    chain(3, True)

    def norm(b, o):
        shift = st1[2 * o, b, 0:1, :] - fin[b, 0:1, :]
        scale = fin[b, 1:2, :]
        q = lax.rem(b, 4)
        idx = jnp.where(q < 2, 0, 2) + q + 2 * lax.div(b, 4)
        for h in range(2):
            rows = slice(128 * h, 128 * h + 128)
            v = cen[idx, rows] if o == 0 else oth[b, rows]
            nrm[b, o * 256 + 128 * h : o * 256 + 128 * h + 128, :] = ((v.astype(F32) + shift) * scale).astype(BF16)

    def norms(o):
        lax.fori_loop(0, 8, lambda b, carry: (norm(b, o), carry)[1], 0)

    x_ring[0].wait_recv()
    x_ring.append(send(M_Y + 8, oth.at[3, top], oth.at[6, top], left))
    x_ring[1].wait_recv()
    x_ring.append(send(M_Y + 9, oth.at[7, low], oth.at[6, low], right))
    chain(4, False)
    for cp in fin_in:
        cp.wait_recv()
    cii = fin[ylo, 3:4, :] * fin[ylo, 1:2, :] * fin[2, 1:2, :] * (1.0 / BATCH)
    dg[0:1, :] = cii
    dg[1:2, :] = (-2.0 * (1.0 - cii)).astype(BF16).astype(F32)
    norms(0)
    chain(4, True)

    fa = ab(2 * c + lax.div(z, 4))
    fk = kb(lax.rem(z, 4))
    pad = jnp.zeros((7, 256), F32)
    ra = jnp.concatenate([fin[fa, 1:2, :] * (2.0 * LAMBDA / BATCH), pad], 0)
    rk = jnp.concatenate([fin[fk, 1:2, :], pad], 0)
    rows_id = lax.broadcasted_iota(jnp.int32, (256, 256), 0)
    cols_id = lax.broadcasted_iota(jnp.int32, (256, 256), 1)
    off = rows_id + jnp.where((c == 0) & (z == 4 * ylo), 0, 512) != cols_id
    scl[...] = jnp.where(off, tn(ra, rk, HIGH), 0.0)
    mu_a = [(st2m[0, 1] if s == 0 else st2[s - 1, 1]) - fin[fa, 2:3, :] for s in range(8)]
    mu_k = [(st2m[0, 2] if s == 0 else st2[s - 1, 2]) - fin[fk, 2:3, :] for s in range(8)]
    fix[...] = scl[...] * tn(jnp.concatenate(mu_a, 0) * 256.0, jnp.concatenate(mu_k, 0), HIGH)

    for cp in y_sum[7]:
        cp.wait_recv()
    for s in range(2):
        for u in range(2):
            q = 2 * u + s
            rows = slice(64 * q, 64 * q + 64)
            v = cown[7, rows] + crecv[7, rows].astype(F32) + yr[7, rows].astype(F32)
            for d in (1 - u, u):
                z_in[(d, 4, u, s)].wait_recv()
                v = v + zr[zslot(d, 4, u) + s].astype(F32)
            part = g.at[c, z, q]
            g[c, z, q] = (v * scl[rows] + fix[rows]).astype(BF16)
            for d in (u, 1 - u):
                send(M_ZG + zslot(d, 1, u) + s, part, part, zto[d])
    send(M_GD + 0, g.at[c, z, pl.ds(0, 2)], g.at[c, z, pl.ds(0, 2)], core)
    send(M_GD + 1, g.at[c, z, pl.ds(2, 2)], g.at[c, z, pl.ds(2, 2)], core)

    def arrive(t, far, onward):
        for s in range(2):
            for d in range(2):
                u = d if far else 1 - d
                i = d * 16 + (t - 1) * 4 + u * 2 + s
                source = lax.rem(z + (8 - t if d == 0 else t), 8)
                part = g.at[c, source, 2 * u + s]
                make(M_ZG + i, part, part, zto[d]).wait_recv()
                if onward is not None:
                    start = make(M_ZG + i + 4, part, part, zto[d]).start
                    if onward is True:
                        start()
                    else:
                        pl.when(onward)(start)
                if s == 1:
                    both = g.at[c, source, pl.ds(2 * u, 2)]
                    make(M_GD + 4 * t + 2 * d + u, both, both, core).start()

    def use(zs_):
        i = lax.div(zs_, 4)
        k = lax.rem(zs_, 4)
        ga = jnp.concatenate([g[0, zs_].reshape(256, 256), g[1, zs_].reshape(256, 256)], 0)
        v = nt(nrm[kb(k)], ga)
        acc1[i] += v[:, 0:256]
        acc1[2 + i] += v[:, 256:512]
        acc2[k] += nn(jnp.concatenate([nrm[i], nrm[4 + i]], 1), ga)
        v = ga.astype(F32)
        s = v * v
        part = s[:, 0:128] + s[:, 128:256]
        rsq[i] += part[0:256]
        rsq[2 + i] += part[256:512]
        csq[k] += jnp.sum(s.reshape(64, 8, 256), 0)

    def from_core(t, d, u):
        part = g.at[0, 0, pl.ds(0, 2)]
        make(M_GD + 4 * t + 2 * d + u, part, part, core).wait_recv()

    def uses(t, n):
        for u in range(2):
            from_core(t, n, u)
        use(lax.rem(z + (8 - t) + n * 2 * t, 8))

    arrive(1, True, True)
    arrive(1, False, True)
    for cp in x_in[2:] + x_ring[2:]:
        cp.wait_recv()
    norms(1)
    uses(0, 0)

    def step(t, carry):
        arrive(t, True, True)
        uses(t - 1, 0)
        arrive(t, False, t < 3)
        uses(t - 1, 1)
        return carry

    def partial1(a, o):
        b = ab(a)
        rows = slice(o * 256, o * 256 + 256)
        f = nrm[b, rows].astype(F32)
        v = acc1[a, rows] - f * rowsq[a, 0:1, :]
        gd = jnp.where(a == ylo, dg[1:2, :], 0.0)
        v = v + (nrm[2, rows].astype(F32) - f * dg[0:1, :]) * gd
        return v * fin[b, 1:2, :]

    def p1_start(ph, e):
        for a in (e, 2 + e):
            rowsq[a] = nt(jnp.ones((8, 128), F32), rsq[a], HIGH) * (0.5 / LAMBDA)
        m = M_P1 + 6 * ph
        p1[ph, 0] = partial1(2 + e, 0).astype(BF16)
        relay = [
            send(m, p1.at[ph, 0, top], p1relay.at[ph, top], sib),
            send(m + 1, p1.at[ph, 0, low], p1relay.at[ph, low], non),
        ]
        p1[ph, 1] = partial1(2 + e, 1).astype(BF16)
        a = send(m + 2, p1.at[ph, 1, low], p1in.at[ph, 1, low], non)
        p1[ph, 2] = partial1(e, 1).astype(BF16)
        b = send(m + 3, p1.at[ph, 2, top], p1in.at[ph, 0, top], sib)
        return relay, [a, b]

    def p1_add(ph, relay):
        m = M_P1 + 6 * ph
        relay[0].wait_recv()
        p1[ph, 1, top] = (p1[ph, 1, top].astype(F32) + p1relay[ph, top].astype(F32)).astype(BF16)
        a = send(m + 4, p1.at[ph, 1, top], p1in.at[ph, 1, top], non)
        relay[1].wait_recv()
        p1[ph, 2, low] = (p1[ph, 2, low].astype(F32) + p1relay[ph, low].astype(F32)).astype(BF16)
        return [a, send(m + 5, p1.at[ph, 2, low], p1in.at[ph, 0, low], sib)]

    lax.fori_loop(2, 4, step, 0)
    uses(3, 0)
    arrive(4, True, None)
    uses(3, 1)
    relay1, in1 = p1_start(0, iz)
    from_core(4, 0, 0)
    from_core(4, 1, 1)
    use(lax.rem(z + 4, 8))

    for k in range(4):
        colsq[k] = jnp.sum(csq[k], 0, keepdims=True) * (0.5 / LAMBDA)

    def partial2(k, o):
        b = KB[k]
        rows = slice(o * 256, o * 256 + 256)
        s = nrm[b, rows].astype(F32)
        v = acc2[k, rows] - s * colsq[k]
        if k == 0:
            v = v + (nrm[ylo, rows].astype(F32) - s * dg[0:1, :]) * dg[1:2, :]
        return v * fin[b, 1:2, :]

    def p2_relay(o):
        p2[2, o] = partial2(2, o).astype(BF16)
        return [
            send(M_P2O + 2 * o, p2.at[2, o, top], p2relay.at[o, top], right),
            send(M_P2O + 2 * o + 1, p2.at[2, o, low], p2relay.at[o, low], left),
        ]

    def p2_send(o):
        p2[1, o] = partial2(1, o).astype(BF16)
        a = send(M_P2R + 2 * o, p2.at[1, o, low], p2in.at[0, o, low], right)
        p2[3, o] = partial2(3, o).astype(BF16)
        return [a, send(M_P2L + 2 * o, p2.at[3, o, top], p2in.at[1, o, top], left)]

    def p2_add(o, relay):
        relay[0].wait_recv()
        p2[1, o, top] = (p2[1, o, top].astype(F32) + p2relay[o, top].astype(F32)).astype(BF16)
        a = send(M_P2R + 2 * o + 1, p2.at[1, o, top], p2in.at[0, o, top], right)
        relay[1].wait_recv()
        p2[3, o, low] = (p2[3, o, low].astype(F32) + p2relay[o, low].astype(F32)).astype(BF16)
        return [a, send(M_P2L + 2 * o + 1, p2.at[3, o, low], p2in.at[1, o, low], left)]

    def sent(i, part):
        make(i, part, part, core).wait_send()

    def finish_sends():
        for cp in done:
            cp.wait_send()
        for s in range(8):
            sent(M_C + s, csend.at[s])
        for d in range(2):
            for t in range(1, 5):
                for u in range(2):
                    if t > 1 and (t < 4 or u == d):
                        for s in range(2):
                            sent(M_ZG + zslot(d, t, u) + s, g.at[0, 0, 0])
                    if t < 4 or u == d:
                        sent(M_GD + 4 * t + 2 * d + u, g.at[0, 0, pl.ds(0, 2)])

    done = list(sends)
    relay2 = p2_relay(1)
    in1 += p1_add(0, relay1)
    in2 = p2_send(1)
    relay1, more = p1_start(1, 1 - iz)
    in1 += more
    in2 += p2_add(1, relay2)
    relay20 = p2_relay(0)
    in20 = p2_send(0)
    ob2[0] = partial2(0, 1)
    ob2[1] = partial2(0, 0)
    in1 += p1_add(1, relay1)
    in20 += p2_add(0, relay20)
    for cp in in2:
        cp.wait_recv()
    xs[...] = (ob2[0] + p2in[0, 1].astype(F32) + p2in[1, 1].astype(F32)).astype(BF16)
    x_last = send(M_X, xs, xr, sib)
    finish_sends()
    ob1[0] = partial1(iz, 0)
    ob1[1] = partial1(1 - iz, 0)
    outs = []

    def put(src, ref, col, i):
        cp = pltpu.make_async_copy(src, ref.at[:, pl.ds(pl.multiple_of(col, 256), 256)], os_.at[i])
        cp.start()
        outs.append(cp)

    for cp in in20:
        cp.wait_recv()
    ob2[1] = ob2[1] + p2in[0, 0].astype(F32) + p2in[1, 0].astype(F32)
    put(ob2.at[1], out2, lo, 0)
    for cp in in1:
        cp.wait_recv()
    for ph, e in enumerate((iz, 1 - iz)):
        ob1[ph] = ob1[ph] + p1in[ph, 0].astype(F32) + p1in[ph, 1].astype(F32)
        put(ob1.at[ph], out1, e * 256, 1 + ph)
    x_last.wait_recv()
    ob2[0] = xr[...].astype(F32)
    put(ob2.at[0], out2, hi, 3)
    for cp in outs:
        cp.wait()
    for cp in sends[len(done) :]:
        cp.wait_send()


def write_kernel(a, b, out1, out2, sem):
    cps = []
    for n, (src, dst) in enumerate(((a, out1), (b, out2))):
        for q in range(2):
            rows = pl.ds(128 * q, 128)
            cps.append(pltpu.make_async_copy(src.at[rows], dst.at[rows], sem.at[2 * n + q]))
    for cp in cps:
        cp.start()
    for cp in cps:
        cp.wait()


def body(first, second):
    v = pltpu.VMEM
    out = jax.ShapeDtypeStruct((256, 512), F32)
    anywhere = pl.BlockSpec(memory_space=pl.ANY)
    parts = pl.pallas_call(
        kernel,
        out_shape=(out, out),
        in_specs=[anywhere, anywhere],
        out_specs=(anywhere, anywhere),
        scratch_shapes=[
            v((16, 256, 256), F32),
            v((16, 256, 256), BF16),
            v((8, 256, 256), BF16),
            v((4, 256, 256), BF16),
            v((16, 4, 256), F32),
            v((2, 4, 4, 256), F32),
            v((4, 8, 4, 256), F32),
            v((8, 4, 256), F32),
            v((8, 4, 4, 256), F32),
            v((7, 4, 4, 256), F32),
            v((8, 4, 256), F32),
            v((2, 256), F32),
            v((256, 256), F32),
            v((256, 256), F32),
            v((8, 512, 256), BF16),
            v((8, 256, 256), F32),
            v((8, 256, 256), F32),
            v((8, 512, 256), BF16),
            v((8, 512, 256), BF16),
            v((8, 256, 256), BF16),
            v((8, 256, 256), BF16),
            v((32, 64, 256), BF16),
            v((32, 64, 256), BF16),
            v((2, 8, 4, 64, 256), BF16),
            v((4, 512, 256), F32),
            v((4, 512, 256), F32),
            v((4, 256, 128), F32),
            v((4, 8, 256), F32),
            v((4, 8, 256), F32),
            v((4, 1, 256), F32),
            v((2, 3, 256, 256), BF16),
            v((2, 2, 256, 256), BF16),
            v((2, 256, 256), BF16),
            v((4, 2, 256, 256), BF16),
            v((2, 2, 256, 256), BF16),
            v((2, 256, 256), BF16),
            v((256, 256), BF16),
            v((256, 256), BF16),
            v((2, 256, 256), F32),
            v((2, 256, 256), F32),
            pltpu.SemaphoreType.DMA((M_ALL,)),
            pltpu.SemaphoreType.DMA((M_ALL,)),
            pltpu.SemaphoreType.DMA((16,)),
            pltpu.SemaphoreType.DMA((4,)),
        ],
        compiler_params=pltpu.CompilerParams(
            collective_id=0, has_side_effects=True, vmem_limit_bytes=51 * 1024 * 1024
        ),
    )(first, second)
    return pl.pallas_call(
        write_kernel,
        out_shape=(out, out),
        in_specs=[pl.BlockSpec(memory_space=pltpu.VMEM)] * 2,
        out_specs=(anywhere, anywhere),
        scratch_shapes=[pltpu.SemaphoreType.DMA((4,))],
        compiler_params=pltpu.CompilerParams(vmem_limit_bytes=8 * 1024 * 1024),
    )(*parts)


def solution(mesh):
    return jax.shard_map(
        body,
        mesh=mesh,
        in_specs=(P("dp", None), P("dp", None)),
        out_specs=(P("dp", "replica"), P("dp", "replica")),
        check_vma=False,
    )
```

```python
import jax
import jax.numpy as jnp
from jax import lax
from jax.experimental import pallas as pl
from jax.experimental.pallas import tpu as pltpu
from jax.sharding import PartitionSpec as P

LAMBDA = 0.0051
EPS = 1e-05
MESH = pl.DeviceIdType.MESH
F32 = jnp.float32
BF16 = jnp.bfloat16
BATCH = 8192

OWN = (0, 1, 4, 5, 2, 3, 6, 7)
STAT_SIB = (0, 1, 8, 9)
STAT_NON = (0, 1, 14, 15)
KB = (2, 3, 6, 7)
AB = (0, 1, 4, 5)

M_Y = 0
M_ST1 = 12
M_ST2 = 17
M_ST3 = 24
M_C = 31
M_YP = 39
M_ZR = 55
M_ZG = 87
M_GD = 119
M_P1 = 139
M_P2O = 151
M_P2R = 155
M_P2L = 159
M_X = 163
M_ALL = 164

HIGH = lax.Precision.HIGHEST


def nt(a, b, precision=None):
    return lax.dot_general(
        a, b, (((1,), (1,)), ((), ())), preferred_element_type=F32, precision=precision
    )


def tn(a, b, precision=None):
    return lax.dot_general(
        a, b, (((0,), (0,)), ((), ())), preferred_element_type=F32, precision=precision
    )


def nn(a, b):
    return lax.dot_general(a, b, (((1,), (0,)), ((), ())), preferred_element_type=F32)


def ab(a):
    return a + 2 * lax.div(a, 2)


def kb(k):
    return k + 2 + 2 * lax.div(k, 2)


def kernel(
    first, second, out1, out2,
    raw, cen, oth, xt, stat, smsg, st1, pst, st2m, st2, fin, dg, scl, fix, nrm, cown, ypart, csend, crecv, ys, yr, zs, zr, g,
    acc1, acc2, rsq, csq, rowsq, colsq,
    p1, p1in, p1relay, p2, p2in, p2relay, xs, xr, ob1, ob2, ss, rs, ls, os_,
):
    dp = lax.axis_index("dp")
    rep = lax.axis_index("replica")
    c = lax.rem(dp, 2)
    ylo = lax.rem(lax.div(dp, 2), 2)
    z = lax.div(dp, 4)
    yhi = lax.div(rep, 4)
    x = lax.rem(rep, 4)

    def dev(x_, yhi_, ylo_, z_, c_):
        return (z_ * 4 + ylo_ * 2 + c_, yhi_ * 4 + x_)

    core = dev(x, yhi, ylo, z, 1 - c)
    sib = dev(x, yhi, 1 - ylo, z, c)
    sibc = dev(x, yhi, 1 - ylo, z, 1 - c)
    non = dev(x, 1 - yhi, 1 - ylo, z, c)
    nonc = dev(x, 1 - yhi, 1 - ylo, z, 1 - c)
    right = dev(lax.rem(x + 1, 4), yhi, ylo, z, c)
    left = dev(lax.rem(x + 3, 4), yhi, ylo, z, c)
    zdev = [dev(x, yhi, ylo, lax.rem(z + q, 8), c) for q in range(8)]
    zto = (zdev[1], zdev[7])

    def load(i, ref, col):
        return pltpu.make_async_copy(
            ref.at[:, pl.ds(pl.multiple_of(col, 256), 256)], raw.at[i], ls.at[i]
        )

    kz = lax.rem(z, 4)
    iz = lax.div(z, 4)
    base = yhi * 2048
    other = 2048 - base
    mine = x * 512
    lo = ylo * 256
    hi = 256 - lo
    def load_first(e):
        for j in range(2):
            load(2 * j + e, first, (base, other)[j] + mine + 256 * e).start()

    def load_second(k):
        piece = lax.rem(x + k, 4) * 512
        for m, col in enumerate((base + lo, base + hi, other + hi)):
            load(4 + 4 * m + k, second, col + piece).start()

    load_first(1 - iz)
    load_second(kz)
    barrier = pltpu.get_barrier_semaphore()
    partners = [core, sib, sibc, non, nonc, right, left] + zdev[1:]
    for d in partners:
        pl.semaphore_signal(barrier, inc=1, device_id=d, device_id_type=MESH)
    load_first(iz)
    for n in (3, 1, 2):
        load_second(lax.rem(kz + n, 4))

    def make(i, src, dst, to):
        return pltpu.make_async_remote_copy(
            src_ref=src, dst_ref=dst, send_sem=ss.at[i], recv_sem=rs.at[i], device_id=to, device_id_type=MESH
        )

    sends = []

    def send(i, src, dst, to):
        cp = make(i, src, dst, to)
        cp.start()
        sends.append(cp)
        return cp

    def local_stats(i, carry):
        pltpu.make_async_copy(first.at[:, pl.ds(0, 256)], raw.at[i], ls.at[i]).wait()
        v = raw[i]
        m = jnp.sum(v, 0, keepdims=True) * (1.0 / 256)
        dv = v - m
        r = dv.astype(BF16)
        cen[i] = r
        stat[i, 0:1, :] = m
        stat[i, 1:2, :] = jnp.sum(dv * dv, 0, keepdims=True)
        stat[i, 2:3, :] = jnp.sum(r.astype(F32), 0, keepdims=True)
        stat[i, 3:4, :] = jnp.zeros_like(m)
        return carry

    top, low = pl.ds(0, 128), pl.ds(128, 128)

    def blocks_k(m, carry):
        return local_stats(4 + 4 * lax.rem(m, 3) + lax.rem(kz + lax.div(m, 3), 4), carry)

    def first_blocks(e):
        def one(j, carry):
            local_stats(2 * j + e, carry)
            xt[2 * j + e] = cen[2 * j + e].T
            return carry

        lax.fori_loop(0, 2, one, 0)

    first_blocks(1 - iz)
    lax.fori_loop(0, 3, blocks_k, 0)
    pl.semaphore_wait(barrier, len(partners))

    def corr(s, carry):
        r = jnp.where(lax.rem(s, 2) == 1, 4 - lax.div(s + 1, 2), 4 + lax.div(s, 2))
        d = lax.rem(z + r, 8)
        i = lax.div(d, 4)
        k = lax.rem(d, 4)
        a = 2 * (1 - c) + i
        b = 2 * c + i
        v = nn(jnp.concatenate([xt[a], xt[b]], 0), cen[4 + k])
        csend[s, 0:256] = v[0:256].astype(BF16)
        cown[s] = v[256:512]
        v = nn(jnp.concatenate([xt[a, top], xt[b, top]], 0), cen[8 + k])
        csend[s, 256:384] = v[0:128].astype(BF16)
        ypart[s, 0:128] = v[128:256]
        v = nn(jnp.concatenate([xt[b, low], xt[a, low]], 0), cen[12 + k])
        csend[s, 384:512] = v[0:128].astype(BF16)
        ypart[s, 128:256] = v[128:256]
        make(M_C + s, csend.at[s], crecv.at[s], core).start()
        return carry

    y_sum = []

    def to_y(s):
        make(M_C + s, csend.at[s], crecv.at[s], core).wait_recv()
        ys[s] = (ypart[s] + crecv[s, 256:512].astype(F32)).astype(BF16)
        y_sum.append(
            (
                send(M_YP + 2 * s, ys.at[s, top], yr.at[s, top], sib),
                send(M_YP + 2 * s + 1, ys.at[s, low], yr.at[s, low], non),
            )
        )

    corr(0, 0)
    first_blocks(iz)
    lax.fori_loop(3, 12, blocks_k, 0)
    def zslot(d, t, u):
        return d * 16 + (t - 1) * 4 + u * 2

    z_in = {}

    def chain(t, far):
        dist = 5 - t
        slot = (7 - 2 * dist, 8 - 2 * dist) if dist < 4 else (0, 0)
        if (t, far) in ((1, True), (2, False), (3, False), (4, False)):
            for n in set(slot):
                for cp in y_sum[n]:
                    cp.wait_recv()
        for s in range(2):
            for d in range(2):
                u = d if far else 1 - d
                n = slot[d]
                rows = slice(128 * u + 64 * s, 128 * u + 64 * s + 64)
                v = cown[n, rows] + crecv[n, rows].astype(F32) + yr[n, rows].astype(F32)
                if (d, t - 1, u, s) in z_in:
                    z_in[(d, t - 1, u, s)].wait_recv()
                    v = v + zr[zslot(d, t - 1, u) + s].astype(F32)
                i = zslot(d, t, u) + s
                zs[i] = v.astype(BF16)
                z_in[(d, t, u, s)] = send(M_ZR + i, zs.at[i], zr.at[i], zto[d])

    def comoment(i, j):
        return jnp.sum((raw[i] - stat[i, 0:1, :]) * (raw[j] - stat[j, 0:1, :]), 0, keepdims=True)

    for n in range(4):
        smsg[0, n] = stat[STAT_SIB[n]]
        smsg[1, n] = stat[STAT_NON[n]]
    for b in range(8):
        st1[0, b] = stat[OWN[b]]
    smsg[0, 1 - ylo, 3:4, :] = comoment(1 - ylo, 8)
    st1[0, ylo, 3:4, :] = comoment(ylo, 4)
    st_in = [
        send(M_ST1 + 0, smsg.at[0], st1.at[2, pl.ds(0, 4)], sib),
        send(M_ST1 + 1, smsg.at[1], st1.at[2, pl.ds(4, 4)], non),
        send(M_ST1 + 2, smsg.at[0], st1.at[3, pl.ds(0, 4)], sibc),
        send(M_ST1 + 3, smsg.at[1], st1.at[3, pl.ds(4, 4)], nonc),
        send(M_ST1 + 4, st1.at[0], st1.at[1], core),
    ]
    to_y(0)
    lax.fori_loop(1, 5, corr, 0)
    to_y(1)
    to_y(2)
    for cp in st_in:
        cp.wait_recv()

    def merge(rows, count):
        total = sum(rows[1:], rows[0])
        m = total[0:1] * (1.0 / len(rows))
        dv = [r[0:1] - m for r in rows]
        m2 = total[1:2] + count * sum([d * d for d in dv[1:]], dv[0] * dv[0])
        return m, m2, total[2:3], total[3:4], dv

    def cross(p, q):
        return sum([a * b for a, b in zip(p[1:], q[1:])], p[0] * q[0])

    merged = [merge([st1[s, b] for s in range(4)], 256.0) for b in range(8)]
    for b, (m, m2, r, co, dv) in enumerate(merged):
        if b < 2:
            co = co + 256.0 * cross(dv, merged[2][4])
        for n, row in enumerate((m, m2, r, co)):
            pst[b, n : n + 1, :] = row
    st2_in = []
    for q in range(8):
        zq = lax.rem(z + q, 8)
        fa = ab(2 * c + lax.div(zq, 4))
        fk = kb(lax.rem(zq, 4))
        st2m[q, 0] = pst[zq]
        st2m[q, 3] = pst[2]
        for s in range(4):
            st2m[q, 1, s : s + 1, :] = st1[s, fa, 0:1, :]
            st2m[q, 2, s : s + 1, :] = st1[s, fk, 0:1, :]
        if q:
            st2_in.append(send(M_ST2 + q - 1, st2m.at[q], st2.at[q - 1], zdev[q]))

    to_y(3)
    to_y(4)
    x_in = [
        send(M_Y + 0, cen.at[8, top], oth.at[2, top], sib),
        send(M_Y + 1, cen.at[12, low], oth.at[2, low], non),
    ]
    chain(1, True)

    lax.fori_loop(5, 8, corr, 0)
    chain(2, False)
    to_y(5)
    to_y(6)
    to_y(7)
    x_in += [
        send(M_Y + 2, cen.at[0], oth.at[0], sib),
        send(M_Y + 3, cen.at[0], oth.at[4], non),
        send(M_Y + 4, cen.at[1], oth.at[1], sib),
        send(M_Y + 5, cen.at[1], oth.at[5], non),
    ]
    chain(2, True)

    def zero(n, carry):
        acc1[n] = jnp.zeros((512, 256), F32)
        acc2[n] = jnp.zeros((512, 256), F32)
        return carry

    lax.fori_loop(0, 4, zero, 0)
    rsq[...] = jnp.zeros_like(rsq)
    csq[...] = jnp.zeros_like(csq)
    x_in[0].wait_recv()
    x_in[1].wait_recv()
    x_ring = [
        send(M_Y + 6, oth.at[2], oth.at[3], left),
        send(M_Y + 7, oth.at[2], oth.at[7], right),
    ]
    for cp in st2_in:
        cp.wait_recv()
    st2m_all = [st2m[0, 0]] + [st2[s, 0] for s in range(7)]
    k0_means = [st2m[0, 3]] + [st2[s, 3] for s in range(7)]
    m, m2, r, co, dv = merge(st2m_all, 1024.0)
    k0_dv = merge(k0_means, 1024.0)[4]
    fin[z, 0:1, :] = m + r * (1.0 / BATCH)
    fin[z, 1:2, :] = lax.rsqrt(m2 * (1.0 / BATCH) + EPS)
    fin[z, 2:3, :] = m
    fin[z, 3:4, :] = co + 1024.0 * cross(dv, k0_dv)
    fin_in = [send(M_ST3 + q - 1, fin.at[z], fin.at[z], zdev[q]) for q in range(1, 8)]

    chain(3, False)

    chain(3, True)

    def norm(b, o):
        shift = st1[2 * o, b, 0:1, :] - fin[b, 0:1, :]
        scale = fin[b, 1:2, :]
        q = lax.rem(b, 4)
        idx = jnp.where(q < 2, 0, 2) + q + 2 * lax.div(b, 4)
        for h in range(2):
            rows = slice(128 * h, 128 * h + 128)
            v = cen[idx, rows] if o == 0 else oth[b, rows]
            nrm[b, o * 256 + 128 * h : o * 256 + 128 * h + 128, :] = ((v.astype(F32) + shift) * scale).astype(BF16)

    def norms(o):
        lax.fori_loop(0, 8, lambda b, carry: (norm(b, o), carry)[1], 0)

    x_ring[0].wait_recv()
    x_ring.append(send(M_Y + 8, oth.at[3, top], oth.at[6, top], left))
    x_ring[1].wait_recv()
    x_ring.append(send(M_Y + 9, oth.at[7, low], oth.at[6, low], right))
    chain(4, False)
    for cp in fin_in:
        cp.wait_recv()
    cii = fin[ylo, 3:4, :] * fin[ylo, 1:2, :] * fin[2, 1:2, :] * (1.0 / BATCH)
    dg[0:1, :] = cii
    dg[1:2, :] = (-2.0 * (1.0 - cii)).astype(BF16).astype(F32)
    norms(0)
    chain(4, True)

    fa = ab(2 * c + lax.div(z, 4))
    fk = kb(lax.rem(z, 4))
    pad = jnp.zeros((7, 256), F32)
    ra = jnp.concatenate([fin[fa, 1:2, :] * (2.0 * LAMBDA / BATCH), pad], 0)
    rk = jnp.concatenate([fin[fk, 1:2, :], pad], 0)
    rows_id = lax.broadcasted_iota(jnp.int32, (256, 256), 0)
    cols_id = lax.broadcasted_iota(jnp.int32, (256, 256), 1)
    off = rows_id + jnp.where((c == 0) & (z == 4 * ylo), 0, 512) != cols_id
    scl[...] = jnp.where(off, tn(ra, rk, HIGH), 0.0)
    mu_a = [(st2m[0, 1] if s == 0 else st2[s - 1, 1]) - fin[fa, 2:3, :] for s in range(8)]
    mu_k = [(st2m[0, 2] if s == 0 else st2[s - 1, 2]) - fin[fk, 2:3, :] for s in range(8)]
    fix[...] = scl[...] * tn(jnp.concatenate(mu_a, 0) * 256.0, jnp.concatenate(mu_k, 0), HIGH)

    for cp in y_sum[7]:
        cp.wait_recv()
    for s in range(2):
        for u in range(2):
            q = 2 * u + s
            rows = slice(64 * q, 64 * q + 64)
            v = cown[7, rows] + crecv[7, rows].astype(F32) + yr[7, rows].astype(F32)
            for d in (1 - u, u):
                z_in[(d, 4, u, s)].wait_recv()
                v = v + zr[zslot(d, 4, u) + s].astype(F32)
            part = g.at[c, z, q]
            g[c, z, q] = (v * scl[rows] + fix[rows]).astype(BF16)
            for d in (u, 1 - u):
                send(M_ZG + zslot(d, 1, u) + s, part, part, zto[d])
    send(M_GD + 0, g.at[c, z, pl.ds(0, 2)], g.at[c, z, pl.ds(0, 2)], core)
    send(M_GD + 1, g.at[c, z, pl.ds(2, 2)], g.at[c, z, pl.ds(2, 2)], core)

    def arrive(t, far, onward):
        for s in range(2):
            for d in range(2):
                u = d if far else 1 - d
                i = d * 16 + (t - 1) * 4 + u * 2 + s
                source = lax.rem(z + (8 - t if d == 0 else t), 8)
                part = g.at[c, source, 2 * u + s]
                make(M_ZG + i, part, part, zto[d]).wait_recv()
                if onward is not None:
                    start = make(M_ZG + i + 4, part, part, zto[d]).start
                    if onward is True:
                        start()
                    else:
                        pl.when(onward)(start)
                if s == 1:
                    both = g.at[c, source, pl.ds(2 * u, 2)]
                    make(M_GD + 4 * t + 2 * d + u, both, both, core).start()

    def use(zs_, o):
        rows = pl.ds(256 * o, 256)
        i = lax.div(zs_, 4)
        k = lax.rem(zs_, 4)
        ga = jnp.concatenate([g[0, zs_].reshape(256, 256), g[1, zs_].reshape(256, 256)], 0)
        v = nt(nrm[kb(k), rows], ga)
        acc1[i, rows] += v[:, 0:256]
        acc1[2 + i, rows] += v[:, 256:512]
        acc2[k, rows] += nn(jnp.concatenate([nrm[i, rows], nrm[4 + i, rows]], 1), ga)
        if o == 0:
            v = ga.astype(F32)
            s = v * v
            part = s[:, 0:128] + s[:, 128:256]
            rsq[i] += part[0:256]
            rsq[2 + i] += part[256:512]
            csq[k] += jnp.sum(s.reshape(64, 8, 256), 0)

    def from_core(t, d, u):
        part = g.at[0, 0, pl.ds(0, 2)]
        make(M_GD + 4 * t + 2 * d + u, part, part, core).wait_recv()

    def uses(t, n, halves):
        for u in range(2):
            from_core(t, n, u)
        for o in halves:
            use(lax.rem(z + (8 - t) + n * 2 * t, 8), o)

    arrive(1, True, True)
    arrive(1, False, True)
    uses(0, 0, (0,))

    def step(t, carry):
        arrive(t, True, True)
        uses(t - 1, 0, (0,))
        arrive(t, False, t < 3)
        uses(t - 1, 1, (0,))
        return carry

    def rest(n, carry):
        use(lax.rem(z + 6 + n, 8), 1)
        return carry

    def partial1(a, o):
        b = ab(a)
        rows = slice(o * 256, o * 256 + 256)
        f = nrm[b, rows].astype(F32)
        v = acc1[a, rows] - f * rowsq[a, 0:1, :]
        gd = jnp.where(a == ylo, dg[1:2, :], 0.0)
        v = v + (nrm[2, rows].astype(F32) - f * dg[0:1, :]) * gd
        return v * fin[b, 1:2, :]

    def p1_start(ph, e):
        for a in (e, 2 + e):
            rowsq[a] = nt(jnp.ones((8, 128), F32), rsq[a], HIGH) * (0.5 / LAMBDA)
        m = M_P1 + 6 * ph
        p1[ph, 0] = partial1(2 + e, 0).astype(BF16)
        relay = [
            send(m, p1.at[ph, 0, top], p1relay.at[ph, top], sib),
            send(m + 1, p1.at[ph, 0, low], p1relay.at[ph, low], non),
        ]
        p1[ph, 1] = partial1(2 + e, 1).astype(BF16)
        a = send(m + 2, p1.at[ph, 1, low], p1in.at[ph, 1, low], non)
        p1[ph, 2] = partial1(e, 1).astype(BF16)
        b = send(m + 3, p1.at[ph, 2, top], p1in.at[ph, 0, top], sib)
        return relay, [a, b]

    def p1_add(ph, relay):
        m = M_P1 + 6 * ph
        relay[0].wait_recv()
        p1[ph, 1, top] = (p1[ph, 1, top].astype(F32) + p1relay[ph, top].astype(F32)).astype(BF16)
        a = send(m + 4, p1.at[ph, 1, top], p1in.at[ph, 1, top], non)
        relay[1].wait_recv()
        p1[ph, 2, low] = (p1[ph, 2, low].astype(F32) + p1relay[ph, low].astype(F32)).astype(BF16)
        return [a, send(m + 5, p1.at[ph, 2, low], p1in.at[ph, 0, low], sib)]

    lax.fori_loop(2, 4, step, 0)
    for cp in x_in[2:] + x_ring[2:]:
        cp.wait_recv()
    norms(1)
    lax.fori_loop(0, 5, rest, 0)
    arrive(4, True, None)
    uses(3, 0, (0, 1))
    uses(3, 1, (0, 1))
    relay1, in1 = p1_start(0, iz)
    from_core(4, 0, 0)
    from_core(4, 1, 1)
    use(lax.rem(z + 4, 8), 1)
    use(lax.rem(z + 4, 8), 0)

    for k in range(4):
        colsq[k] = jnp.sum(csq[k], 0, keepdims=True) * (0.5 / LAMBDA)

    def partial2(k, o):
        b = KB[k]
        rows = slice(o * 256, o * 256 + 256)
        s = nrm[b, rows].astype(F32)
        v = acc2[k, rows] - s * colsq[k]
        if k == 0:
            v = v + (nrm[ylo, rows].astype(F32) - s * dg[0:1, :]) * dg[1:2, :]
        return v * fin[b, 1:2, :]

    def p2_relay(o):
        p2[2, o] = partial2(2, o).astype(BF16)
        return [
            send(M_P2O + 2 * o, p2.at[2, o, top], p2relay.at[o, top], right),
            send(M_P2O + 2 * o + 1, p2.at[2, o, low], p2relay.at[o, low], left),
        ]

    def p2_send(o):
        p2[1, o] = partial2(1, o).astype(BF16)
        a = send(M_P2R + 2 * o, p2.at[1, o, low], p2in.at[0, o, low], right)
        p2[3, o] = partial2(3, o).astype(BF16)
        return [a, send(M_P2L + 2 * o, p2.at[3, o, top], p2in.at[1, o, top], left)]

    def p2_add(o, relay):
        relay[0].wait_recv()
        p2[1, o, top] = (p2[1, o, top].astype(F32) + p2relay[o, top].astype(F32)).astype(BF16)
        a = send(M_P2R + 2 * o + 1, p2.at[1, o, top], p2in.at[0, o, top], right)
        relay[1].wait_recv()
        p2[3, o, low] = (p2[3, o, low].astype(F32) + p2relay[o, low].astype(F32)).astype(BF16)
        return [a, send(M_P2L + 2 * o + 1, p2.at[3, o, low], p2in.at[1, o, low], left)]

    def sent(i, part):
        make(i, part, part, core).wait_send()

    def finish_sends():
        for cp in done:
            cp.wait_send()
        for s in range(8):
            sent(M_C + s, csend.at[s])
        for d in range(2):
            for t in range(1, 5):
                for u in range(2):
                    if t > 1 and (t < 4 or u == d):
                        for s in range(2):
                            sent(M_ZG + zslot(d, t, u) + s, g.at[0, 0, 0])
                    if t < 4 or u == d:
                        sent(M_GD + 4 * t + 2 * d + u, g.at[0, 0, pl.ds(0, 2)])

    done = list(sends)
    relay2 = p2_relay(1)
    in1 += p1_add(0, relay1)
    in2 = p2_send(1)
    relay1, more = p1_start(1, 1 - iz)
    in1 += more
    in2 += p2_add(1, relay2)
    relay20 = p2_relay(0)
    in20 = p2_send(0)
    ob2[0] = partial2(0, 1)
    ob2[1] = partial2(0, 0)
    in1 += p1_add(1, relay1)
    in20 += p2_add(0, relay20)
    for cp in in2:
        cp.wait_recv()
    xs[...] = (ob2[0] + p2in[0, 1].astype(F32) + p2in[1, 1].astype(F32)).astype(BF16)
    x_last = send(M_X, xs, xr, sib)
    finish_sends()
    ob1[0] = partial1(iz, 0)
    ob1[1] = partial1(1 - iz, 0)
    outs = []

    def put(src, ref, col, i):
        cp = pltpu.make_async_copy(src, ref.at[:, pl.ds(pl.multiple_of(col, 256), 256)], os_.at[i])
        cp.start()
        outs.append(cp)

    for cp in in20:
        cp.wait_recv()
    ob2[1] = ob2[1] + p2in[0, 0].astype(F32) + p2in[1, 0].astype(F32)
    put(ob2.at[1], out2, lo, 0)
    for cp in in1:
        cp.wait_recv()
    for ph, e in enumerate((iz, 1 - iz)):
        ob1[ph] = ob1[ph] + p1in[ph, 0].astype(F32) + p1in[ph, 1].astype(F32)
        put(ob1.at[ph], out1, e * 256, 1 + ph)
    x_last.wait_recv()
    ob2[0] = xr[...].astype(F32)
    put(ob2.at[0], out2, hi, 3)
    for cp in outs:
        cp.wait()
    for cp in sends[len(done) :]:
        cp.wait_send()


def write_kernel(a, b, out1, out2, sem):
    cps = []
    for n, (src, dst) in enumerate(((a, out1), (b, out2))):
        for q in range(2):
            rows = pl.ds(128 * q, 128)
            cps.append(pltpu.make_async_copy(src.at[rows], dst.at[rows], sem.at[2 * n + q]))
    for cp in cps:
        cp.start()
    for cp in cps:
        cp.wait()


def body(first, second):
    v = pltpu.VMEM
    out = jax.ShapeDtypeStruct((256, 512), F32)
    anywhere = pl.BlockSpec(memory_space=pl.ANY)
    parts = pl.pallas_call(
        kernel,
        out_shape=(out, out),
        in_specs=[anywhere, anywhere],
        out_specs=(anywhere, anywhere),
        scratch_shapes=[
            v((16, 256, 256), F32),
            v((16, 256, 256), BF16),
            v((8, 256, 256), BF16),
            v((4, 256, 256), BF16),
            v((16, 4, 256), F32),
            v((2, 4, 4, 256), F32),
            v((4, 8, 4, 256), F32),
            v((8, 4, 256), F32),
            v((8, 4, 4, 256), F32),
            v((7, 4, 4, 256), F32),
            v((8, 4, 256), F32),
            v((2, 256), F32),
            v((256, 256), F32),
            v((256, 256), F32),
            v((8, 512, 256), BF16),
            v((8, 256, 256), F32),
            v((8, 256, 256), F32),
            v((8, 512, 256), BF16),
            v((8, 512, 256), BF16),
            v((8, 256, 256), BF16),
            v((8, 256, 256), BF16),
            v((32, 64, 256), BF16),
            v((32, 64, 256), BF16),
            v((2, 8, 4, 64, 256), BF16),
            v((4, 512, 256), F32),
            v((4, 512, 256), F32),
            v((4, 256, 128), F32),
            v((4, 8, 256), F32),
            v((4, 8, 256), F32),
            v((4, 1, 256), F32),
            v((2, 3, 256, 256), BF16),
            v((2, 2, 256, 256), BF16),
            v((2, 256, 256), BF16),
            v((4, 2, 256, 256), BF16),
            v((2, 2, 256, 256), BF16),
            v((2, 256, 256), BF16),
            v((256, 256), BF16),
            v((256, 256), BF16),
            v((2, 256, 256), F32),
            v((2, 256, 256), F32),
            pltpu.SemaphoreType.DMA((M_ALL,)),
            pltpu.SemaphoreType.DMA((M_ALL,)),
            pltpu.SemaphoreType.DMA((16,)),
            pltpu.SemaphoreType.DMA((4,)),
        ],
        compiler_params=pltpu.CompilerParams(
            collective_id=0, has_side_effects=True, vmem_limit_bytes=51 * 1024 * 1024
        ),
    )(first, second)
    return pl.pallas_call(
        write_kernel,
        out_shape=(out, out),
        in_specs=[pl.BlockSpec(memory_space=pltpu.VMEM)] * 2,
        out_specs=(anywhere, anywhere),
        scratch_shapes=[pltpu.SemaphoreType.DMA((4,))],
        compiler_params=pltpu.CompilerParams(vmem_limit_bytes=8 * 1024 * 1024),
    )(*parts)


def solution(mesh):
    return jax.shard_map(
        body,
        mesh=mesh,
        in_specs=(P("dp", None), P("dp", None)),
        out_specs=(P("dp", "replica"), P("dp", "replica")),
        check_vma=False,
    )
```
